32 devices in a mesh: fsdp: 32 (over z, y, x, core).
Axes of the slice: x: 2, y: 2, z: 4, core: 2. Of those that a mesh axis runs over, the one named last changes fastest.
Arguments:
- inputs: bfloat16 [2, 16384, 1024], P(None, 'fsdp'), may hold values from -6 to 6
- segments: int32 [2, 16384], P(None, 'fsdp'), may hold values from 0 to 24, as said below
- attn_gain: bfloat16 [1024], P('fsdp'), may hold values from 0.5 to 1.5
- w_query: bfloat16 [1024, 1024], P('fsdp'), may hold values from -0.1875 to 0.1875
- key_projection: bfloat16 [1024, 512], P('fsdp'), may hold values from -0.1875 to 0.1875
- value_projection: bfloat16 [1024, 512], P('fsdp'), may hold values from -0.1875 to 0.1875
- w_output: bfloat16 [1024, 1024], P(None, 'fsdp'), may hold values from -1 to 1
- query_gain: bfloat16 [64], replicated, may hold values from 0.5 to 1.5
- key_norm_gain: bfloat16 [64], replicated, may hold values from 0.5 to 1.5
- ffn_gain: bfloat16 [1024], P('fsdp'), may hold values from 0.5 to 1.5
- w_gate: bfloat16 [1024, 4608], P('fsdp'), may hold values from -0.1875 to 0.1875
- w_up: bfloat16 [1024, 4608], P('fsdp'), may hold values from -0.1875 to 0.1875
- w_down: bfloat16 [4608, 1024], P(None, 'fsdp'), may hold values from -0.09375 to 0.09375
- cotangent: bfloat16 [2, 16384, 1024], P(None, 'fsdp'), may hold values from -6 to 6
Outputs:
- outputs: bfloat16 [2, 16384, 1024], P(None, 'fsdp')
- input_grad: bfloat16 [2, 16384, 1024], P(None, 'fsdp')
- attn_gain_grad: float32 [1024], P('fsdp')
- w_query_grad: float32 [1024, 1024], P('fsdp')
- w_key_grad: float32 [1024, 512], P('fsdp')
- w_value_grad: float32 [1024, 512], P('fsdp')
- w_output_grad: float32 [1024, 1024], P(None, 'fsdp')
- query_gain_grad: float32 [64], replicated
- key_gain_grad: float32 [64], replicated
- ffn_gain_grad: float32 [1024], P('fsdp')
- w_gate_grad: float32 [1024, 4608], P('fsdp')
- w_up_grad: float32 [1024, 4608], P('fsdp')
- w_down_grad: float32 [4608, 1024], P(None, 'fsdp')
The draws below stay inside these ranges and needn't reach their ends.
Inputs may be any that keep to these rules, and one draw needn't show every extreme that they name: `segments`: within each sequence of 1024 tokens beginning at a multiple of 1024 along a micro-batch, the numbers start at 0, never fall, and are 24 at the sequence's last token; a document is a maximal stretch of one number inside a sequence.
All inputs are finite; a program needn't handle non-finite values.
Results may differ from the reference program's by a relative error of at most 0.013.
Values may be sent and summed in bfloat16 or wider, within the bound.
A program may use at most 320 MiB of HBM per device.

```python
import math
import jax
import jax.numpy as jnp
from jax import lax

MODEL_WIDTH = 1024
QUERY_HEADS = 16
KEY_VALUE_HEADS = 8
HEAD_SIZE = 64
FF = 4608
MB = 2
CUTS = 12
SEQ = 1024
TOK_MB = 16384


def draw_segments(key, part):
    seq_count = MB * TOK_MB // SEQ
    left_key = jax.random.fold_in(key, 11)
    right_key = jax.random.fold_in(key, 23)
    left_pick = jax.random.randint(left_key, (seq_count, CUTS), 0, 16)
    right_pick = jax.random.randint(right_key, (seq_count, CUTS), 0, 16)
    half_len = SEQ // 2
    left_cut = 1 + left_pick * left_pick * left_pick * half_len // 4096
    right_cut = SEQ - 1 - right_pick * right_pick * right_pick * half_len // 4096
    starts = jnp.concatenate([left_cut, right_cut], axis=1)
    places = jnp.arange(SEQ, dtype=jnp.int32)
    numbers = jnp.sum((starts[:, None, :] <= places[None, :, None]).astype(jnp.int32), axis=2)
    return numbers.reshape(MB, TOK_MB).astype(jnp.int32)


def steps_of(rng, shape, pieces, low, top_value):
    level, own = 1.0, jax.random.fold_in(rng, 6)
    for position, blocks in pieces:
        heights = jnp.exp(jax.random.uniform(jax.random.fold_in(own, position), (blocks,), jnp.float32, low / len(pieces), top_value / len(pieces)))
        level = level * jnp.repeat(heights, shape[position] // blocks).reshape([-1 if axis == position else 1 for axis in range(len(shape))])
    return level


def normal_values(stream_key, extent, scale, reach, shards=(), kind=jnp.bfloat16):
    loudness = steps_of(stream_key, extent, shards, -0.22, 0.18) if shards else 1.0
    values = jax.random.normal(stream_key, extent, jnp.float32) * scale * loudness
    return jnp.minimum(jnp.maximum(values, -reach), reach).astype(kind)


def setup_inputs(seed: int = 0) -> dict:
    key_list = jax.random.split(jax.random.key(seed), 15)
    return {
        "inputs": normal_values(key_list[0], (MB, TOK_MB, MODEL_WIDTH), 1.0, 6.0, ((1, 32),)),
        "segments": draw_segments(jax.random.fold_in(key_list[14], 71), 0),
        "attn_gain": jnp.clip(1.0 + 0.1 * jax.random.normal(key_list[2], (MODEL_WIDTH,), jnp.float32), 0.5, 1.5).astype(jnp.bfloat16),
        "w_query": normal_values(key_list[3], (MODEL_WIDTH, QUERY_HEADS * HEAD_SIZE), MODEL_WIDTH ** -0.5, 0.1875, ((0, 32),)),
        "key_projection": normal_values(key_list[4], (MODEL_WIDTH, KEY_VALUE_HEADS * HEAD_SIZE), MODEL_WIDTH ** -0.5, 0.1875, ((0, 32),)),
        "value_projection": normal_values(key_list[5], (MODEL_WIDTH, KEY_VALUE_HEADS * HEAD_SIZE), MODEL_WIDTH ** -0.5, 0.1875, ((0, 32),)),
        "w_output": normal_values(key_list[6], (QUERY_HEADS * HEAD_SIZE, MODEL_WIDTH), (QUERY_HEADS * HEAD_SIZE // 32) ** -0.5, 1.0, ((1, 32),)),
        "query_gain": jnp.clip(1.0 + 0.1 * jax.random.normal(key_list[7], (HEAD_SIZE,), jnp.float32), 0.5, 1.5).astype(jnp.bfloat16),
        "key_norm_gain": jnp.clip(1.0 + 0.1 * jax.random.normal(key_list[8], (HEAD_SIZE,), jnp.float32), 0.5, 1.5).astype(jnp.bfloat16),
        "ffn_gain": jnp.clip(1.0 + 0.1 * jax.random.normal(key_list[9], (MODEL_WIDTH,), jnp.float32), 0.5, 1.5).astype(jnp.bfloat16),
        "w_gate": normal_values(key_list[10], (MODEL_WIDTH, FF), MODEL_WIDTH ** -0.5, 0.1875, ((0, 32),)),
        "w_up": normal_values(key_list[11], (MODEL_WIDTH, FF), MODEL_WIDTH ** -0.5, 0.1875, ((0, 32),)),
        "w_down": normal_values(key_list[12], (FF, MODEL_WIDTH), FF ** -0.5, 0.09375, ((1, 32),)),
        "cotangent": normal_values(key_list[13], (MB, TOK_MB, MODEL_WIDTH), 1.0, 6.0, ((1, 32),)),
    }


EPS = 1e-05
THETA = 1000000.0
NEG = -1e+30

@jax.custom_vjp
def low(v):
    return lax.optimization_barrier(v.astype(jnp.bfloat16)).astype(jnp.float32)

@jax.custom_vjp
def low_back(v):
    return v

def low_keep(v):
    return (low(v), None)

def low_pass(kept, grad):
    return (grad,)

def back_keep(v):
    return (v, None)

def back_low(kept, grad):
    return (low(grad),)
low.defvjp(low_keep, low_pass)
low_back.defvjp(back_keep, back_low)

def row_norm(values, gain_row):
    return values * lax.rsqrt(lax.optimization_barrier(jnp.mean(values * values, axis=-1, keepdims=True)) + EPS) * gain_row

def angles(places, head_width):
    counter = jnp.arange(head_width // 2, dtype=jnp.float32)
    inverse = jnp.power(jnp.float32(THETA), -2.0 * counter / head_width)
    turned = places.astype(jnp.float32)[:, None] * inverse[None, :]
    return (jnp.cos(turned), jnp.sin(turned))

def prepare_inputs(raw_rows, gain_row, cosine_table, sine_table_rows, head_count):
    token_count = raw_rows.shape[0]
    head_width = gain_row.shape[0]
    split_rows = raw_rows.reshape(token_count, head_count, head_width)
    normed = row_norm(split_rows, gain_row)
    first_half = normed[..., :head_width // 2]
    second = normed[..., head_width // 2:]
    cos_rows = cosine_table[:, None, :]
    sin_rows = sine_table_rows[:, None, :]
    turned = jnp.concatenate([first_half * cos_rows - second * sin_rows, second * cos_rows + first_half * sin_rows], axis=-1)
    return turned.reshape(token_count, head_count * head_width)

def mat_high(left_rows, right_rows):
    return jnp.dot(left_rows, right_rows, precision=lax.Precision.HIGHEST, preferred_element_type=jnp.float32)

def doc_places(segment):
    lower_count = lax.optimization_barrier(jnp.sum((segment[:, None, :] < segment[:, :, None]).astype(jnp.int32), axis=2))
    return jnp.arange(segment.shape[1], dtype=jnp.int32)[None, :] - lower_count

def group_forward(hidden, segment, params):
    attn_gain, w_query, key_projection, value_projection, w_output, query_gain, key_norm_gain, ffn_gain, w_gate, w_up, w_down = params
    document_runs, length_total = segment.shape
    token_count = document_runs * length_total
    heads_per_group = QUERY_HEADS // KEY_VALUE_HEADS
    normed = low(row_norm(hidden, attn_gain))
    query_raw = low_back(mat_high(normed, w_query))
    key_projected = low_back(mat_high(normed, key_projection))
    value_reduced = low(low_back(mat_high(normed, value_projection)))
    cosine_table, sine_table_rows = angles(doc_places(segment).reshape(token_count), HEAD_SIZE)
    query_rotated = low(prepare_inputs(query_raw, query_gain, cosine_table, sine_table_rows, QUERY_HEADS))
    key_rotated = low(prepare_inputs(key_projected, key_norm_gain, cosine_table, sine_table_rows, KEY_VALUE_HEADS))
    query_head_rows = query_rotated.reshape(document_runs, length_total, KEY_VALUE_HEADS, heads_per_group, HEAD_SIZE)
    key_head_rows = key_rotated.reshape(document_runs, length_total, KEY_VALUE_HEADS, HEAD_SIZE)
    value_head_rows = value_reduced.reshape(document_runs, length_total, KEY_VALUE_HEADS, HEAD_SIZE)
    scores = jnp.einsum('bihgd,bjhd->bhgij', query_head_rows, key_head_rows, precision=lax.Precision.HIGHEST) * (1.0 / math.sqrt(HEAD_SIZE))
    places = jnp.arange(length_total, dtype=jnp.int32)
    allowed = (places[None, :] <= places[:, None])[None] & (segment[:, None, :] == segment[:, :, None])
    scores = low_back(jnp.where(allowed[:, None, None], scores, NEG))
    row_peak = lax.optimization_barrier(jnp.max(scores, axis=-1, keepdims=True))
    raised = jnp.exp(scores - row_peak)
    prob_rows = low(raised / lax.optimization_barrier(jnp.sum(raised, axis=-1, keepdims=True)))
    attn_mix = jnp.einsum('bhgij,bjhd->bihgd', prob_rows, value_head_rows, precision=lax.Precision.HIGHEST)
    attn_mix = low(low_back(attn_mix.reshape(token_count, QUERY_HEADS * HEAD_SIZE)))
    attended = hidden + low_back(mat_high(attn_mix, w_output))
    ffn_in = low(row_norm(attended, ffn_gain))
    gate_raw = low_back(mat_high(ffn_in, w_gate))
    upward = low_back(mat_high(ffn_in, w_up))
    active = low(gate_raw * jax.nn.sigmoid(gate_raw) * upward)
    return attended + low_back(mat_high(active, w_down))

def layer_forward(hidden, segment, params):
    token_count = hidden.shape[0]
    document_runs = token_count // SEQ
    group_runs = math.gcd(max(1, 4096 // SEQ), document_runs)
    group_count = document_runs // group_runs
    hidden_groups = hidden.reshape(group_count, group_runs * SEQ, MODEL_WIDTH)
    segment_groups = segment.reshape(group_count, group_runs, SEQ)
    checked = jax.checkpoint(lambda part_hidden, part_segment: group_forward(part_hidden, part_segment, params))

    def advance(running, blocks):
        return (running, checked(blocks[0], blocks[1]))
    running, result = lax.scan(advance, jnp.zeros((), jnp.float32), (hidden_groups, segment_groups))
    return result.reshape(token_count, MODEL_WIDTH)

def reference(inputs, segments, attn_gain, w_query, key_projection, value_projection, w_output, query_gain, key_norm_gain, ffn_gain, w_gate, w_up, w_down, cotangent):
    params = tuple((weight.astype(jnp.float32) for weight in (attn_gain, w_query, key_projection, value_projection, w_output, query_gain, key_norm_gain, ffn_gain, w_gate, w_up, w_down)))
    outputs_list = []
    grads_list = []
    totals = None
    for batch_index in range(MB):
        hidden = inputs[batch_index].astype(jnp.float32)
        segment = segments[batch_index]
        result, pullback = jax.vjp(lambda moved, weights: layer_forward(moved, segment, weights), hidden, params)
        grad_hidden, grad_params = pullback(cotangent[batch_index].astype(jnp.float32))
        outputs_list.append(result.astype(jnp.bfloat16))
        grads_list.append(grad_hidden.astype(jnp.bfloat16))
        totals = grad_params if totals is None else jax.tree.map(jnp.add, totals, grad_params)
    return (jnp.stack(outputs_list), jnp.stack(grads_list), totals[0], totals[1], totals[2], totals[3], totals[4], totals[5], totals[6], totals[7], totals[8], totals[9], totals[10])
```

```python
import functools
import math

import jax
import jax.numpy as jnp
from jax import lax
from jax.experimental import pallas as pl
from jax.experimental.pallas import tpu as pltpu
from jax.sharding import PartitionSpec as P

SEQ = 1024
CHUNKS = 11
WIDE = 768
MESH = pl.DeviceIdType.MESH
ALL = slice(None)
F32 = jnp.float32
BF16 = jnp.bfloat16
PARTS = (
    ("A", pl.ds(0, 48), pl.ds(0, 384)),
    ("B", pl.ds(0, 48), pl.ds(384, 384)),
    ("C", pl.ds(48, 16), pl.ds(0, 768)),
)
OUTWARD = {
    "A": ("z0", "z1", "z2", "y", "x"),
    "B": ("z0", "z1", "z2", "x", "y"),
    "C": ("x", "y", "z0", "z1", "z2"),
}
INWARD = {
    "A": ("x", "y", "z0", "z1", "z2"),
    "B": ("y", "x", "z0", "z1", "z2"),
    "C": ("z0", "z1", "z2", "y", "x"),
}
SUM_SLOTS = 7
LAND_SLOTS = 3


def place():
    me = lax.axis_index("fsdp")
    return me, me // 8, (me // 4) % 2, (me // 2) % 2, me % 2


def guarded(condition, action):
    if condition is None:
        action()
    else:
        pl.when(condition)(action)


def greet(me, z):
    gate = pltpu.get_barrier_semaphore()
    for bit in (1, 2, 4):
        pl.semaphore_signal(gate, inc=1, device_id=(me ^ bit,), device_id_type=MESH)

    @pl.when(z > 0)
    def _():
        pl.semaphore_signal(gate, inc=1, device_id=(me - 8,), device_id_type=MESH)

    @pl.when(z < 3)
    def _():
        pl.semaphore_signal(gate, inc=1, device_id=(me + 8,), device_id_type=MESH)

    pl.semaphore_wait(gate, 3 + (z > 0).astype(jnp.int32) + (z < 3).astype(jnp.int32))


class Gather:
    def __init__(self, full, sent, landed):
        self.full, self.sent, self.landed = full, sent, landed
        self.me, self.z, self.y, self.x, self.core = place()

    def moves(self, part, step, chunk):
        kind, rows, columns = PARTS[part]
        z, y, x, me = self.z, self.y, self.x, self.me

        def view(zz, yy, xx):
            return self.full.at[chunk, zz, yy, xx, rows, columns]

        axis = OUTWARD[kind][step]
        if axis[0] == "z":
            far = int(axis[1])
            yy, xx = (ALL, ALL) if kind == "C" else (y, x)
            return (
                ((z >= far) & (z < 3), z - far, me + 8, z >= far + 1, z - 1 - far),
                ((z <= 3 - far) & (z > 0), z + far, me - 8, z <= 2 - far, z + 1 + far),
            ), lambda zz: view(zz, yy, xx)
        zz = z if kind == "C" else ALL
        if axis == "y":
            xx = x if kind == "A" else ALL
            return ((None, y, me ^ 4, None, 1 - y),), lambda yy: view(zz, yy, xx)
        yy = ALL if kind == "A" else y
        return ((None, x, me ^ 2, None, 1 - x),), lambda xx: view(zz, yy, xx)

    def copy(self, ref, device, part, step, chunk, way):
        return pltpu.make_async_remote_copy(
            src_ref=ref,
            dst_ref=ref,
            send_sem=self.sent.at[chunk, part, step, way],
            recv_sem=self.landed.at[chunk, part, step, way],
            device_id=(device,),
            device_id_type=MESH,
        )

    def send(self, part, step, chunk):
        moves, view = self.moves(part, step, chunk)
        for way, (sends, mine, device, _, _) in enumerate(moves):
            guarded(
                sends,
                lambda: self.copy(view(mine), device, part, step, chunk, way).start(),
            )

    def receive(self, part, step, chunk):
        moves, view = self.moves(part, step, chunk)
        for way, (_, _, _, receives, other) in enumerate(moves):
            guarded(
                receives,
                lambda: self.copy(view(other), self.me ^ 2, part, step, chunk, way).wait_recv(),
            )

    def finish(self, part, step, chunk):
        moves, view = self.moves(part, step, chunk)
        for way, (sends, mine, device, _, _) in enumerate(moves):
            guarded(
                sends,
                lambda: self.copy(view(mine), device, part, step, chunk, way).wait_send(),
            )

    def tick(self, time):
        for step in range(6):
            chunk = time - step

            @pl.when((chunk >= 0) & (chunk < CHUNKS))
            def _():
                for part in range(len(PARTS)):
                    if step > 0:
                        self.receive(part, step - 1, chunk)
                    if step < 5:
                        self.send(part, step, chunk)

    def drain(self):
        def body(chunk, carry):
            for part in range(len(PARTS)):
                for step in range(5):
                    self.finish(part, step, chunk)
            return carry

        lax.fori_loop(0, CHUNKS, body, 0)


class Scatter:
    def __init__(self, sums, lands, totals, sent, landed):
        self.sums, self.lands, self.totals = sums, lands, totals
        self.sent, self.landed = sent, landed
        self.me, self.z, self.y, self.x, self.core = place()

    def moves(self, part, step, chunk):
        kind, rows, columns = PARTS[part]
        z, y, x, me = self.z, self.y, self.x, self.me
        slot, land = lax.rem(chunk, SUM_SLOTS), lax.rem(chunk, LAND_SLOTS)
        first, second, up, down = self.lands[part]
        axis = INWARD[kind][step]

        def view(zz, yy, xx):
            return self.sums.at[slot, zz, yy, xx, rows, columns]

        if axis[0] == "z":
            far = int(axis[1])
            count = 3 - far
            yy, xx = (ALL, ALL) if kind == "C" else (y, x)
            above, below = pl.ds(far + 1, count), pl.ds(0, count)
            up_land, down_land = up.at[land, pl.ds(far, count)], down.at[land, pl.ds(0, count)]
            return (
                (z == far, view(above, yy, xx), up_land, me + 8, z == far + 1, view(above, yy, xx)),
                (z == 3 - far, view(below, yy, xx), down_land, me - 8, z == 2 - far, view(below, yy, xx)),
            )
        zz = z if kind == "C" else ALL
        ref = (first if step == 0 or (kind == "C" and step == 3) else second).at[land]
        if axis == "x":
            yy = ALL if kind == "A" else y
            return ((None, view(zz, yy, 1 - x), ref, me ^ 2, None, view(zz, yy, x)),)
        xx = x if kind == "A" else ALL
        return ((None, view(zz, 1 - y, xx), ref, me ^ 4, None, view(zz, y, xx)),)

    def copy(self, source, target, device, part, step, chunk, way):
        return pltpu.make_async_remote_copy(
            src_ref=source,
            dst_ref=target,
            send_sem=self.sent.at[chunk, part, step, way],
            recv_sem=self.landed.at[chunk, part, step, way],
            device_id=(device,),
            device_id_type=MESH,
        )

    def step(self, part, step, chunk):
        if step > 0:
            for way, move in enumerate(self.moves(part, step - 1, chunk)):
                sends, source, land, device, receives, target = move

                def add():
                    self.copy(land, land, self.me ^ 2, part, step - 1, chunk, way).wait_recv()
                    target[...] = (target[...].astype(F32) + land[...].astype(F32)).astype(BF16)

                guarded(receives, add)
                guarded(
                    sends,
                    lambda: self.copy(source, land, device, part, step - 1, chunk, way).wait_send(),
                )
        if step < 5:
            for way, move in enumerate(self.moves(part, step, chunk)):
                sends, source, land, device, _, _ = move
                guarded(
                    sends,
                    lambda: self.copy(source, land, device, part, step, chunk, way).start(),
                )
        else:
            _, rows, columns = PARTS[part]
            slot = lax.rem(chunk, SUM_SLOTS)
            self.totals[chunk, rows, columns] = self.sums[
                slot, self.z, self.y, self.x, rows, columns
            ].astype(F32)

    def tick(self, time, ready):
        for step in range(5, -1, -1):
            chunk = time - step

            @pl.when((chunk >= 0) & (chunk < CHUNKS))
            def _():
                if step == 0:
                    ready(chunk)
                for part in range(len(PARTS)):
                    self.step(part, step, chunk)


def pair_rows(core):
    mine = pl.ds(pl.multiple_of(core * 32, 32), 32)
    other = pl.ds(pl.multiple_of((1 - core) * 32, 32), 32)
    return mine, other


def gather_kernel(w_ref, o_ref, full, local_sem, pair_sent, pair_landed, sent, landed):
    me, z, y, x, core = place()
    greet(me, z)
    mine, other = pair_rows(core)

    def to_pair(rows):
        return pltpu.make_async_remote_copy(
            src_ref=w_ref.at[1 - core],
            dst_ref=full.at[:, z, y, x, rows, :],
            send_sem=pair_sent,
            recv_sem=pair_landed,
            device_id=(me ^ 1,),
            device_id_type=MESH,
        )

    own = pltpu.make_async_copy(w_ref.at[core], full.at[:, z, y, x, mine, :], local_sem)
    own.start()
    to_pair(mine).start()
    own.wait()
    to_pair(mine).wait_send()
    to_pair(other).wait_recv()
    gather = Gather(full, sent, landed)

    def body(time, carry):
        gather.tick(time)
        return carry

    lax.fori_loop(0, CHUNKS + 5, body, 0)
    gather.drain()
    out = pltpu.make_async_copy(full, o_ref, local_sem)
    out.start()
    out.wait()


def scatter_kernel(d_ref, o_ref, sums, *rest):
    lands = (rest[0:4], rest[4:8], rest[8:12])
    totals, load_sem, pair_sent, pair_landed, sent, landed = rest[12:]
    me, z, y, x, core = place()
    greet(me, z)
    mine, other = pair_rows(core)
    scatter = Scatter(sums, lands, totals, sent, landed)

    def load(chunk):
        return pltpu.make_async_copy(
            d_ref.at[chunk], sums.at[lax.rem(chunk, SUM_SLOTS)], load_sem.at[lax.rem(chunk, 2)]
        )

    load(0).start()

    def ready(chunk):
        @pl.when(chunk + 1 < CHUNKS)
        def _():
            load(chunk + 1).start()

        load(chunk).wait()

    def body(time, carry):
        scatter.tick(time, ready)
        return carry

    lax.fori_loop(0, CHUNKS + 5, body, 0)

    def to_pair(half):
        return pltpu.make_async_remote_copy(
            src_ref=totals.at[:, other, :],
            dst_ref=o_ref.at[half],
            send_sem=pair_sent,
            recv_sem=pair_landed,
            device_id=(me ^ 1,),
            device_id_type=MESH,
        )

    own = pltpu.make_async_copy(totals.at[:, mine, :], o_ref.at[core], load_sem.at[0])
    own.start()
    to_pair(core).start()
    to_pair(core).wait_send()
    to_pair(1 - core).wait_recv()
    own.wait()


def semaphores():
    return [pltpu.SemaphoreType.DMA((CHUNKS, len(PARTS), 5, 2))] * 2


def land_shapes():
    slots = LAND_SLOTS
    plain = [(slots, 4, 2, 48, 384), (slots, 4, 48, 384), (slots, 3, 48, 384), (slots, 3, 48, 384)]
    late = [(slots, 2, 16, 768), (slots, 16, 768), (slots, 3, 2, 2, 16, 768), (slots, 3, 2, 2, 16, 768)]
    return [pltpu.VMEM(shape, BF16) for shape in plain + plain + late]


def params(number):
    return pltpu.CompilerParams(
        collective_id=number, has_side_effects=True, vmem_limit_bytes=60 * 2**20
    )


def pair_swap(block):
    return lax.ppermute(block, "fsdp", [(i, i ^ 1) for i in range(lax.axis_size("fsdp"))])


def gather_grid(w_query, w_key, w_value, w_output, w_gate, w_up, w_down):
    rows = w_query.shape[0]
    halves = [
        jnp.stack(jnp.split(w, 2, axis=1)) for w in (w_query, w_key, w_value, w_output.T)
    ]
    first = jnp.concatenate(halves[:2], axis=2)[:, None]
    second = jnp.concatenate(halves[2:], axis=2)[:, None]
    wide = jnp.concatenate(
        [w.reshape(rows, 2, CHUNKS - 2, 256).transpose(1, 2, 0, 3) for w in (w_gate, w_up, w_down.T)],
        axis=3,
    )
    packed = jnp.concatenate([first, second, wide], axis=1)
    full = pl.pallas_call(
        gather_kernel,
        out_shape=jax.ShapeDtypeStruct((CHUNKS, 4, 2, 2, 64, WIDE), BF16),
        in_specs=[pl.BlockSpec(memory_space=pl.ANY)],
        out_specs=pl.BlockSpec(memory_space=pl.ANY),
        scratch_shapes=[pltpu.VMEM((CHUNKS, 4, 2, 2, 64, WIDE), BF16)]
        + [pltpu.SemaphoreType.DMA] * 3
        + semaphores(),
        compiler_params=params(0),
        name="gather",
    )(packed)
    full = full.reshape(CHUNKS, 1024, WIDE)
    other = pair_swap(full)
    core = lax.axis_index("fsdp") % 2
    low, high = jnp.where(core == 0, full, other), jnp.where(core == 0, other, full)

    def both(chunk, start, stop):
        return jnp.concatenate([low[chunk, :, start:stop], high[chunk, :, start:stop]], axis=1)

    def wide_of(start):
        parts = [half[2:, :, start : start + 256].transpose(1, 0, 2).reshape(1024, -1) for half in (low, high)]
        return jnp.concatenate(parts, axis=1)

    return (
        both(0, 0, 512),
        both(0, 512, 768),
        both(1, 0, 256),
        both(1, 256, 768).T,
        wide_of(0),
        wide_of(256),
        wide_of(512).T,
    )


def scatter_all(sums):
    attn_gain, w_query, w_key, w_value, w_output, ffn_gain, w_gate, w_up, w_down = sums
    halves = [jnp.stack(jnp.split(w, 2, axis=1)) for w in (w_query, w_key, w_value, w_output)]
    first = jnp.concatenate(halves[:2], axis=2)[:, None]
    second = jnp.concatenate(halves[2:], axis=2)[:, None]
    wide = jnp.concatenate(
        [w.reshape(1024, 2, CHUNKS - 2, 256).transpose(1, 2, 0, 3) for w in (w_gate, w_up, w_down)],
        axis=3,
    )
    packed = jnp.concatenate([first, second, wide], axis=1)
    core = lax.axis_index("fsdp") % 2
    other = pair_swap(packed[1 - core].astype(BF16))
    terms = (packed[core] + other.astype(F32)).astype(BF16)
    out = pl.pallas_call(
        scatter_kernel,
        out_shape=jax.ShapeDtypeStruct((2, CHUNKS, 32, WIDE), F32),
        in_specs=[pl.BlockSpec(memory_space=pl.ANY)],
        out_specs=pl.BlockSpec(memory_space=pl.ANY),
        scratch_shapes=[pltpu.VMEM((SUM_SLOTS, 4, 2, 2, 64, WIDE), BF16)]
        + land_shapes()
        + [pltpu.VMEM((CHUNKS, 64, WIDE), F32), pltpu.SemaphoreType.DMA((2,))]
        + [pltpu.SemaphoreType.DMA] * 2
        + semaphores(),
        compiler_params=params(1),
        name="scatter",
    )(terms.reshape(CHUNKS, 4, 2, 2, 64, WIDE))

    def both(chunk, start, stop):
        return jnp.concatenate([out[0, chunk, :, start:stop], out[1, chunk, :, start:stop]], axis=1)

    def wide_of(start):
        return out[:, 2:, :, start : start + 256].transpose(2, 0, 1, 3).reshape(32, -1)

    def gain(term):
        return lax.psum_scatter(term, "fsdp", scatter_dimension=0, tiled=True)

    return (
        gain(attn_gain),
        both(0, 0, 512),
        both(0, 512, 768),
        both(1, 0, 256),
        both(1, 256, 768),
        gain(ffn_gain),
        wide_of(0),
        wide_of(256),
        wide_of(512),
    )


EPS = 1e-05
THETA = 1000000.0
NEG = -1e30


def from_behind(block, axis, distance):
    devices = range(lax.axis_size(axis))
    route = [(i - distance, i) for i in devices if i - distance in devices]
    return lax.ppermute(block, axis, route)


def row_norm(values, gain_row):
    return values * lax.rsqrt(jnp.mean(values * values, axis=-1, keepdims=True) + EPS) * gain_row


def angles(places, head_width):
    counter = jnp.arange(head_width // 2, dtype=jnp.float32)
    inverse = jnp.power(jnp.float32(THETA), -2.0 * counter / head_width)
    turned = places.astype(jnp.float32)[:, None] * inverse[None, :]
    return (jnp.cos(turned), jnp.sin(turned))


def prepare_inputs(raw_rows, gain_row, cosine_table, sine_table_rows, head_count):
    token_count = raw_rows.shape[0]
    head_width = gain_row.shape[0]
    split_rows = raw_rows.reshape(token_count, head_count, head_width)
    normed = row_norm(split_rows, gain_row)
    first_half = normed[..., : head_width // 2]
    second = normed[..., head_width // 2 :]
    cos_rows = cosine_table[:, None, :]
    sin_rows = sine_table_rows[:, None, :]
    turned = jnp.concatenate(
        [first_half * cos_rows - second * sin_rows, second * cos_rows + first_half * sin_rows],
        axis=-1,
    )
    return turned.reshape(token_count, head_count * head_width)


def plain_product(left_rows, right_rows):
    return jnp.dot(left_rows, right_rows, preferred_element_type=jnp.float32)


def rows_product(left_rows, right_rows):
    return lax.dot_general(
        left_rows, right_rows, (((0,), (0,)), ((), ())), preferred_element_type=jnp.float32
    )


def cols_product(left_rows, right_rows):
    return lax.dot_general(
        left_rows, right_rows, (((1,), (1,)), ((), ())), preferred_element_type=jnp.float32
    )


def silu_product(gate_raw, upward):
    return gate_raw * jax.nn.sigmoid(gate_raw) * upward


def add_sets(former_set, latter_set):
    if former_set is None:
        return latter_set
    return tuple((former + latter for former, latter in zip(former_set, latter_set)))


def local(
    inputs,
    segments,
    attn_gain,
    w_query,
    key_projection,
    value_projection,
    w_output,
    query_gain,
    key_norm_gain,
    ffn_gain,
    w_gate,
    w_up,
    w_down,
    cotangent,
):
    batches = inputs.shape[0]
    tokens = inputs.shape[1]
    head_width = query_gain.shape[0]
    query_width = w_query.shape[1]
    kv_width = key_projection.shape[1]
    query_head_rows = query_width // head_width
    kv_heads = kv_width // head_width
    heads_per_group = query_head_rows // kv_heads
    scale = 1.0 / math.sqrt(head_width)
    query_gain_f = query_gain.astype(jnp.float32)
    key_gain_f = key_norm_gain.astype(jnp.float32)
    device_index = lax.axis_index("fsdp")
    places_row = jnp.arange(tokens, dtype=jnp.int32)
    causal = places_row[None, :] <= places_row[:, None]
    same_run = device_index * tokens // SEQ == (device_index - 1) * tokens // SEQ
    outputs_list = []
    grads_list = []
    shard_sums = None
    gain_sums = None
    for batch_index in range(batches):
        gathered = (
            lax.all_gather(attn_gain, "fsdp", axis=0, tiled=True),
            lax.all_gather(w_query, "fsdp", axis=0, tiled=True),
            lax.all_gather(key_projection, "fsdp", axis=0, tiled=True),
            lax.all_gather(value_projection, "fsdp", axis=0, tiled=True),
            lax.all_gather(w_output, "fsdp", axis=1, tiled=True),
            lax.all_gather(ffn_gain, "fsdp", axis=0, tiled=True),
            lax.all_gather(w_gate, "fsdp", axis=0, tiled=True),
            lax.all_gather(w_up, "fsdp", axis=0, tiled=True),
            lax.all_gather(w_down, "fsdp", axis=1, tiled=True),
        )
        (
            gain_attn,
            full_query,
            full_key,
            full_value,
            full_output,
            gain_ffn,
            full_gate,
            full_up,
            full_down,
        ) = gathered
        hidden = inputs[batch_index].astype(jnp.float32)
        segment = segments[batch_index]
        normed_f, norm_pull = jax.vjp(row_norm, hidden, gain_attn.astype(jnp.float32))
        normed = normed_f.astype(jnp.bfloat16)
        query_raw = plain_product(normed, full_query)
        key_projected = plain_product(normed, full_key)
        value_reduced = plain_product(normed, full_value).astype(jnp.bfloat16)
        lower_count = jnp.sum((segment[None, :] < segment[:, None]).astype(jnp.int32), axis=1)
        local_places = places_row - lower_count
        cos_local, sin_local = angles(local_places, head_width)
        key_sent = prepare_inputs(key_projected, key_gain_f, cos_local, sin_local, kv_heads).astype(
            jnp.bfloat16
        )
        remote_key, remote_value, remote_segment = from_behind(
            (key_sent, value_reduced, segment.astype(jnp.bfloat16)), "fsdp", 1
        )
        remote_match = (remote_segment.astype(jnp.int32)[None, :] == segment[:, None]) & same_run
        places_all = local_places + jnp.sum(remote_match.astype(jnp.int32), axis=1)
        cosine_table, sine_table_rows = angles(places_all, head_width)
        query_f, query_pull = jax.vjp(
            lambda raw_rows, gain_row: prepare_inputs(
                raw_rows, gain_row, cosine_table, sine_table_rows, query_head_rows
            ),
            query_raw,
            query_gain_f,
        )
        key_f, key_pull = jax.vjp(
            lambda raw_rows, gain_row: prepare_inputs(
                raw_rows, gain_row, cosine_table, sine_table_rows, kv_heads
            ),
            key_projected,
            key_gain_f,
        )
        query_low = query_f.astype(jnp.bfloat16)
        key_low = key_f.astype(jnp.bfloat16)
        allowed = jnp.concatenate(
            [remote_match, causal & (segment[None, :] == segment[:, None])], axis=1
        )
        query_split = query_low.reshape(tokens, kv_heads, heads_per_group, head_width).transpose(
            1, 0, 2, 3
        )
        key_split = (
            jnp.concatenate([remote_key, key_low], axis=0)
            .reshape(2 * tokens, kv_heads, head_width)
            .transpose(1, 0, 2)
        )
        value_split = (
            jnp.concatenate([remote_value, value_reduced], axis=0)
            .reshape(2 * tokens, kv_heads, head_width)
            .transpose(1, 0, 2)
        )

        def head_forward(blocks):
            query_part, key_part, value_part = blocks
            scores = (
                jnp.einsum("tgd,ld->gtl", query_part, key_part, preferred_element_type=jnp.float32)
                * scale
            )
            scores = jnp.where(allowed[None], scores, NEG)
            row_peak = jnp.max(scores, axis=-1, keepdims=True)
            raised = jnp.exp(scores - row_peak)
            row_total = jnp.sum(raised, axis=-1, keepdims=True)
            prob_rows = (raised / row_total).astype(jnp.bfloat16)
            mixed_part = jnp.einsum(
                "gtl,ld->tgd", prob_rows, value_part, preferred_element_type=jnp.float32
            )
            return (mixed_part.astype(jnp.bfloat16), (row_peak + jnp.log(row_total))[..., 0])

        mixed_split, log_totals = lax.map(head_forward, (query_split, key_split, value_split))
        attn_mix = mixed_split.transpose(1, 0, 2, 3).reshape(tokens, query_width)
        attended = hidden + plain_product(attn_mix, full_output)
        ffn_f, ffn_pull = jax.vjp(row_norm, attended, gain_ffn.astype(jnp.float32))
        ffn_in = ffn_f.astype(jnp.bfloat16)
        gate_raw = plain_product(ffn_in, full_gate)
        upward = plain_product(ffn_in, full_up)
        active_f, active_pull = jax.vjp(silu_product, gate_raw, upward)
        active = active_f.astype(jnp.bfloat16)
        result = attended + plain_product(active, full_down)
        outputs_list.append(result.astype(jnp.bfloat16))
        back_query, back_key, back_value, back_output, back_gate, back_up, back_down = (
            lax.all_gather(w_query, "fsdp", axis=0, tiled=True),
            lax.all_gather(key_projection, "fsdp", axis=0, tiled=True),
            lax.all_gather(value_projection, "fsdp", axis=0, tiled=True),
            lax.all_gather(w_output, "fsdp", axis=1, tiled=True),
            lax.all_gather(w_gate, "fsdp", axis=0, tiled=True),
            lax.all_gather(w_up, "fsdp", axis=0, tiled=True),
            lax.all_gather(w_down, "fsdp", axis=1, tiled=True),
        )
        grad_result = cotangent[batch_index]
        grad_down_t = rows_product(grad_result, active)
        grad_active = cols_product(grad_result, back_down)
        grad_gate_f, grad_up_f = active_pull(grad_active)
        grad_gate_low = grad_gate_f.astype(jnp.bfloat16)
        grad_up_low = grad_up_f.astype(jnp.bfloat16)
        grad_gate_w = rows_product(ffn_in, grad_gate_low)
        grad_up_w = rows_product(ffn_in, grad_up_low)
        grad_ffn_in = cols_product(grad_gate_low, back_gate) + cols_product(grad_up_low, back_up)
        grad_attended_norm, grad_ffn_gain = ffn_pull(grad_ffn_in)
        grad_attended = grad_result.astype(jnp.float32) + grad_attended_norm
        grad_branch = grad_attended.astype(jnp.bfloat16)
        grad_output_t = rows_product(grad_branch, attn_mix)
        grad_mixed = cols_product(grad_branch, back_output).astype(jnp.bfloat16)
        grad_split = grad_mixed.reshape(tokens, kv_heads, heads_per_group, head_width).transpose(
            1, 0, 2, 3
        )

        def head_backward(blocks):
            query_part, key_part, value_part, grad_part, log_part = blocks
            scores = (
                jnp.einsum("tgd,ld->gtl", query_part, key_part, preferred_element_type=jnp.float32)
                * scale
            )
            scores = jnp.where(allowed[None], scores, NEG)
            prob_rows = jnp.exp(scores - log_part[..., None])
            grad_probs = jnp.einsum(
                "tgd,ld->gtl", grad_part, value_part, preferred_element_type=jnp.float32
            )
            center = jnp.sum(prob_rows * grad_probs, axis=-1, keepdims=True)
            grad_scores = (prob_rows * (grad_probs - center)).astype(jnp.bfloat16)
            grad_query_part = (
                jnp.einsum("gtl,ld->tgd", grad_scores, key_part, preferred_element_type=jnp.float32)
                * scale
            )
            grad_key_part = (
                jnp.einsum(
                    "gtl,tgd->ld", grad_scores, query_part, preferred_element_type=jnp.float32
                )
                * scale
            )
            grad_value_part = jnp.einsum(
                "gtl,tgd->ld",
                prob_rows.astype(jnp.bfloat16),
                grad_part,
                preferred_element_type=jnp.float32,
            )
            return (grad_query_part, grad_key_part, grad_value_part)

        grad_query_split, grad_key_split, grad_value_split = lax.map(
            head_backward, (query_split, key_split, value_split, grad_split, log_totals)
        )
        grad_query_rot = grad_query_split.transpose(1, 0, 2, 3).reshape(tokens, query_width)
        grad_key_all = grad_key_split.transpose(1, 0, 2).reshape(2 * tokens, kv_width)
        grad_value_all = grad_value_split.transpose(1, 0, 2).reshape(2 * tokens, kv_width)
        back_key_grad, back_value_grad = (
            from_behind(grad_key_all[:tokens].astype(jnp.bfloat16), "fsdp", -1).astype(jnp.float32),
            from_behind(grad_value_all[:tokens].astype(jnp.bfloat16), "fsdp", -1).astype(
                jnp.float32
            ),
        )
        grad_key_rot = grad_key_all[tokens:] + back_key_grad
        grad_value_low = (grad_value_all[tokens:] + back_value_grad).astype(jnp.bfloat16)
        grad_query_raw, grad_query_gain = query_pull(grad_query_rot)
        grad_key_raw, grad_key_gain = key_pull(grad_key_rot)
        grad_query_low = grad_query_raw.astype(jnp.bfloat16)
        grad_key_low = grad_key_raw.astype(jnp.bfloat16)
        grad_query_w = rows_product(normed, grad_query_low)
        grad_key_w = rows_product(normed, grad_key_low)
        grad_value_w = rows_product(normed, grad_value_low)
        grad_normed = (
            cols_product(grad_query_low, back_query)
            + cols_product(grad_key_low, back_key)
            + cols_product(grad_value_low, back_value)
        )
        grad_hidden_norm, grad_attn_gain = norm_pull(grad_normed)
        grads_list.append((grad_attended + grad_hidden_norm).astype(jnp.bfloat16))
        gain_sums = add_sets(gain_sums, (grad_query_gain, grad_key_gain))
        shard_terms = (
            lax.psum_scatter(grad_attn_gain, "fsdp", scatter_dimension=0, tiled=True),
            lax.psum_scatter(grad_query_w, "fsdp", scatter_dimension=0, tiled=True),
            lax.psum_scatter(grad_key_w, "fsdp", scatter_dimension=0, tiled=True),
            lax.psum_scatter(grad_value_w, "fsdp", scatter_dimension=0, tiled=True),
            lax.psum_scatter(grad_output_t, "fsdp", scatter_dimension=0, tiled=True),
            lax.psum_scatter(grad_ffn_gain, "fsdp", scatter_dimension=0, tiled=True),
            lax.psum_scatter(grad_gate_w, "fsdp", scatter_dimension=0, tiled=True),
            lax.psum_scatter(grad_up_w, "fsdp", scatter_dimension=0, tiled=True),
            lax.psum_scatter(grad_down_t, "fsdp", scatter_dimension=0, tiled=True),
        )
        shard_sums = add_sets(shard_sums, shard_terms)
    head_sums = lax.psum((gain_sums[0], gain_sums[1]), "fsdp")
    return (
        jnp.stack(outputs_list),
        jnp.stack(grads_list),
        shard_sums[0],
        shard_sums[1],
        shard_sums[2],
        shard_sums[3],
        shard_sums[4].T,
        head_sums[0],
        head_sums[1],
        shard_sums[5],
        shard_sums[6],
        shard_sums[7],
        shard_sums[8].T,
    )


def local_grid(
    inputs,
    segments,
    attn_gain,
    w_query,
    key_projection,
    value_projection,
    w_output,
    query_gain,
    key_norm_gain,
    ffn_gain,
    w_gate,
    w_up,
    w_down,
    cotangent,
):
    batches = inputs.shape[0]
    tokens = inputs.shape[1]
    head_width = query_gain.shape[0]
    query_width = w_query.shape[1]
    kv_width = key_projection.shape[1]
    query_head_rows = query_width // head_width
    kv_heads = kv_width // head_width
    heads_per_group = query_head_rows // kv_heads
    scale = 1.0 / math.sqrt(head_width)
    query_gain_f = query_gain.astype(jnp.float32)
    key_gain_f = key_norm_gain.astype(jnp.float32)
    device_index = lax.axis_index("fsdp")
    places_row = jnp.arange(tokens, dtype=jnp.int32)
    causal = places_row[None, :] <= places_row[:, None]
    same_run = device_index * tokens // SEQ == (device_index - 1) * tokens // SEQ
    outputs_list = []
    grads_list = []
    shard_sums = None
    gain_sums = None
    gain_attn = lax.all_gather(attn_gain, "fsdp", axis=0, tiled=True)
    gain_ffn = lax.all_gather(ffn_gain, "fsdp", axis=0, tiled=True)
    full_query, full_key, full_value, full_output, full_gate, full_up, full_down = gather_grid(
        w_query, key_projection, value_projection, w_output, w_gate, w_up, w_down
    )
    for batch_index in range(batches):
        hidden = inputs[batch_index].astype(jnp.float32)
        segment = segments[batch_index]
        normed_f, norm_pull = jax.vjp(row_norm, hidden, gain_attn.astype(jnp.float32))
        normed = normed_f.astype(jnp.bfloat16)
        query_raw = plain_product(normed, full_query)
        key_projected = plain_product(normed, full_key)
        value_reduced = plain_product(normed, full_value).astype(jnp.bfloat16)
        lower_count = jnp.sum((segment[None, :] < segment[:, None]).astype(jnp.int32), axis=1)
        local_places = places_row - lower_count
        cos_local, sin_local = angles(local_places, head_width)
        key_sent = prepare_inputs(key_projected, key_gain_f, cos_local, sin_local, kv_heads).astype(
            jnp.bfloat16
        )
        remote_key, remote_value, remote_segment = from_behind(
            (key_sent, value_reduced, segment.astype(jnp.bfloat16)), "fsdp", 1
        )
        remote_match = (remote_segment.astype(jnp.int32)[None, :] == segment[:, None]) & same_run
        places_all = local_places + jnp.sum(remote_match.astype(jnp.int32), axis=1)
        cosine_table, sine_table_rows = angles(places_all, head_width)
        query_f, query_pull = jax.vjp(
            lambda raw_rows, gain_row: prepare_inputs(
                raw_rows, gain_row, cosine_table, sine_table_rows, query_head_rows
            ),
            query_raw,
            query_gain_f,
        )
        key_f, key_pull = jax.vjp(
            lambda raw_rows, gain_row: prepare_inputs(
                raw_rows, gain_row, cosine_table, sine_table_rows, kv_heads
            ),
            key_projected,
            key_gain_f,
        )
        query_low = query_f.astype(jnp.bfloat16)
        key_low = key_f.astype(jnp.bfloat16)
        allowed = jnp.concatenate(
            [remote_match, causal & (segment[None, :] == segment[:, None])], axis=1
        )
        query_split = query_low.reshape(tokens, kv_heads, heads_per_group, head_width).transpose(
            1, 0, 2, 3
        )
        key_split = (
            jnp.concatenate([remote_key, key_low], axis=0)
            .reshape(2 * tokens, kv_heads, head_width)
            .transpose(1, 0, 2)
        )
        value_split = (
            jnp.concatenate([remote_value, value_reduced], axis=0)
            .reshape(2 * tokens, kv_heads, head_width)
            .transpose(1, 0, 2)
        )

        def head_forward(blocks):
            query_part, key_part, value_part = blocks
            scores = (
                jnp.einsum("tgd,ld->gtl", query_part, key_part, preferred_element_type=jnp.float32)
                * scale
            )
            scores = jnp.where(allowed[None], scores, NEG)
            row_peak = jnp.max(scores, axis=-1, keepdims=True)
            raised = jnp.exp(scores - row_peak)
            row_total = jnp.sum(raised, axis=-1, keepdims=True)
            prob_rows = (raised / row_total).astype(jnp.bfloat16)
            mixed_part = jnp.einsum(
                "gtl,ld->tgd", prob_rows, value_part, preferred_element_type=jnp.float32
            )
            return (mixed_part.astype(jnp.bfloat16), (row_peak + jnp.log(row_total))[..., 0])

        mixed_split, log_totals = lax.map(head_forward, (query_split, key_split, value_split))
        attn_mix = mixed_split.transpose(1, 0, 2, 3).reshape(tokens, query_width)
        attended = hidden + plain_product(attn_mix, full_output)
        ffn_f, ffn_pull = jax.vjp(row_norm, attended, gain_ffn.astype(jnp.float32))
        ffn_in = ffn_f.astype(jnp.bfloat16)
        gate_raw = plain_product(ffn_in, full_gate)
        upward = plain_product(ffn_in, full_up)
        active_f, active_pull = jax.vjp(silu_product, gate_raw, upward)
        active = active_f.astype(jnp.bfloat16)
        result = attended + plain_product(active, full_down)
        outputs_list.append(result.astype(jnp.bfloat16))
        grad_result = cotangent[batch_index]
        grad_down_t = rows_product(grad_result, active)
        grad_active = cols_product(grad_result, full_down)
        grad_gate_f, grad_up_f = active_pull(grad_active)
        grad_gate_low = grad_gate_f.astype(jnp.bfloat16)
        grad_up_low = grad_up_f.astype(jnp.bfloat16)
        grad_gate_w = rows_product(ffn_in, grad_gate_low)
        grad_up_w = rows_product(ffn_in, grad_up_low)
        grad_ffn_in = cols_product(grad_gate_low, full_gate) + cols_product(grad_up_low, full_up)
        grad_attended_norm, grad_ffn_gain = ffn_pull(grad_ffn_in)
        grad_attended = grad_result.astype(jnp.float32) + grad_attended_norm
        grad_branch = grad_attended.astype(jnp.bfloat16)
        grad_output_t = rows_product(grad_branch, attn_mix)
        grad_mixed = cols_product(grad_branch, full_output).astype(jnp.bfloat16)
        grad_split = grad_mixed.reshape(tokens, kv_heads, heads_per_group, head_width).transpose(
            1, 0, 2, 3
        )

        def head_backward(blocks):
            query_part, key_part, value_part, grad_part, log_part = blocks
            scores = (
                jnp.einsum("tgd,ld->gtl", query_part, key_part, preferred_element_type=jnp.float32)
                * scale
            )
            scores = jnp.where(allowed[None], scores, NEG)
            prob_rows = jnp.exp(scores - log_part[..., None])
            grad_probs = jnp.einsum(
                "tgd,ld->gtl", grad_part, value_part, preferred_element_type=jnp.float32
            )
            center = jnp.sum(prob_rows * grad_probs, axis=-1, keepdims=True)
            grad_scores = (prob_rows * (grad_probs - center)).astype(jnp.bfloat16)
            grad_query_part = (
                jnp.einsum("gtl,ld->tgd", grad_scores, key_part, preferred_element_type=jnp.float32)
                * scale
            )
            grad_key_part = (
                jnp.einsum(
                    "gtl,tgd->ld", grad_scores, query_part, preferred_element_type=jnp.float32
                )
                * scale
            )
            grad_value_part = jnp.einsum(
                "gtl,tgd->ld",
                prob_rows.astype(jnp.bfloat16),
                grad_part,
                preferred_element_type=jnp.float32,
            )
            return (grad_query_part, grad_key_part, grad_value_part)

        grad_query_split, grad_key_split, grad_value_split = lax.map(
            head_backward, (query_split, key_split, value_split, grad_split, log_totals)
        )
        grad_query_rot = grad_query_split.transpose(1, 0, 2, 3).reshape(tokens, query_width)
        grad_key_all = grad_key_split.transpose(1, 0, 2).reshape(2 * tokens, kv_width)
        grad_value_all = grad_value_split.transpose(1, 0, 2).reshape(2 * tokens, kv_width)
        back_key_grad, back_value_grad = (
            from_behind(grad_key_all[:tokens].astype(jnp.bfloat16), "fsdp", -1).astype(jnp.float32),
            from_behind(grad_value_all[:tokens].astype(jnp.bfloat16), "fsdp", -1).astype(
                jnp.float32
            ),
        )
        grad_key_rot = grad_key_all[tokens:] + back_key_grad
        grad_value_low = (grad_value_all[tokens:] + back_value_grad).astype(jnp.bfloat16)
        grad_query_raw, grad_query_gain = query_pull(grad_query_rot)
        grad_key_raw, grad_key_gain = key_pull(grad_key_rot)
        grad_query_low = grad_query_raw.astype(jnp.bfloat16)
        grad_key_low = grad_key_raw.astype(jnp.bfloat16)
        grad_query_w = rows_product(normed, grad_query_low)
        grad_key_w = rows_product(normed, grad_key_low)
        grad_value_w = rows_product(normed, grad_value_low)
        grad_normed = (
            cols_product(grad_query_low, full_query)
            + cols_product(grad_key_low, full_key)
            + cols_product(grad_value_low, full_value)
        )
        grad_hidden_norm, grad_attn_gain = norm_pull(grad_normed)
        grads_list.append((grad_attended + grad_hidden_norm).astype(jnp.bfloat16))
        gain_sums = add_sets(gain_sums, (grad_query_gain, grad_key_gain))
        shard_terms = (
            grad_attn_gain,
            grad_query_w,
            grad_key_w,
            grad_value_w,
            grad_output_t,
            grad_ffn_gain,
            grad_gate_w,
            grad_up_w,
            grad_down_t,
        )
        shard_sums = add_sets(shard_sums, shard_terms)
    shard_sums = scatter_all(shard_sums)
    head_sums = lax.psum((gain_sums[0], gain_sums[1]), "fsdp")
    return (
        jnp.stack(outputs_list),
        jnp.stack(grads_list),
        shard_sums[0],
        shard_sums[1],
        shard_sums[2],
        shard_sums[3],
        shard_sums[4].T,
        head_sums[0],
        head_sums[1],
        shard_sums[5],
        shard_sums[6],
        shard_sums[7],
        shard_sums[8].T,
    )


def solution(mesh):
    return jax.shard_map(
        local_grid if mesh.shape["fsdp"] == 32 else local,
        mesh=mesh,
        in_specs=(
            P(None, "fsdp", None),
            P(None, "fsdp"),
            P("fsdp"),
            P("fsdp", None),
            P("fsdp", None),
            P("fsdp", None),
            P(None, "fsdp"),
            P(),
            P(),
            P("fsdp"),
            P("fsdp", None),
            P("fsdp", None),
            P(None, "fsdp"),
            P(None, "fsdp", None),
        ),
        out_specs=(
            P(None, "fsdp", None),
            P(None, "fsdp", None),
            P("fsdp"),
            P("fsdp", None),
            P("fsdp", None),
            P("fsdp", None),
            P(None, "fsdp"),
            P(),
            P(),
            P("fsdp"),
            P("fsdp", None),
            P("fsdp", None),
            P(None, "fsdp"),
        ),
        check_vma=False,
    )
```

```python
import functools
import math

import jax
import jax.numpy as jnp
from jax import lax
from jax.experimental import pallas as pl
from jax.experimental.pallas import tpu as pltpu
from jax.sharding import PartitionSpec as P

SEQ = 1024


EPS = 1e-05
THETA = 1000000.0
NEG = -1e30


CHUNKS = 11
WIDE = 768
MESH = pl.DeviceIdType.MESH
ALL = slice(None)
F32 = jnp.float32
BF16 = jnp.bfloat16
PARTS = (
    ("A", pl.ds(0, 48), pl.ds(0, 384)),
    ("B", pl.ds(0, 48), pl.ds(384, 384)),
    ("C", pl.ds(48, 16), pl.ds(0, 768)),
)
GAINS = len(PARTS)
OUTWARD = {
    "A": ("z0", "z1", "z2", "y", "x"),
    "B": ("z0", "z1", "z2", "x", "y"),
    "C": ("x", "y", "z0", "z1", "z2"),
}
INWARD = {
    "A": ("x", "y", "z0", "z1", "z2"),
    "B": ("y", "x", "z0", "z1", "z2"),
    "C": ("z0", "z1", "z2", "y", "x"),
}
SUM_SLOTS = 6
LAND_SLOTS = 3


def place():
    me = lax.axis_index("fsdp")
    return me, me // 8, (me // 4) % 2, (me // 2) % 2, me % 2


def guarded(condition, action):
    if condition is None:
        action()
    else:
        pl.when(condition)(action)


def greet(me, z, far=0):
    gate = pltpu.get_barrier_semaphore()
    for bit in (1, 2, 4):
        pl.semaphore_signal(gate, inc=1, device_id=(me ^ bit,), device_id_type=MESH)

    @pl.when(z > 0)
    def _():
        pl.semaphore_signal(gate, inc=1, device_id=(me - 8,), device_id_type=MESH)

    @pl.when(z < 3)
    def _():
        pl.semaphore_signal(gate, inc=1, device_id=(me + 8,), device_id_type=MESH)

    if far:
        pl.semaphore_signal(gate, inc=1, device_id=(me ^ far,), device_id_type=MESH)
    pl.semaphore_wait(gate, (4 if far else 3) + (z > 0).astype(jnp.int32) + (z < 3).astype(jnp.int32))


class Gather:
    def __init__(self, full, tiles, sent, landed):
        self.full, self.tiles, self.sent, self.landed = full, tiles, sent, landed
        self.me, self.z, self.y, self.x, self.core = place()

    def moves(self, part, step, chunk):
        kind, rows, columns = PARTS[0] if part == GAINS else PARTS[part]
        z, y, x, me = self.z, self.y, self.x, self.me

        def view(zz, yy, xx):
            if part == GAINS:
                return self.tiles.at[zz, yy, xx]
            return self.full.at[chunk, zz, yy, xx, rows, columns]

        axis = OUTWARD[kind][step]
        if axis[0] == "z":
            far = int(axis[1])
            yy, xx = (ALL, ALL) if kind == "C" else (y, x)
            return (
                ((z >= far) & (z < 3), z - far, me + 8, z >= far + 1, z - 1 - far),
                ((z <= 3 - far) & (z > 0), z + far, me - 8, z <= 2 - far, z + 1 + far),
            ), lambda zz: view(zz, yy, xx)
        zz = z if kind == "C" else ALL
        if axis == "y":
            xx = x if kind == "A" else ALL
            return ((None, y, me ^ 4, None, 1 - y),), lambda yy: view(zz, yy, xx)
        yy = ALL if kind == "A" else y
        return ((None, x, me ^ 2, None, 1 - x),), lambda xx: view(zz, yy, xx)

    def copy(self, ref, device, part, step, chunk, way):
        return pltpu.make_async_remote_copy(
            src_ref=ref,
            dst_ref=ref,
            send_sem=self.sent.at[chunk, part, step, way],
            recv_sem=self.landed.at[chunk, part, step, way],
            device_id=(device,),
            device_id_type=MESH,
        )

    def send(self, part, step, chunk):
        moves, view = self.moves(part, step, chunk)
        for way, (sends, mine, device, _, _) in enumerate(moves):
            guarded(
                sends,
                lambda: self.copy(view(mine), device, part, step, chunk, way).start(),
            )

    def receive(self, part, step, chunk):
        moves, view = self.moves(part, step, chunk)
        for way, (_, _, _, receives, other) in enumerate(moves):
            guarded(
                receives,
                lambda: self.copy(view(other), self.me ^ 2, part, step, chunk, way).wait_recv(),
            )

    def finish(self, part, step, chunk):
        moves, view = self.moves(part, step, chunk)
        for way, (sends, mine, device, _, _) in enumerate(moves):
            guarded(
                sends,
                lambda: self.copy(view(mine), device, part, step, chunk, way).wait_send(),
            )

    def tick(self, time):
        for step in range(6):
            chunk = time - step

            @pl.when((chunk >= 0) & (chunk < CHUNKS))
            def _():
                for part in range(len(PARTS)):
                    if step > 0:
                        self.receive(part, step - 1, chunk)
                    if step < 5:
                        self.send(part, step, chunk)

    def tick_gains(self, step):
        if step > 0:
            self.receive(GAINS, step - 1, 0)
        if step < 5:
            self.send(GAINS, step, 0)

    def drain(self):
        def body(chunk, carry):
            for part in range(len(PARTS)):
                for step in range(5):
                    self.finish(part, step, chunk)
            return carry

        lax.fori_loop(0, CHUNKS, body, 0)
        for step in range(5):
            self.finish(GAINS, step, 0)


class Scatter:
    def __init__(self, sums, lands, totals, sent, landed):
        self.sums, self.lands, self.totals = sums, lands, totals
        self.sent, self.landed = sent, landed
        self.me, self.z, self.y, self.x, self.core = place()

    def moves(self, part, step, chunk):
        kind, rows, columns = PARTS[part]
        z, y, x, me = self.z, self.y, self.x, self.me
        slot, land = lax.rem(chunk, SUM_SLOTS), lax.rem(chunk, LAND_SLOTS)
        first, second, up, down = self.lands[part]
        axis = INWARD[kind][step]

        def view(zz, yy, xx):
            return self.sums.at[slot, zz, yy, xx, rows, columns]

        if axis[0] == "z":
            far = int(axis[1])
            count = 3 - far
            yy, xx = (ALL, ALL) if kind == "C" else (y, x)
            above, below = pl.ds(far + 1, count), pl.ds(0, count)
            up_land, down_land = up.at[land, pl.ds(far, count)], down.at[land, pl.ds(0, count)]
            return (
                (z == far, view(above, yy, xx), up_land, me + 8, z == far + 1, view(above, yy, xx)),
                (z == 3 - far, view(below, yy, xx), down_land, me - 8, z == 2 - far, view(below, yy, xx)),
            )
        zz = z if kind == "C" else ALL
        ref = (first if step == 0 or (kind == "C" and step == 3) else second).at[land]
        if axis == "x":
            yy = ALL if kind == "A" else y
            return ((None, view(zz, yy, 1 - x), ref, me ^ 2, None, view(zz, yy, x)),)
        xx = x if kind == "A" else ALL
        return ((None, view(zz, 1 - y, xx), ref, me ^ 4, None, view(zz, y, xx)),)

    def copy(self, source, target, device, part, step, chunk, way):
        return pltpu.make_async_remote_copy(
            src_ref=source,
            dst_ref=target,
            send_sem=self.sent.at[chunk, part, step, way],
            recv_sem=self.landed.at[chunk, part, step, way],
            device_id=(device,),
            device_id_type=MESH,
        )

    def step(self, part, step, chunk):
        if step > 0:
            for way, move in enumerate(self.moves(part, step - 1, chunk)):
                sends, source, land, device, receives, target = move

                def add():
                    self.copy(land, land, self.me ^ 2, part, step - 1, chunk, way).wait_recv()
                    target[...] = (target[...].astype(F32) + land[...].astype(F32)).astype(BF16)

                guarded(receives, add)
                guarded(
                    sends,
                    lambda: self.copy(source, land, device, part, step - 1, chunk, way).wait_send(),
                )
        if step < 5:
            for way, move in enumerate(self.moves(part, step, chunk)):
                sends, source, land, device, _, _ = move
                guarded(
                    sends,
                    lambda: self.copy(source, land, device, part, step, chunk, way).start(),
                )
        else:
            _, rows, columns = PARTS[part]
            slot = lax.rem(chunk, SUM_SLOTS)
            self.totals[chunk, rows, columns] = self.sums[
                slot, self.z, self.y, self.x, rows, columns
            ].astype(F32)

    def tick(self, time):
        for step in range(5, -1, -1):
            chunk = time - step

            @pl.when((chunk >= 0) & (chunk < CHUNKS))
            def _():
                for part in range(len(PARTS)):
                    self.step(part, step, chunk)


def pair_rows(core):
    mine = pl.ds(pl.multiple_of(core * 32, 32), 32)
    other = pl.ds(pl.multiple_of((1 - core) * 32, 32), 32)
    return mine, other


def semaphores():
    return [pltpu.SemaphoreType.DMA((CHUNKS, len(PARTS) + 1, 5, 2))] * 2


def land_shapes():
    slots = LAND_SLOTS
    plain = [(slots, 4, 2, 48, 384), (slots, 4, 48, 384), (slots, 3, 48, 384), (slots, 3, 48, 384)]
    late = [(slots, 2, 16, 768), (slots, 16, 768), (slots, 3, 2, 2, 16, 768), (slots, 3, 2, 2, 16, 768)]
    return [pltpu.VMEM(shape, BF16) for shape in plain + plain + late]


def params(number):
    return pltpu.CompilerParams(
        collective_id=number, has_side_effects=True, vmem_limit_bytes=62 * 2**20
    )


EAGER = 7
SPREAD = 4


def contract(left, right, left_dim, right_dim):
    return lax.dot_general(
        left, right, (((left_dim,), (right_dim,)), ((), ())), preferred_element_type=F32
    )


def lane_index(shape):
    return lax.broadcasted_iota(jnp.int32, shape, 1)


def half_turn(rows):
    width = rows.shape[1]
    first = lane_index(rows.shape) % 64 < 32
    return jnp.where(first, pltpu.roll(rows, width - 32, 1), pltpu.roll(rows, 32, 1))


def head_means(rows, ones):
    parts = [
        contract(rows[:, k : k + 256].astype(BF16), ones, 1, 0)
        for k in range(0, rows.shape[1], 256)
    ]
    return jnp.concatenate(parts, axis=1)


def head_ones():
    row = lax.broadcasted_iota(jnp.int32, (256, 256), 0) // 64
    column = lax.broadcasted_iota(jnp.int32, (256, 256), 1) // 64
    return jnp.where(row == column, 1.0 / 64.0, 0.0).astype(BF16)


def tiled(table, copies):
    return jnp.concatenate([table] * copies, axis=1)


def split_pair(rows, group):
    pair = rows[:, 128 * (group // 2) : 128 * (group // 2) + 128]
    low = lane_index(pair.shape) < 64
    if group % 2 == 0:
        kept = jnp.where(low, pair, 0.0)
        return kept, pltpu.roll(kept, 64, 1)
    kept = jnp.where(low, 0.0, pair)
    return pltpu.roll(kept, 64, 1), kept


def lanes_at(block, width):
    return pl.ds(pl.multiple_of(block * width, width), width)


def forward_kernel(*refs):
    packed, tile_in, x_in, cot_in, seg_in, gains, inverse = refs[:7]
    (
        w_out, normed_out, raw_out, qkv_out, table_out, mask_out, total_out, mix_out,
        ffn_out, cot_out, saved_out, result_out, branch_out, kept_out, gain_out,
    ) = refs[7:22]
    (
        full, tiles, gain_rows, rows_all, cots, seg_rows, mixed, mixed_pair, wo_pair, attended,
        lent, local, pair_sent, pair_landed, sent, landed,
    ) = refs[22:]
    me, z, y, x, core = place()
    pair = (me ^ 1,)
    greet(me, z)
    mine, other = pair_rows(core)

    def to_pair(number, source, target):
        return pltpu.make_async_remote_copy(
            src_ref=source,
            dst_ref=target,
            send_sem=pair_sent.at[number],
            recv_sem=pair_landed.at[number],
            device_id=pair,
            device_id_type=MESH,
        )

    def keep(number, source, target):
        return pltpu.make_async_copy(source, target, local.at[number])

    own_w = keep(0, packed.at[core], full.at[:, z, y, x, mine, :])
    own_x = keep(1, x_in, rows_all.at[:, core])
    own_cot = keep(2, cot_in, cots.at[:, core])
    own_seg = keep(3, seg_in, seg_rows.at[core])
    give_w = to_pair(0, packed.at[1 - core], full.at[:, z, y, x, mine, :])
    take_w = to_pair(0, packed.at[1 - core], full.at[:, z, y, x, other, :])
    give_x = to_pair(1, x_in, rows_all.at[:, core])
    take_x = to_pair(1, x_in, rows_all.at[:, 1 - core])
    give_cot = to_pair(2, cot_in, cots.at[:, core])
    take_cot = to_pair(2, cot_in, cots.at[:, 1 - core])
    give_seg = to_pair(3, seg_in, seg_rows.at[core])
    take_seg = to_pair(3, seg_in, seg_rows.at[1 - core])
    own_tile = keep(4, tile_in, tiles.at[z, y, x, core])
    give_tile = to_pair(9, tile_in, tiles.at[z, y, x, core])
    own_tile.start()
    give_tile.start()
    own_w.start()
    give_w.start()
    own_seg.start()
    give_seg.start()
    own_x.start()
    give_x.start()
    own_cot.start()
    give_cot.start()
    own_w.wait()
    take_w.wait_recv()
    own_tile.wait()
    to_pair(9, tile_in, tiles.at[z, y, x, 1 - core]).wait_recv()
    gather = Gather(full, tiles, sent, landed)

    def early(time, carry):
        for step in range(6):

            @pl.when(time == step)
            def _():
                gather.tick_gains(step)

        gather.tick(time)
        return carry

    lax.fori_loop(0, EAGER, early, 0)
    for block in range(8):
        quad = tiles[block // 2, block % 2]
        quad = quad[0, 0] + quad[0, 1] + quad[1, 0] + quad[1, 1]
        gain_rows[:, 128 * block : 128 * block + 128] = quad
    keep_gain = keep(11, gain_rows, gain_out)
    keep_gain.start()
    give_wo = to_pair(4, full.at[1, :, :, :, :, pl.ds(256, 512)], wo_pair)
    give_wo.start()
    keep_w = keep(0, full.at[pl.ds(0, 2)], w_out)
    keep_w.start()
    own_x.wait()
    own_seg.wait()
    own_cot.wait()
    take_x.wait_recv()
    take_seg.wait_recv()
    take_cot.wait_recv()
    keep_cot = keep(2, cots, cot_out)
    keep_cot.start()

    def attention(normed, raw, qkv, table, mask, total, keys, values):
        def copies(batch):
            return (
                keep(4, normed, normed_out.at[batch]),
                keep(5, raw, raw_out.at[batch]),
                keep(6, qkv, qkv_out.at[batch]),
                keep(7, table, table_out.at[batch]),
                keep(8, mask, mask_out.at[batch]),
                keep(9, total, total_out.at[batch]),
                keep(10, mixed.at[batch], mix_out.at[batch]),
            )

        def project(batch):
            segment = jnp.concatenate([seg_rows[0, batch], seg_rows[1, batch]], axis=1)
            column = jnp.broadcast_to(segment, (128, SEQ)).T
            below = jnp.zeros((SEQ, 128), F32)
            for k in range(0, SEQ, 128):
                below += (segment[:, k : k + 128] < column).astype(F32)
            before = jnp.sum(below, axis=1, keepdims=True)
            spot = lax.broadcasted_iota(jnp.int32, (SEQ, 128), 0).astype(F32) - before
            angle = spot * inverse[...]
            sine = jnp.sin(angle)
            first = lane_index((SEQ, 128)) % 64 < 32
            table[:, 0:128] = jnp.cos(angle)
            table[:, 128:256] = jnp.where(first, -sine, sine)
            for quarter in range(4):
                span = pl.ds(quarter * 256, 256)
                width = (quarter + 1) * 256
                same = segment[:, :width] == column[quarter * 256 : quarter * 256 + 256, 0:1]
                spots = lax.broadcasted_iota(jnp.int32, (256, width), 0) + quarter * 256
                behind = lane_index((256, width)) <= spots
                mask[span, 0:width] = jnp.where(same & behind, 1.0, 0.0).astype(BF16)
            total[...] = jnp.zeros_like(total)
            ones = head_ones()

            def block(half, carry):
                span = pl.ds(pl.multiple_of(half * 512, 512), 512)
                rows = rows_all[batch, half].astype(F32)
                scale = lax.rsqrt(jnp.mean(rows * rows, axis=1, keepdims=True) + EPS)
                unit = (rows * scale * gain_rows[0:1]).astype(BF16)
                normed[span, :] = unit
                weights = full[0].reshape(1024, WIDE)
                product = contract(unit, weights, 1, 0)
                raw[span, :] = product.astype(BF16)
                level = lax.rsqrt(head_means(product * product, ones) + EPS)
                turned = product * level * gains[...]
                cosine = tiled(table[span, 0:128], 6)
                sine_signed = tiled(table[span, 128:256], 6)
                turned = turned * cosine + half_turn(turned) * sine_signed
                query = turned[:, 0:512] * 0.125
                key = turned[:, 512:768].astype(BF16).astype(F32)
                value_weights = full[1, :, :, :, :, 0:256].reshape(1024, 256)
                value = contract(unit, value_weights, 1, 0).astype(BF16).astype(F32)
                qkv[span, 0:512] = query.astype(BF16)
                qkv[span, 512:768] = key.astype(BF16)
                qkv[span, 768:1024] = value.astype(BF16)
                for group in range(4):
                    low, high = split_pair(key, group)
                    keys[group, 0, span, :] = low.astype(BF16)
                    keys[group, 1, span, :] = high.astype(BF16)
                    low, high = split_pair(value, group)
                    values[group, 0, span, :] = low.astype(BF16)
                    values[group, 1, span, :] = high.astype(BF16)
                return carry

            lax.fori_loop(0, 2, block, 0)

        def attend(batch, quarter):
            span = pl.ds(quarter * 256, 256)
            width = (quarter + 1) * 256
            allowed = mask[span, 0:width].astype(F32)
            lane = lane_index((256, 128))

            def group_step(group, carry):
                queries = qkv[span, lanes_at(group, 128)]
                parts, sums = [], []
                for side in range(2):
                    scores = contract(queries, keys[group, side, 0:width, :], 1, 1)
                    raised = jnp.exp(scores) * allowed
                    sums.append(1.0 / jnp.sum(raised, axis=1, keepdims=True))
                    parts.append(
                        contract(raised.astype(BF16), values[group, side, 0:width, :], 1, 0)
                    )
                result = (parts[0] + parts[1]) * jnp.where(lane < 64, sums[0], sums[1])
                mixed[batch, span, lanes_at(group, 128)] = result.astype(BF16)
                old = total[span, :]
                old = jnp.where(lane == 2 * group, sums[0], old)
                total[span, :] = jnp.where(lane == 2 * group + 1, sums[1], old)
                return carry

            lax.fori_loop(0, 4, group_step, 0)

        def piece(number, carry):
            batch, part = number // 4, number % 4

            @pl.when(part == 0)
            def _():
                @pl.when(batch > 0)
                def _():
                    for copy in copies(0):
                        copy.wait()

                project(batch)

            @pl.when(number % 2 == 0)
            def _():
                gather.tick(EAGER + number // 2)

            for quarter in range(4):

                @pl.when(part == quarter)
                def _():
                    attend(batch, quarter)

            @pl.when(part == 3)
            def _():
                for copy in copies(batch):
                    copy.start()
                to_pair(5 + batch, mixed.at[batch, lanes_at(1 - core, 512), :], mixed_pair.at[batch]).start()

            return carry

        lax.fori_loop(0, 8, piece, 0)
        for copy in copies(1):
            copy.wait()

    pl.run_scoped(
        attention,
        pltpu.VMEM((SEQ, 1024), BF16),
        pltpu.VMEM((SEQ, WIDE), BF16),
        pltpu.VMEM((SEQ, 1024), BF16),
        pltpu.VMEM((SEQ, 256), F32),
        pltpu.VMEM((SEQ, SEQ), BF16),
        pltpu.VMEM((SEQ, 128), F32),
        pltpu.VMEM((4, 2, SEQ, 128), BF16),
        pltpu.VMEM((4, 2, SEQ, 128), BF16),
    )
    give_wo.wait_send()
    give_wo.wait_recv()
    give_x.wait_send()

    def swap_mixed(batch):
        return to_pair(5 + batch, mixed.at[batch, lanes_at(1 - core, 512), :], mixed_pair.at[batch])

    def join(batch, carry):
        swap_mixed(batch).wait_recv()
        span = lanes_at(core, 512)
        own_wo = full[1, :, :, :, :, 256:768].reshape(1024, 512)
        result = rows_all[batch, core].astype(F32)
        result += contract(mixed[batch, span, :], own_wo, 1, 1)
        result += contract(mixed_pair[batch], wo_pair[...].reshape(1024, 512), 1, 1)
        attended[batch] = result
        scale = lax.rsqrt(jnp.mean(result * result, axis=1, keepdims=True) + EPS)
        rows_all[batch, core] = (result * scale * gain_rows[1:2]).astype(BF16)
        to_pair(7 + batch, rows_all.at[batch, core], rows_all.at[batch, core]).start()
        return carry

    lax.fori_loop(0, 2, join, 0)
    for batch in range(2):
        to_pair(7 + batch, rows_all.at[batch, core], rows_all.at[batch, 1 - core]).wait_recv()
    keep_ffn = keep(3, rows_all, ffn_out)
    keep_ffn.start()

    def feed_forward(result, back, saved):
        def save(chunk, part):
            slot = part % 2
            return keep(4 + slot, saved.at[slot], saved_out.at[chunk, part // 2, part % 2])

        def chunk_step(chunk, carry):
            @pl.when(chunk < CHUNKS + 5 - EAGER - SPREAD)
            def _():
                gather.tick(EAGER + SPREAD + chunk)

            def block(part, inner):
                batch, half = part // 2, part % 2
                slot = part % 2

                @pl.when((chunk > 0) | (part > 1))
                def _():
                    save(chunk, part).wait()

                up_weights = full[chunk + 2, :, :, :, :, 0:512].reshape(1024, 512)
                down_weights = full[chunk + 2, :, :, :, :, 512:768].reshape(1024, 256)
                both = contract(rows_all[batch, half], up_weights, 1, 0)
                grad = contract(cots[batch, half], down_weights, 1, 0)
                gate, up = both[:, 0:256], both[:, 256:512]
                bend = 1.0 / (1.0 + jnp.exp(-gate))
                silu = gate * bend
                active = (silu * up).astype(BF16)
                grad_up = (grad * silu).astype(BF16)
                grad_gate = (grad * up * bend * (1.0 + gate * (1.0 - bend))).astype(BF16)
                saved[slot, :, 0:256] = grad_gate
                saved[slot, :, 256:512] = grad_up
                saved[slot, :, 512:768] = active
                save(chunk, part).start()
                forward = contract(active, down_weights, 1, 1)
                backward = contract(saved[slot, :, 0:512], up_weights, 1, 1)

                @pl.when(chunk == 0)
                def _():
                    result[batch, half] = forward
                    back[batch, half] = backward

                @pl.when(chunk > 0)
                def _():
                    result[batch, half] += forward
                    back[batch, half] += backward

                return inner

            lax.fori_loop(0, 4, block, 0)
            return carry

        lax.fori_loop(0, CHUNKS - 2, chunk_step, 0)
        for part in range(2, 4):
            save(CHUNKS - 3, part).wait()
        keep_ffn.wait()
        keep_cot.wait()
        for batch in range(2):
            to_pair(7 + batch, rows_all.at[batch, core], rows_all.at[batch, core]).wait_send()

        def lend(batch, carry):
            rows_all[0, batch] = result[batch, 1 - core].astype(BF16)
            rows_all[1, batch] = back[batch, 1 - core].astype(BF16)
            return carry

        lax.fori_loop(0, 2, lend, 0)
        give_lent = to_pair(10, rows_all, lent)
        give_lent.start()
        give_lent.wait()

        def close(batch, carry):
            joined = attended[batch]
            outputs = joined + result[batch, core] + lent[0, batch].astype(F32)
            lent[0, batch] = outputs.astype(BF16)
            scale = lax.rsqrt(jnp.mean(joined * joined, axis=1, keepdims=True) + EPS)
            unit = joined * scale
            pulled = (back[batch, core] + lent[1, batch].astype(F32)) * gain_rows[1:2]
            shared = jnp.mean(pulled * unit, axis=1, keepdims=True)
            total = cots[batch, core].astype(F32) + scale * (pulled - unit * shared)
            attended[batch] = total
            cots[batch, core] = total.astype(BF16)
            to_pair(7 + batch, cots.at[batch, core], cots.at[batch, core]).start()
            return carry

        lax.fori_loop(0, 2, close, 0)
        ends = [
            keep(4, lent.at[0], result_out),
            keep(5, attended, kept_out),
        ]
        for copy in ends:
            copy.start()
        for batch in range(2):
            to_pair(7 + batch, cots.at[batch, core], cots.at[batch, 1 - core]).wait_recv()
        ends.append(keep(6, cots, branch_out))
        ends[-1].start()
        for copy in ends:
            copy.wait()

    pl.run_scoped(
        feed_forward,
        pltpu.VMEM((2, 2, 512, 1024), F32),
        pltpu.VMEM((2, 2, 512, 1024), F32),
        pltpu.VMEM((2, 512, WIDE), BF16),
    )
    give_w.wait_send()
    give_seg.wait_send()
    for batch in range(2):
        swap_mixed(batch).wait_send()
        to_pair(7 + batch, cots.at[batch, core], cots.at[batch, core]).wait_send()
    give_tile.wait_send()
    give_cot.wait_send()
    keep_w.wait()
    keep_gain.wait()
    gather.drain()


def forward_call(packed, tile, inputs, cotangent, segments, query_gain, key_gain):
    rows = inputs.shape[1]
    head = query_gain.shape[0]
    gains = jnp.concatenate([jnp.tile(query_gain, 8), jnp.tile(key_gain, 4)]).astype(F32)[None]
    counter = (jnp.arange(128) % (head // 2)).astype(F32)
    inverse = jnp.power(jnp.float32(THETA), -2.0 * counter / head)[None]
    shapes = [
        ((2, 4, 2, 2, 64, WIDE), BF16),
        ((2, SEQ, 1024), BF16),
        ((2, SEQ, WIDE), BF16),
        ((2, SEQ, 1024), BF16),
        ((2, SEQ, 256), F32),
        ((2, SEQ, SEQ), BF16),
        ((2, SEQ, 128), F32),
        ((2, SEQ, 512), BF16),
        ((2, 2, rows, 1024), BF16),
        ((2, 2, rows, 1024), BF16),
        ((CHUNKS - 2, 2, 2, rows, WIDE), BF16),
        ((2, rows, 1024), BF16),
        ((2, 2, rows, 1024), BF16),
        ((2, rows, 1024), F32),
        ((8, 1024), F32),
    ]
    anywhere = pl.BlockSpec(memory_space=pl.ANY)
    inside = pl.BlockSpec(memory_space=pltpu.VMEM)
    return pl.pallas_call(
        forward_kernel,
        out_shape=[jax.ShapeDtypeStruct(*shape) for shape in shapes],
        in_specs=[anywhere] * 5 + [inside] * 2,
        out_specs=[anywhere] * len(shapes),
        scratch_shapes=[
            pltpu.VMEM((CHUNKS, 4, 2, 2, 64, WIDE), BF16),
            pltpu.VMEM((4, 2, 2, 2, 8, 128), F32),
            pltpu.VMEM((8, 1024), F32),
            pltpu.VMEM((2, 2, rows, 1024), BF16),
            pltpu.VMEM((2, 2, rows, 1024), BF16),
            pltpu.VMEM((2, 2, 1, rows), F32),
            pltpu.VMEM((2, SEQ, 512), BF16),
            pltpu.VMEM((2, rows, 512), BF16),
            pltpu.VMEM((4, 2, 2, 64, 512), BF16),
            pltpu.VMEM((2, rows, 1024), F32),
            pltpu.VMEM((2, 2, rows, 1024), BF16),
            pltpu.SemaphoreType.DMA((12,)),
            pltpu.SemaphoreType.DMA((11,)),
            pltpu.SemaphoreType.DMA((11,)),
        ]
        + semaphores(),
        compiler_params=params(0),
        name="forward",
    )(packed, tile, inputs, cotangent, segments.astype(F32)[:, None, :], gains, inverse)


def pack_halves(w_query, w_key, w_value, output_t, w_gate, w_up, down_t):
    rows = w_query.shape[0]
    halves = [jnp.stack(jnp.split(w, 2, axis=1)) for w in (w_query, w_key, w_value, output_t)]
    first = jnp.concatenate(halves[:2], axis=2)[:, None]
    second = jnp.concatenate(halves[2:], axis=2)[:, None]
    wide = jnp.concatenate(
        [w.reshape(rows, 2, CHUNKS - 2, 256).transpose(1, 2, 0, 3) for w in (w_gate, w_up, down_t)],
        axis=3,
    )
    return jnp.concatenate([first, second, wide], axis=1)


def pack_gains(attn_gain, ffn_gain):
    count = attn_gain.shape[0]
    slot = lax.axis_index("fsdp") % (128 // count)
    pair = jnp.stack([attn_gain, ffn_gain]).astype(F32)
    place_of = (jnp.arange(128 // count) == slot).astype(F32)
    spread = (place_of[None, :, None] * pair[:, None, :]).reshape(2, 128)
    return jnp.concatenate([spread, jnp.zeros((6, 128), F32)])


def backward_kernel(*refs):
    (
        w_in, normed_in, raw_in, qkv_in, table_in, mask_in, total_in, mix_in, ffn_in, cot_in,
        saved_in, branch_in, kept_in, x_in, gain_rows, head_gains,
    ) = refs[:16]
    grad_out, sums_out, head_out = refs[16:19]
    sums = refs[19]
    lands = (refs[20:24], refs[24:28], refs[28:32])
    (
        totals, pair_land, rows_all, cots, saved, branch, grads, qkv, raw, table, total, mask, mixed,
        grad_mixed, wo, keys, values, key_sum, value_sum, head_sum, head_land, kept,
        local, pair_sent, pair_landed, head_sent, head_landed, sent, landed,
    ) = refs[32:]
    me, z, y, x, core = place()
    greet(me, z, 16)
    mine, other = pair_rows(core)
    scatter = Scatter(sums, lands, totals, sent, landed)

    def to_pair(number, source, target):
        return pltpu.make_async_remote_copy(
            src_ref=source,
            dst_ref=target,
            send_sem=pair_sent.at[number],
            recv_sem=pair_landed.at[number],
            device_id=(me ^ 1,),
            device_id_type=MESH,
        )

    def load(number, source, target):
        return pltpu.make_async_copy(source, target, local.at[number])

    loads = [
        load(0, ffn_in, rows_all),
        load(1, cot_in, cots),
        load(2, saved_in.at[0], saved),
        load(3, branch_in, branch),
        load(4, w_in.at[1, :, :, pl.ds(256, 512)], wo),
        load(5, mix_in, mixed),
    ]
    for copy in loads:
        copy.start()
    head_sum[...] = jnp.zeros_like(head_sum)
    for copy in loads[:3]:
        copy.wait()

    def put(slot, columns, left, right):
        product = contract(left, right, 0, 0).astype(BF16)
        sums[slot, :, :, :, :, columns] = product.reshape(4, 2, 2, 64, columns.size)

    def wide_terms(chunk):
        slot = lax.rem(chunk, SUM_SLOTS)
        flat = saved[...].reshape(2048, WIDE)
        put(slot, pl.ds(0, 512), rows_all[...].reshape(2048, 1024), flat[:, 0:512])
        put(slot, pl.ds(512, 256), cots[...].reshape(2048, 1024), flat[:, 512:768])

    wide_terms(0)
    load(2, saved_in.at[1], saved).start()
    for copy in loads[3:]:
        copy.wait()

    def mixed_back(half, carry):
        product = contract(branch[half].reshape(1024, 1024), wo[...].reshape(1024, 512), 1, 0)
        grad_mixed[half] = product.astype(BF16)
        return carry

    def batch_loads(batch):
        return (
            load(6, qkv_in.at[batch], qkv),
            load(7, raw_in.at[batch], raw),
            load(8, table_in.at[batch], table),
            load(9, total_in.at[batch], total),
            load(10, mask_in.at[batch], mask),
        )

    def pull_back(grad, span, columns, gain, number):
        plain = raw[span, columns].astype(F32)
        width = plain.shape[1]
        row = lax.broadcasted_iota(jnp.int32, (width, width), 0) // 64
        column = lax.broadcasted_iota(jnp.int32, (width, width), 1) // 64
        ones = jnp.where(row == column, 1.0 / 64.0, 0.0).astype(BF16)
        level = lax.rsqrt(contract((plain * plain).astype(BF16), ones, 1, 0) + EPS)
        unit = plain * level
        turned = grad * table[span, 0:128] - half_turn(grad) * table[span, 128:256]
        terms = turned * unit
        head_sum[number] += jnp.sum(terms.reshape(-1, 8, width), axis=0)
        scaled = terms * gain
        shared = contract(scaled.astype(BF16), ones, 1, 0)
        return level * (turned * gain - unit * shared)

    def sides(pair, parity):
        low = lane_index(pair.shape) < 64
        rows = pair.astype(F32)
        first, second = jnp.where(low, rows, 0.0), jnp.where(low, 0.0, rows)
        if parity == 0:
            second = pltpu.roll(second, 64, 1)
        else:
            first = pltpu.roll(first, 64, 1)
        return first.astype(BF16), second.astype(BF16)

    def attend_back(batch, couple, parity):
        key_pair = qkv[:, pl.ds(pl.multiple_of(512 + couple * 128, 128), 128)].astype(F32)
        value_pair = qkv[:, pl.ds(pl.multiple_of(768 + couple * 128, 128), 128)].astype(F32)
        for target, pair in ((keys, key_pair), (values, value_pair)):
            low, high = split_pair(pair, parity)
            target[0] = low.astype(BF16)
            target[1] = high.astype(BF16)
        if parity == 0:
            key_sum[...] = jnp.zeros_like(key_sum)
            value_sum[...] = jnp.zeros_like(value_sum)
        group = couple * 2 + parity
        lane = lane_index((256, 128))
        for quarter in range(4):
            span = pl.ds(quarter * 256, 256)
            width = (quarter + 1) * 256
            allowed = mask[span, 0:width].astype(F32)
            queries = qkv[span, lanes_at(group, 128)]
            pulled = grad_mixed[batch, span, lanes_at(group, 128)]
            product = pulled.astype(F32) * mixed[batch, span, lanes_at(group, 128)].astype(F32)
            inverse = total[span, :]
            query_sides, pulled_sides = sides(queries, parity), sides(pulled, parity)
            grad_query = jnp.zeros((256, 128), F32)
            grad_key = jnp.zeros((width, 128), F32)
            grad_value = jnp.zeros((width, 128), F32)
            for side in range(2):
                inside = lane < 64 if side == 0 else lane >= 64
                center = jnp.sum(jnp.where(inside, product, 0.0), axis=1, keepdims=True)
                level = jnp.sum(jnp.where(lane == 2 * group + side, inverse, 0.0), axis=1, keepdims=True)
                near_keys, near_values = keys[side, 0:width, :], values[side, 0:width, :]
                scores = contract(queries, near_keys, 1, 1)
                probs = jnp.exp(scores) * (allowed * level)
                grad_probs = contract(pulled, near_values, 1, 1)
                grad_scores = (probs * (grad_probs - center)).astype(BF16)
                grad_query += contract(grad_scores, near_keys, 1, 0)
                grad_key += contract(grad_scores, query_sides[side], 0, 0)
                grad_value += contract(probs.astype(BF16), pulled_sides[side], 0, 0)
            key_sum[0:width, :] += grad_key
            value_sum[0:width, :] += grad_value
            grad_raw = pull_back(
                grad_query * 0.125, span, lanes_at(group, 128), head_gains[:, 0:128], 0
            )
            grads[batch, span, lanes_at(group, 128)] = grad_raw.astype(BF16)
        if parity == 1:
            whole = pl.ds(0, SEQ)
            columns = pl.ds(pl.multiple_of(512 + couple * 128, 128), 128)
            grad_raw = pull_back(key_sum[...], whole, columns, head_gains[:, 512:640], 1)
            grads[batch, :, columns] = grad_raw.astype(BF16)
            columns = pl.ds(pl.multiple_of(768 + couple * 128, 128), 128)
            grads[batch, :, columns] = value_sum[...].astype(BF16)

    def head_copy(step):
        bit = (1, 2, 4, 8, 16)[step]
        return pltpu.make_async_remote_copy(
            src_ref=head_sum,
            dst_ref=head_land.at[step],
            send_sem=head_sent.at[step],
            recv_sem=head_landed.at[step],
            device_id=(me ^ bit,),
            device_id_type=MESH,
        )

    def send_heads(step):
        if step > 0:
            head_copy(step - 1).wait()
            head_sum[...] += head_land[step - 1]
        if step < 5:
            head_copy(step).start()

    def near_normed(batch, half):
        part = grads[batch, pl.ds(pl.multiple_of(half * 512, 512), 512), :]
        first = contract(part[:, 0:768], saved[0].reshape(1024, WIDE), 1, 1)
        value_weights = saved[1].reshape(1024, WIDE)[:, 0:256]
        return first + contract(part[:, 768:1024], value_weights, 1, 1)

    def work(time):
        @pl.when(time == 0)
        def _():
            lax.fori_loop(0, 2, mixed_back, 0)

        @pl.when((time >= 1) & (time <= 8))
        def _():
            unit = time - 1
            batch, couple, parity = unit // 4, (unit // 2) % 2, unit % 2

            @pl.when(unit % 4 == 0)
            def _():
                for copy in batch_loads(batch):
                    copy.start()
                for copy in batch_loads(batch):
                    copy.wait()

            for each in range(2):

                @pl.when(parity == each)
                def _():
                    attend_back(batch, couple, each)

        for step in range(6):

            @pl.when(time == 9 + step)
            def _():
                send_heads(step)

        @pl.when(time == 10)
        def _():
            load(2, w_in, saved).wait()

            def lend(batch, carry):
                cots[0, batch] = near_normed(batch, 1 - core).astype(BF16)
                return carry

            lax.fori_loop(0, 2, lend, 0)
            to_pair(1, cots.at[0], pair_land).start()
            load(7, x_in, cots.at[1]).start()
            load(6, kept_in.at[0], kept).start()

        @pl.when(time == 11)
        def _():
            to_pair(1, cots.at[0], pair_land).wait()
            load(7, x_in, cots.at[1]).wait()

            def close(batch, carry):
                load(6, kept_in.at[batch], kept).wait()
                rows = cots[1, batch].astype(F32)
                scale = lax.rsqrt(jnp.mean(rows * rows, axis=1, keepdims=True) + EPS)
                unit = rows * scale
                pulled = near_normed(batch, core) + pair_land[batch].astype(F32)
                pulled = pulled * gain_rows[0:1]
                shared = jnp.mean(pulled * unit, axis=1, keepdims=True)
                grad = kept[...] + scale * (pulled - unit * shared)
                cots[0, batch] = grad.astype(BF16)

                @pl.when(batch == 0)
                def _():
                    load(6, kept_in.at[1], kept).start()

                return carry

            lax.fori_loop(0, 2, close, 0)
            load(7, cots.at[0], grad_out).start()

    def next_terms(time):
        @pl.when(time + 1 < CHUNKS - 2)
        def _():
            load(2, saved_in.at[0], saved).wait()
            wide_terms(time + 1)

        @pl.when(time + 2 < CHUNKS - 2)
        def _():
            load(2, saved_in.at[time + 2], saved).start()

        @pl.when(time == CHUNKS - 4)
        def _():
            load(0, normed_in, rows_all).start()
            load(2, w_in, saved).start()

        @pl.when(time == CHUNKS - 3)
        def _():
            load(0, normed_in, rows_all).wait()
            slot = (CHUNKS - 2) % SUM_SLOTS
            put(slot, pl.ds(0, 768), rows_all[...].reshape(2048, 1024), grads[:, :, 0:768].reshape(2048, 768))

        @pl.when(time == CHUNKS - 2)
        def _():
            slot = (CHUNKS - 1) % SUM_SLOTS
            put(slot, pl.ds(0, 256), rows_all[...].reshape(2048, 1024), grads[:, :, 768:1024].reshape(2048, 256))
            put(slot, pl.ds(256, 512), branch[...].reshape(2048, 1024), mixed[...].reshape(2048, 512))

    def body(time, carry):
        scatter.tick(time)
        work(time)
        next_terms(time)
        return carry

    lax.fori_loop(0, CHUNKS + 5, body, 0)
    load(7, cots.at[0], grad_out).wait()

    def hand(half):
        return to_pair(0, totals.at[:, other, :], sums_out.at[half])

    own = load(0, totals.at[:, mine, :], sums_out.at[core])
    own.start()
    hand(core).start()
    head_store = load(1, head_sum, head_out)
    head_store.start()
    hand(core).wait_send()
    hand(1 - core).wait_recv()
    head_store.wait()
    own.wait()


def backward_call(forward, inputs, query_gain, key_gain):
    rows = inputs.shape[1]
    (
        w, normed, raw, qkv, table, mask, total, mix, ffn, cot, saved, _, branch, kept, gain_rows,
    ) = forward
    gains = jnp.concatenate([jnp.tile(query_gain, 8), jnp.tile(key_gain, 4)]).astype(F32)[None]
    anywhere = pl.BlockSpec(memory_space=pl.ANY)
    inside = pl.BlockSpec(memory_space=pltpu.VMEM)
    return pl.pallas_call(
        backward_kernel,
        out_shape=[
            jax.ShapeDtypeStruct((2, rows, 1024), BF16),
            jax.ShapeDtypeStruct((2, CHUNKS, 32, WIDE), F32),
            jax.ShapeDtypeStruct((2, 8, 128), F32),
        ],
        in_specs=[anywhere] * 14 + [inside] * 2,
        out_specs=[anywhere] * 3,
        scratch_shapes=[pltpu.VMEM((SUM_SLOTS, 4, 2, 2, 64, WIDE), BF16)]
        + land_shapes()
        + [
            pltpu.VMEM((CHUNKS, 64, WIDE), F32),
            pltpu.VMEM((2, rows, 1024), BF16),
            pltpu.VMEM((2, 2, rows, 1024), BF16),
            pltpu.VMEM((2, 2, rows, 1024), BF16),
            pltpu.VMEM((2, 2, rows, WIDE), BF16),
            pltpu.VMEM((2, 2, rows, 1024), BF16),
            pltpu.VMEM((2, SEQ, 1024), BF16),
            pltpu.VMEM((SEQ, 1024), BF16),
            pltpu.VMEM((SEQ, WIDE), BF16),
            pltpu.VMEM((SEQ, 256), F32),
            pltpu.VMEM((SEQ, 128), F32),
            pltpu.VMEM((SEQ, SEQ), BF16),
            pltpu.VMEM((2, SEQ, 512), BF16),
            pltpu.VMEM((2, SEQ, 512), BF16),
            pltpu.VMEM((2, 512, 512), BF16),
            pltpu.VMEM((2, SEQ, 128), BF16),
            pltpu.VMEM((2, SEQ, 128), BF16),
            pltpu.VMEM((SEQ, 128), F32),
            pltpu.VMEM((SEQ, 128), F32),
            pltpu.VMEM((2, 8, 128), F32),
            pltpu.VMEM((5, 2, 8, 128), F32),
            pltpu.VMEM((rows, 1024), F32),
            pltpu.SemaphoreType.DMA((11,)),
            pltpu.SemaphoreType.DMA((2,)),
            pltpu.SemaphoreType.DMA((2,)),
            pltpu.SemaphoreType.DMA((5,)),
            pltpu.SemaphoreType.DMA((5,)),
        ]
        + semaphores(),
        compiler_params=params(1),
        name="backward",
    )(
        w.reshape(2, 2, rows, WIDE), normed.reshape(2, 2, rows, 1024), raw, qkv, table, mask, total,
        mix, ffn, cot, saved, branch, kept, inputs, gain_rows, gains,
    )


def unpack(out):
    def both(chunk, start, stop):
        return jnp.concatenate([out[0, chunk, :, start:stop], out[1, chunk, :, start:stop]], axis=1)

    def wide_of(start):
        return out[:, :-2, :, start : start + 256].transpose(2, 0, 1, 3).reshape(out.shape[2], -1)

    return (
        both(-2, 0, 512),
        both(-2, 512, 768),
        both(-1, 0, 256),
        both(-1, 256, 768),
        wide_of(0),
        wide_of(256),
        wide_of(512),
    )


def gain_terms(gain, weights, grads):
    total = sum(jnp.sum(w.astype(F32) * g, axis=1) for w, g in zip(weights, grads))
    return total / gain.astype(F32)


def local_grid(
    inputs,
    segments,
    attn_gain,
    w_query,
    key_projection,
    value_projection,
    w_output,
    query_gain,
    key_norm_gain,
    ffn_gain,
    w_gate,
    w_up,
    w_down,
    cotangent,
):
    packed = pack_halves(
        w_query, key_projection, value_projection, w_output.T, w_gate, w_up, w_down.T
    )
    forward = forward_call(
        packed, pack_gains(attn_gain, ffn_gain), inputs, cotangent, segments, query_gain, key_norm_gain
    )
    input_grad, sums, heads = backward_call(forward, inputs, query_gain, key_norm_gain)
    query, key, value, output_t, gate, up, down_t = unpack(sums)
    heads = jnp.sum(heads, axis=1)
    heads = heads[:, :64] + heads[:, 64:]
    attn_weights = (w_query, key_projection, value_projection)
    return (
        forward[11],
        input_grad,
        gain_terms(attn_gain, attn_weights, (query, key, value)),
        query,
        key,
        value,
        output_t.T,
        heads[0],
        heads[1],
        gain_terms(ffn_gain, (w_gate, w_up), (gate, up)),
        gate,
        up,
        down_t.T,
    )


def from_behind(block, axis, distance):
    devices = range(lax.axis_size(axis))
    route = [(i - distance, i) for i in devices if i - distance in devices]
    return lax.ppermute(block, axis, route)


def row_norm(values, gain_row):
    return values * lax.rsqrt(jnp.mean(values * values, axis=-1, keepdims=True) + EPS) * gain_row


def angles(places, head_width):
    counter = jnp.arange(head_width // 2, dtype=jnp.float32)
    inverse = jnp.power(jnp.float32(THETA), -2.0 * counter / head_width)
    turned = places.astype(jnp.float32)[:, None] * inverse[None, :]
    return (jnp.cos(turned), jnp.sin(turned))


def prepare_inputs(raw_rows, gain_row, cosine_table, sine_table_rows, head_count):
    token_count = raw_rows.shape[0]
    head_width = gain_row.shape[0]
    split_rows = raw_rows.reshape(token_count, head_count, head_width)
    normed = row_norm(split_rows, gain_row)
    first_half = normed[..., : head_width // 2]
    second = normed[..., head_width // 2 :]
    cos_rows = cosine_table[:, None, :]
    sin_rows = sine_table_rows[:, None, :]
    turned = jnp.concatenate(
        [first_half * cos_rows - second * sin_rows, second * cos_rows + first_half * sin_rows],
        axis=-1,
    )
    return turned.reshape(token_count, head_count * head_width)


def plain_product(left_rows, right_rows):
    return jnp.dot(left_rows, right_rows, preferred_element_type=jnp.float32)


def rows_product(left_rows, right_rows):
    return lax.dot_general(
        left_rows, right_rows, (((0,), (0,)), ((), ())), preferred_element_type=jnp.float32
    )


def cols_product(left_rows, right_rows):
    return lax.dot_general(
        left_rows, right_rows, (((1,), (1,)), ((), ())), preferred_element_type=jnp.float32
    )


def silu_product(gate_raw, upward):
    return gate_raw * jax.nn.sigmoid(gate_raw) * upward


def add_sets(former_set, latter_set):
    if former_set is None:
        return latter_set
    return tuple((former + latter for former, latter in zip(former_set, latter_set)))


def local(
    inputs,
    segments,
    attn_gain,
    w_query,
    key_projection,
    value_projection,
    w_output,
    query_gain,
    key_norm_gain,
    ffn_gain,
    w_gate,
    w_up,
    w_down,
    cotangent,
):
    batches = inputs.shape[0]
    tokens = inputs.shape[1]
    head_width = query_gain.shape[0]
    query_width = w_query.shape[1]
    kv_width = key_projection.shape[1]
    query_head_rows = query_width // head_width
    kv_heads = kv_width // head_width
    heads_per_group = query_head_rows // kv_heads
    scale = 1.0 / math.sqrt(head_width)
    query_gain_f = query_gain.astype(jnp.float32)
    key_gain_f = key_norm_gain.astype(jnp.float32)
    device_index = lax.axis_index("fsdp")
    places_row = jnp.arange(tokens, dtype=jnp.int32)
    causal = places_row[None, :] <= places_row[:, None]
    same_run = device_index * tokens // SEQ == (device_index - 1) * tokens // SEQ
    outputs_list = []
    grads_list = []
    shard_sums = None
    gain_sums = None
    for batch_index in range(batches):
        gathered = (
            lax.all_gather(attn_gain, "fsdp", axis=0, tiled=True),
            lax.all_gather(w_query, "fsdp", axis=0, tiled=True),
            lax.all_gather(key_projection, "fsdp", axis=0, tiled=True),
            lax.all_gather(value_projection, "fsdp", axis=0, tiled=True),
            lax.all_gather(w_output, "fsdp", axis=1, tiled=True),
            lax.all_gather(ffn_gain, "fsdp", axis=0, tiled=True),
            lax.all_gather(w_gate, "fsdp", axis=0, tiled=True),
            lax.all_gather(w_up, "fsdp", axis=0, tiled=True),
            lax.all_gather(w_down, "fsdp", axis=1, tiled=True),
        )
        (
            gain_attn,
            full_query,
            full_key,
            full_value,
            full_output,
            gain_ffn,
            full_gate,
            full_up,
            full_down,
        ) = gathered
        hidden = inputs[batch_index].astype(jnp.float32)
        segment = segments[batch_index]
        normed_f, norm_pull = jax.vjp(row_norm, hidden, gain_attn.astype(jnp.float32))
        normed = normed_f.astype(jnp.bfloat16)
        query_raw = plain_product(normed, full_query)
        key_projected = plain_product(normed, full_key)
        value_reduced = plain_product(normed, full_value).astype(jnp.bfloat16)
        lower_count = jnp.sum((segment[None, :] < segment[:, None]).astype(jnp.int32), axis=1)
        local_places = places_row - lower_count
        cos_local, sin_local = angles(local_places, head_width)
        key_sent = prepare_inputs(key_projected, key_gain_f, cos_local, sin_local, kv_heads).astype(
            jnp.bfloat16
        )
        remote_key, remote_value, remote_segment = from_behind(
            (key_sent, value_reduced, segment.astype(jnp.bfloat16)), "fsdp", 1
        )
        remote_match = (remote_segment.astype(jnp.int32)[None, :] == segment[:, None]) & same_run
        places_all = local_places + jnp.sum(remote_match.astype(jnp.int32), axis=1)
        cosine_table, sine_table_rows = angles(places_all, head_width)
        query_f, query_pull = jax.vjp(
            lambda raw_rows, gain_row: prepare_inputs(
                raw_rows, gain_row, cosine_table, sine_table_rows, query_head_rows
            ),
            query_raw,
            query_gain_f,
        )
        key_f, key_pull = jax.vjp(
            lambda raw_rows, gain_row: prepare_inputs(
                raw_rows, gain_row, cosine_table, sine_table_rows, kv_heads
            ),
            key_projected,
            key_gain_f,
        )
        query_low = query_f.astype(jnp.bfloat16)
        key_low = key_f.astype(jnp.bfloat16)
        allowed = jnp.concatenate(
            [remote_match, causal & (segment[None, :] == segment[:, None])], axis=1
        )
        query_split = query_low.reshape(tokens, kv_heads, heads_per_group, head_width).transpose(
            1, 0, 2, 3
        )
        key_split = (
            jnp.concatenate([remote_key, key_low], axis=0)
            .reshape(2 * tokens, kv_heads, head_width)
            .transpose(1, 0, 2)
        )
        value_split = (
            jnp.concatenate([remote_value, value_reduced], axis=0)
            .reshape(2 * tokens, kv_heads, head_width)
            .transpose(1, 0, 2)
        )

        def head_forward(blocks):
            query_part, key_part, value_part = blocks
            scores = (
                jnp.einsum("tgd,ld->gtl", query_part, key_part, preferred_element_type=jnp.float32)
                * scale
            )
            scores = jnp.where(allowed[None], scores, NEG)
            row_peak = jnp.max(scores, axis=-1, keepdims=True)
            raised = jnp.exp(scores - row_peak)
            row_total = jnp.sum(raised, axis=-1, keepdims=True)
            prob_rows = (raised / row_total).astype(jnp.bfloat16)
            mixed_part = jnp.einsum(
                "gtl,ld->tgd", prob_rows, value_part, preferred_element_type=jnp.float32
            )
            return (mixed_part.astype(jnp.bfloat16), (row_peak + jnp.log(row_total))[..., 0])

        mixed_split, log_totals = lax.map(head_forward, (query_split, key_split, value_split))
        attn_mix = mixed_split.transpose(1, 0, 2, 3).reshape(tokens, query_width)
        attended = hidden + plain_product(attn_mix, full_output)
        ffn_f, ffn_pull = jax.vjp(row_norm, attended, gain_ffn.astype(jnp.float32))
        ffn_in = ffn_f.astype(jnp.bfloat16)
        gate_raw = plain_product(ffn_in, full_gate)
        upward = plain_product(ffn_in, full_up)
        active_f, active_pull = jax.vjp(silu_product, gate_raw, upward)
        active = active_f.astype(jnp.bfloat16)
        result = attended + plain_product(active, full_down)
        outputs_list.append(result.astype(jnp.bfloat16))
        back_query, back_key, back_value, back_output, back_gate, back_up, back_down = (
            lax.all_gather(w_query, "fsdp", axis=0, tiled=True),
            lax.all_gather(key_projection, "fsdp", axis=0, tiled=True),
            lax.all_gather(value_projection, "fsdp", axis=0, tiled=True),
            lax.all_gather(w_output, "fsdp", axis=1, tiled=True),
            lax.all_gather(w_gate, "fsdp", axis=0, tiled=True),
            lax.all_gather(w_up, "fsdp", axis=0, tiled=True),
            lax.all_gather(w_down, "fsdp", axis=1, tiled=True),
        )
        grad_result = cotangent[batch_index]
        grad_down_t = rows_product(grad_result, active)
        grad_active = cols_product(grad_result, back_down)
        grad_gate_f, grad_up_f = active_pull(grad_active)
        grad_gate_low = grad_gate_f.astype(jnp.bfloat16)
        grad_up_low = grad_up_f.astype(jnp.bfloat16)
        grad_gate_w = rows_product(ffn_in, grad_gate_low)
        grad_up_w = rows_product(ffn_in, grad_up_low)
        grad_ffn_in = cols_product(grad_gate_low, back_gate) + cols_product(grad_up_low, back_up)
        grad_attended_norm, grad_ffn_gain = ffn_pull(grad_ffn_in)
        grad_attended = grad_result.astype(jnp.float32) + grad_attended_norm
        grad_branch = grad_attended.astype(jnp.bfloat16)
        grad_output_t = rows_product(grad_branch, attn_mix)
        grad_mixed = cols_product(grad_branch, back_output).astype(jnp.bfloat16)
        grad_split = grad_mixed.reshape(tokens, kv_heads, heads_per_group, head_width).transpose(
            1, 0, 2, 3
        )

        def head_backward(blocks):
            query_part, key_part, value_part, grad_part, log_part = blocks
            scores = (
                jnp.einsum("tgd,ld->gtl", query_part, key_part, preferred_element_type=jnp.float32)
                * scale
            )
            scores = jnp.where(allowed[None], scores, NEG)
            prob_rows = jnp.exp(scores - log_part[..., None])
            grad_probs = jnp.einsum(
                "tgd,ld->gtl", grad_part, value_part, preferred_element_type=jnp.float32
            )
            center = jnp.sum(prob_rows * grad_probs, axis=-1, keepdims=True)
            grad_scores = (prob_rows * (grad_probs - center)).astype(jnp.bfloat16)
            grad_query_part = (
                jnp.einsum("gtl,ld->tgd", grad_scores, key_part, preferred_element_type=jnp.float32)
                * scale
            )
            grad_key_part = (
                jnp.einsum(
                    "gtl,tgd->ld", grad_scores, query_part, preferred_element_type=jnp.float32
                )
                * scale
            )
            grad_value_part = jnp.einsum(
                "gtl,tgd->ld",
                prob_rows.astype(jnp.bfloat16),
                grad_part,
                preferred_element_type=jnp.float32,
            )
            return (grad_query_part, grad_key_part, grad_value_part)

        grad_query_split, grad_key_split, grad_value_split = lax.map(
            head_backward, (query_split, key_split, value_split, grad_split, log_totals)
        )
        grad_query_rot = grad_query_split.transpose(1, 0, 2, 3).reshape(tokens, query_width)
        grad_key_all = grad_key_split.transpose(1, 0, 2).reshape(2 * tokens, kv_width)
        grad_value_all = grad_value_split.transpose(1, 0, 2).reshape(2 * tokens, kv_width)
        back_key_grad, back_value_grad = (
            from_behind(grad_key_all[:tokens].astype(jnp.bfloat16), "fsdp", -1).astype(jnp.float32),
            from_behind(grad_value_all[:tokens].astype(jnp.bfloat16), "fsdp", -1).astype(
                jnp.float32
            ),
        )
        grad_key_rot = grad_key_all[tokens:] + back_key_grad
        grad_value_low = (grad_value_all[tokens:] + back_value_grad).astype(jnp.bfloat16)
        grad_query_raw, grad_query_gain = query_pull(grad_query_rot)
        grad_key_raw, grad_key_gain = key_pull(grad_key_rot)
        grad_query_low = grad_query_raw.astype(jnp.bfloat16)
        grad_key_low = grad_key_raw.astype(jnp.bfloat16)
        grad_query_w = rows_product(normed, grad_query_low)
        grad_key_w = rows_product(normed, grad_key_low)
        grad_value_w = rows_product(normed, grad_value_low)
        grad_normed = (
            cols_product(grad_query_low, back_query)
            + cols_product(grad_key_low, back_key)
            + cols_product(grad_value_low, back_value)
        )
        grad_hidden_norm, grad_attn_gain = norm_pull(grad_normed)
        grads_list.append((grad_attended + grad_hidden_norm).astype(jnp.bfloat16))
        gain_sums = add_sets(gain_sums, (grad_query_gain, grad_key_gain))
        shard_terms = (
            lax.psum_scatter(grad_attn_gain, "fsdp", scatter_dimension=0, tiled=True),
            lax.psum_scatter(grad_query_w, "fsdp", scatter_dimension=0, tiled=True),
            lax.psum_scatter(grad_key_w, "fsdp", scatter_dimension=0, tiled=True),
            lax.psum_scatter(grad_value_w, "fsdp", scatter_dimension=0, tiled=True),
            lax.psum_scatter(grad_output_t, "fsdp", scatter_dimension=0, tiled=True),
            lax.psum_scatter(grad_ffn_gain, "fsdp", scatter_dimension=0, tiled=True),
            lax.psum_scatter(grad_gate_w, "fsdp", scatter_dimension=0, tiled=True),
            lax.psum_scatter(grad_up_w, "fsdp", scatter_dimension=0, tiled=True),
            lax.psum_scatter(grad_down_t, "fsdp", scatter_dimension=0, tiled=True),
        )
        shard_sums = add_sets(shard_sums, shard_terms)
    head_sums = lax.psum((gain_sums[0], gain_sums[1]), "fsdp")
    return (
        jnp.stack(outputs_list),
        jnp.stack(grads_list),
        shard_sums[0],
        shard_sums[1],
        shard_sums[2],
        shard_sums[3],
        shard_sums[4].T,
        head_sums[0],
        head_sums[1],
        shard_sums[5],
        shard_sums[6],
        shard_sums[7],
        shard_sums[8].T,
    )


def solution(mesh):
    return jax.shard_map(
        local_grid if mesh.shape["fsdp"] == 32 else local,
        mesh=mesh,
        in_specs=(
            P(None, "fsdp", None),
            P(None, "fsdp"),
            P("fsdp"),
            P("fsdp", None),
            P("fsdp", None),
            P("fsdp", None),
            P(None, "fsdp"),
            P(),
            P(),
            P("fsdp"),
            P("fsdp", None),
            P("fsdp", None),
            P(None, "fsdp"),
            P(None, "fsdp", None),
        ),
        out_specs=(
            P(None, "fsdp", None),
            P(None, "fsdp", None),
            P("fsdp"),
            P("fsdp", None),
            P("fsdp", None),
            P("fsdp", None),
            P(None, "fsdp"),
            P(),
            P(),
            P("fsdp"),
            P("fsdp", None),
            P("fsdp", None),
            P(None, "fsdp"),
        ),
        check_vma=False,
    )
```

```python
import math

import jax
import jax.numpy as jnp
import numpy as np
from jax import lax
from jax.experimental import pallas as pl
from jax.experimental.pallas import tpu as pltpu
from jax.sharding import PartitionSpec as P

SEQ = 1024


EPS = 1e-05
THETA = 1000000.0
NEG = -1e30


CHUNKS = 11
WIDE = 768
MESH = pl.DeviceIdType.MESH
ALL = slice(None)
F32 = jnp.float32
BF16 = jnp.bfloat16
PARTS = (
    ("A", pl.ds(0, 48), pl.ds(0, 384)),
    ("B", pl.ds(0, 48), pl.ds(384, 384)),
    ("C", pl.ds(48, 16), pl.ds(0, 768)),
)
GAINS = len(PARTS)
OUTWARD = {
    "A": ("z0", "z1", "z2", "y", "x"),
    "B": ("z0", "z1", "z2", "x", "y"),
    "C": ("x", "y", "z0", "z1", "z2"),
}
INWARD = {
    "A": ("x", "y", "z0", "z1", "z2"),
    "B": ("y", "x", "z0", "z1", "z2"),
    "C": ("z0", "z1", "z2", "y", "x"),
}
SUM_SLOTS = 6
HELD = 2
LAND_SLOTS = 3


def place():
    me = lax.axis_index("fsdp")
    return me, me // 8, (me // 4) % 2, (me // 2) % 2, me % 2


def guarded(condition, action):
    if condition is None:
        action()
    else:
        pl.when(condition)(action)


def greet(me, z, far=0):
    gate = pltpu.get_barrier_semaphore()
    for bit in (1, 2, 4):
        pl.semaphore_signal(gate, inc=1, device_id=(me ^ bit,), device_id_type=MESH)

    @pl.when(z > 0)
    def _():
        pl.semaphore_signal(gate, inc=1, device_id=(me - 8,), device_id_type=MESH)

    @pl.when(z < 3)
    def _():
        pl.semaphore_signal(gate, inc=1, device_id=(me + 8,), device_id_type=MESH)

    if far:
        pl.semaphore_signal(gate, inc=1, device_id=(me ^ far,), device_id_type=MESH)
    pl.semaphore_wait(gate, (4 if far else 3) + (z > 0).astype(jnp.int32) + (z < 3).astype(jnp.int32))


class Gather:
    def __init__(self, full, tiles, sent, landed):
        self.full, self.tiles, self.sent, self.landed = full, tiles, sent, landed
        self.me, self.z, self.y, self.x, self.core = place()

    def moves(self, part, step, chunk):
        kind, rows, columns = PARTS[0] if part == GAINS else PARTS[part]
        z, y, x, me = self.z, self.y, self.x, self.me

        def view(zz, yy, xx):
            if part == GAINS:
                return self.tiles.at[zz, yy, xx]
            return self.full.at[chunk, zz, yy, xx, rows, columns]

        axis = OUTWARD[kind][step]
        if axis[0] == "z":
            far = int(axis[1])
            yy, xx = (ALL, ALL) if kind == "C" else (y, x)
            return (
                ((z >= far) & (z < 3), z - far, me + 8, z >= far + 1, z - 1 - far),
                ((z <= 3 - far) & (z > 0), z + far, me - 8, z <= 2 - far, z + 1 + far),
            ), lambda zz: view(zz, yy, xx)
        zz = z if kind == "C" else ALL
        if axis == "y":
            xx = x if kind == "A" else ALL
            return ((None, y, me ^ 4, None, 1 - y),), lambda yy: view(zz, yy, xx)
        yy = ALL if kind == "A" else y
        return ((None, x, me ^ 2, None, 1 - x),), lambda xx: view(zz, yy, xx)

    def copy(self, ref, device, part, step, chunk, way):
        return pltpu.make_async_remote_copy(
            src_ref=ref,
            dst_ref=ref,
            send_sem=self.sent.at[chunk, part, step, way],
            recv_sem=self.landed.at[chunk, part, step, way],
            device_id=(device,),
            device_id_type=MESH,
        )

    def send(self, part, step, chunk):
        moves, view = self.moves(part, step, chunk)
        for way, (sends, mine, device, _, _) in enumerate(moves):
            guarded(
                sends,
                lambda: self.copy(view(mine), device, part, step, chunk, way).start(),
            )

    def receive(self, part, step, chunk):
        moves, view = self.moves(part, step, chunk)
        for way, (_, _, _, receives, other) in enumerate(moves):
            guarded(
                receives,
                lambda: self.copy(view(other), self.me ^ 2, part, step, chunk, way).wait_recv(),
            )

    def finish(self, part, step, chunk):
        moves, view = self.moves(part, step, chunk)
        for way, (sends, mine, device, _, _) in enumerate(moves):
            guarded(
                sends,
                lambda: self.copy(view(mine), device, part, step, chunk, way).wait_send(),
            )

    def tick(self, time, parts):
        for step in range(6):
            age = time - step
            chunk = jnp.where(age < 2, age, age - HELD)

            @pl.when((age >= 0) & (chunk < CHUNKS) & ((age < 2) | (chunk >= 2)))
            def _():
                for part in parts:
                    if step > 0:
                        self.receive(part, step - 1, chunk)
                    if step < 5:
                        self.send(part, step, chunk)

    def tick_gains(self, step):
        if step > 0:
            self.receive(GAINS, step - 1, 0)
        if step < 5:
            self.send(GAINS, step, 0)

    def drain(self):
        def body(chunk, carry):
            for part in range(len(PARTS)):
                for step in range(5):
                    self.finish(part, step, chunk)
            return carry

        lax.fori_loop(0, CHUNKS, body, 0)
        for step in range(5):
            self.finish(GAINS, step, 0)


class Scatter:
    def __init__(self, sums, lands, totals, sent, landed):
        self.sums, self.lands, self.totals = sums, lands, totals
        self.sent, self.landed = sent, landed
        self.me, self.z, self.y, self.x, self.core = place()

    def moves(self, part, step, chunk):
        kind, rows, columns = PARTS[part]
        z, y, x, me = self.z, self.y, self.x, self.me
        slot, land = lax.rem(chunk, SUM_SLOTS), lax.rem(chunk, LAND_SLOTS)
        first, second, up, down = self.lands[part]
        axis = INWARD[kind][step]

        def view(zz, yy, xx):
            return self.sums.at[slot, zz, yy, xx, rows, columns]

        if axis[0] == "z":
            far = int(axis[1])
            count = 3 - far
            yy, xx = (ALL, ALL) if kind == "C" else (y, x)
            above, below = pl.ds(far + 1, count), pl.ds(0, count)
            up_land, down_land = up.at[land, pl.ds(far, count)], down.at[land, pl.ds(0, count)]
            return (
                (z == far, view(above, yy, xx), up_land, me + 8, z == far + 1, view(above, yy, xx)),
                (z == 3 - far, view(below, yy, xx), down_land, me - 8, z == 2 - far, view(below, yy, xx)),
            )
        zz = z if kind == "C" else ALL
        ref = (first if step == 0 or (kind == "C" and step == 3) else second).at[land]
        if axis == "x":
            yy = ALL if kind == "A" else y
            return ((None, view(zz, yy, 1 - x), ref, me ^ 2, None, view(zz, yy, x)),)
        xx = x if kind == "A" else ALL
        return ((None, view(zz, 1 - y, xx), ref, me ^ 4, None, view(zz, y, xx)),)

    def copy(self, source, target, device, part, step, chunk, way):
        return pltpu.make_async_remote_copy(
            src_ref=source,
            dst_ref=target,
            send_sem=self.sent.at[chunk, part, step, way],
            recv_sem=self.landed.at[chunk, part, step, way],
            device_id=(device,),
            device_id_type=MESH,
        )

    def step(self, part, step, chunk):
        if step > 0:
            for way, move in enumerate(self.moves(part, step - 1, chunk)):
                sends, source, land, device, receives, target = move

                def add():
                    self.copy(land, land, self.me ^ 2, part, step - 1, chunk, way).wait_recv()
                    target[...] = (target[...].astype(F32) + land[...].astype(F32)).astype(BF16)

                guarded(receives, add)
                guarded(
                    sends,
                    lambda: self.copy(source, land, device, part, step - 1, chunk, way).wait_send(),
                )
        if step < 5:
            for way, move in enumerate(self.moves(part, step, chunk)):
                sends, source, land, device, _, _ = move
                guarded(
                    sends,
                    lambda: self.copy(source, land, device, part, step, chunk, way).start(),
                )
        else:
            _, rows, columns = PARTS[part]
            slot = lax.rem(chunk, SUM_SLOTS)
            self.totals[lax.rem(chunk + 2, CHUNKS), rows, columns] = self.sums[
                slot, self.z, self.y, self.x, rows, columns
            ].astype(F32)

    def tick(self, time, parts):
        for step in range(5, -1, -1):
            chunk = time - step

            @pl.when((chunk >= 0) & (chunk < CHUNKS))
            def _():
                for part in parts:
                    self.step(part, step, chunk)


def pair_rows(core):
    mine = pl.ds(pl.multiple_of(core * 32, 32), 32)
    other = pl.ds(pl.multiple_of((1 - core) * 32, 32), 32)
    return mine, other


def semaphores():
    return [pltpu.SemaphoreType.DMA((CHUNKS, len(PARTS) + 1, 5, 2))] * 2


def land_shapes():
    slots = LAND_SLOTS
    plain = [(slots, 4, 2, 48, 384), (slots, 4, 48, 384), (slots, 3, 48, 384), (slots, 3, 48, 384)]
    late = [(slots, 2, 16, 768), (slots, 16, 768), (slots, 3, 2, 2, 16, 768), (slots, 3, 2, 2, 16, 768)]
    return [pltpu.VMEM(shape, BF16) for shape in plain + plain + late]


def params(number):
    return pltpu.CompilerParams(
        collective_id=number, has_side_effects=True, vmem_limit_bytes=62 * 2**20
    )


EAGER = 7
SPREAD = 3
LATER = CHUNKS + 5 + HELD - EAGER - SPREAD


def contract(left, right, left_dim, right_dim):
    return lax.dot_general(
        left, right, (((left_dim,), (right_dim,)), ((), ())), preferred_element_type=F32
    )


def lane_index(shape):
    return lax.broadcasted_iota(jnp.int32, shape, 1)


def half_turn(rows):
    width = rows.shape[1]
    first = lane_index(rows.shape) % 64 < 32
    return jnp.where(first, pltpu.roll(rows, width - 32, 1), pltpu.roll(rows, 32, 1))


def head_means(rows, ones):
    parts = [
        contract(rows[:, k : k + 256].astype(BF16), ones, 1, 0)
        for k in range(0, rows.shape[1], 256)
    ]
    return jnp.concatenate(parts, axis=1)


def head_ones():
    row = lax.broadcasted_iota(jnp.int32, (256, 256), 0) // 64
    column = lax.broadcasted_iota(jnp.int32, (256, 256), 1) // 64
    return jnp.where(row == column, 1.0 / 64.0, 0.0).astype(BF16)


def tiled(table, copies):
    return jnp.concatenate([table] * copies, axis=1)


def split_pair(rows, group):
    pair = rows[:, 128 * (group // 2) : 128 * (group // 2) + 128]
    low = lane_index(pair.shape) < 64
    if group % 2 == 0:
        kept = jnp.where(low, pair, 0.0)
        return kept, pltpu.roll(kept, 64, 1)
    kept = jnp.where(low, 0.0, pair)
    return pltpu.roll(kept, 64, 1), kept


def lanes_at(block, width):
    return pl.ds(pl.multiple_of(block * width, width), width)


def forward_kernel(*refs):
    packed, tile_in, x_in, cot_in, seg_in, gains, inverse = refs[:7]
    (
        w_out, normed_out, raw_out, qkv_out, table_out, mask_out, total_out, mix_out,
        ffn_out, cot_out, saved_out, result_out, branch_out, kept_out, gain_out,
    ) = refs[7:22]
    (
        full, tiles, gain_rows, rows_all, cots, seg_rows, mixed, mixed_pair, wo_pair, attended,
        lent, local, pair_sent, pair_landed, sent, landed,
    ) = refs[22:]
    me, z, y, x, core = place()
    pair = (me ^ 1,)
    greet(me, z)
    mine, other = pair_rows(core)

    def to_pair(number, source, target):
        return pltpu.make_async_remote_copy(
            src_ref=source,
            dst_ref=target,
            send_sem=pair_sent.at[number],
            recv_sem=pair_landed.at[number],
            device_id=pair,
            device_id_type=MESH,
        )

    def keep(number, source, target):
        return pltpu.make_async_copy(source, target, local.at[number])

    own_w = keep(0, packed.at[core], full.at[:, z, y, x, mine, :])
    own_x = keep(1, x_in, rows_all.at[:, core])
    own_cot = keep(2, cot_in, cots.at[:, core])
    own_seg = keep(3, seg_in, seg_rows.at[core])
    give_w = to_pair(0, packed.at[1 - core], full.at[:, z, y, x, mine, :])
    take_w = to_pair(0, packed.at[1 - core], full.at[:, z, y, x, other, :])
    give_x = to_pair(1, x_in, rows_all.at[:, core])
    take_x = to_pair(1, x_in, rows_all.at[:, 1 - core])
    give_cot = to_pair(2, cot_in, cots.at[:, core])
    take_cot = to_pair(2, cot_in, cots.at[:, 1 - core])
    give_seg = to_pair(3, seg_in, seg_rows.at[core])
    take_seg = to_pair(3, seg_in, seg_rows.at[1 - core])
    own_tile = keep(4, tile_in, tiles.at[z, y, x, core])
    give_tile = to_pair(9, tile_in, tiles.at[z, y, x, core])
    own_tile.start()
    give_tile.start()
    own_w.start()
    give_w.start()
    own_seg.start()
    give_seg.start()
    own_x.start()
    give_x.start()
    own_cot.start()
    give_cot.start()
    own_w.wait()
    take_w.wait_recv()
    own_tile.wait()
    to_pair(9, tile_in, tiles.at[z, y, x, 1 - core]).wait_recv()
    gather = Gather(full, tiles, sent, landed)

    def early(time, carry):
        for step in range(6):

            @pl.when(time == step)
            def _():
                gather.tick_gains(step)

        gather.tick(time, (0, 1, 2))
        return carry

    lax.fori_loop(0, EAGER, early, 0)
    for block in range(8):
        quad = tiles[block // 2, block % 2]
        quad = quad[0, 0] + quad[0, 1] + quad[1, 0] + quad[1, 1]
        gain_rows[:, 128 * block : 128 * block + 128] = quad
    keep_gain = keep(11, gain_rows, gain_out)
    keep_gain.start()
    give_wo = to_pair(4, full.at[1, :, :, :, :, pl.ds(256, 512)], wo_pair)
    give_wo.start()
    keep_w = keep(0, full.at[pl.ds(0, 2)], w_out)
    keep_w.start()
    own_x.wait()
    own_seg.wait()
    own_cot.wait()
    take_x.wait_recv()
    take_seg.wait_recv()
    take_cot.wait_recv()
    keep_cot = keep(2, cots, cot_out)
    keep_cot.start()

    def attention(normed, raw, qkv, table, mask, total, keys, values):
        def early_copies(batch):
            return (
                keep(4, normed, normed_out.at[batch]),
                keep(5, raw, raw_out.at[batch]),
                keep(6, qkv, qkv_out.at[batch]),
                keep(7, table, table_out.at[batch]),
                keep(8, mask, mask_out.at[batch]),
            )

        def late_copies(batch):
            return (
                keep(9, total, total_out.at[batch]),
                keep(10, mixed.at[batch], mix_out.at[batch]),
            )

        def project(batch):
            segment = jnp.concatenate([seg_rows[0, batch], seg_rows[1, batch]], axis=1)
            column = jnp.broadcast_to(segment, (128, SEQ)).T
            below = jnp.zeros((SEQ, 128), F32)
            for k in range(0, SEQ, 128):
                below += (segment[:, k : k + 128] < column).astype(F32)
            before = jnp.sum(below, axis=1, keepdims=True)
            spot = lax.broadcasted_iota(jnp.int32, (SEQ, 128), 0).astype(F32) - before
            angle = spot * inverse[...]
            sine = jnp.sin(angle)
            first = lane_index((SEQ, 128)) % 64 < 32
            table[:, 0:128] = jnp.cos(angle)
            table[:, 128:256] = jnp.where(first, -sine, sine)
            for quarter in range(4):
                span = pl.ds(quarter * 256, 256)
                width = (quarter + 1) * 256
                same = segment[:, :width] == column[quarter * 256 : quarter * 256 + 256, 0:1]
                spots = lax.broadcasted_iota(jnp.int32, (256, width), 0) + quarter * 256
                behind = lane_index((256, width)) <= spots
                mask[span, 0:width] = jnp.where(same & behind, 1.0, 0.0).astype(BF16)
            total[...] = jnp.zeros_like(total)
            ones = head_ones()

            def block(half, carry):
                span = pl.ds(pl.multiple_of(half * 512, 512), 512)
                rows = rows_all[batch, half].astype(F32)
                scale = lax.rsqrt(jnp.mean(rows * rows, axis=1, keepdims=True) + EPS)
                unit = (rows * scale * gain_rows[0:1]).astype(BF16)
                normed[span, :] = unit
                weights = full[0].reshape(1024, WIDE)
                product = contract(unit, weights, 1, 0)
                raw[span, :] = product.astype(BF16)
                level = lax.rsqrt(head_means(product * product, ones) + EPS)
                turned = product * level * gains[...]
                cosine = tiled(table[span, 0:128], 6)
                sine_signed = tiled(table[span, 128:256], 6)
                turned = turned * cosine + half_turn(turned) * sine_signed
                query = turned[:, 0:512] * 0.125
                key = turned[:, 512:768].astype(BF16).astype(F32)
                value_weights = full[1, :, :, :, :, 0:256].reshape(1024, 256)
                value = contract(unit, value_weights, 1, 0).astype(BF16).astype(F32)
                qkv[span, 0:512] = query.astype(BF16)
                qkv[span, 512:768] = key.astype(BF16)
                qkv[span, 768:1024] = value.astype(BF16)
                for group in range(4):
                    low, high = split_pair(key, group)
                    keys[group, 0, span, :] = low.astype(BF16)
                    keys[group, 1, span, :] = high.astype(BF16)
                    low, high = split_pair(value, group)
                    values[group, 0, span, :] = low.astype(BF16)
                    values[group, 1, span, :] = high.astype(BF16)
                return carry

            lax.fori_loop(0, 2, block, 0)

        def attend(batch, quarter):
            span = pl.ds(quarter * 256, 256)
            width = (quarter + 1) * 256
            allowed = mask[span, 0:width].astype(F32)
            lane = lane_index((256, 128))

            def group_step(group, carry):
                queries = qkv[span, lanes_at(group, 128)]
                parts, sums = [], []
                for side in range(2):
                    scores = contract(queries, keys[group, side, 0:width, :], 1, 1)
                    raised = jnp.exp(scores) * allowed
                    sums.append(1.0 / jnp.sum(raised, axis=1, keepdims=True))
                    parts.append(
                        contract(raised.astype(BF16), values[group, side, 0:width, :], 1, 0)
                    )
                result = (parts[0] + parts[1]) * jnp.where(lane < 64, sums[0], sums[1])
                mixed[batch, span, lanes_at(group, 128)] = result.astype(BF16)
                old = total[span, :]
                old = jnp.where(lane == 2 * group, sums[0], old)
                total[span, :] = jnp.where(lane == 2 * group + 1, sums[1], old)
                return carry

            lax.fori_loop(0, 4, group_step, 0)

        def piece(number, carry):
            batch, part = number // 4, number % 4

            @pl.when(part == 0)
            def _():
                @pl.when(batch > 0)
                def _():
                    for copy in early_copies(0) + late_copies(0):
                        copy.wait()

                project(batch)
                for copy in early_copies(batch):
                    copy.start()

            for turn in range(2):

                @pl.when((number % 2 == turn) & (number < 2 * SPREAD))
                def _():
                    gather.tick(EAGER + number // 2, ((0,), (1, 2))[turn])

            for quarter in range(4):

                @pl.when(part == quarter)
                def _():
                    attend(batch, quarter)

            @pl.when(part == 3)
            def _():
                for copy in late_copies(batch):
                    copy.start()
                to_pair(5 + batch, mixed.at[batch, lanes_at(1 - core, 512), :], mixed_pair.at[batch]).start()

            return carry

        lax.fori_loop(0, 8, piece, 0)
        for copy in early_copies(1) + late_copies(1):
            copy.wait()

    pl.run_scoped(
        attention,
        pltpu.VMEM((SEQ, 1024), BF16),
        pltpu.VMEM((SEQ, WIDE), BF16),
        pltpu.VMEM((SEQ, 1024), BF16),
        pltpu.VMEM((SEQ, 256), F32),
        pltpu.VMEM((SEQ, SEQ), BF16),
        pltpu.VMEM((SEQ, 128), F32),
        pltpu.VMEM((4, 2, SEQ, 128), BF16),
        pltpu.VMEM((4, 2, SEQ, 128), BF16),
    )
    give_wo.wait_send()
    give_wo.wait_recv()
    give_x.wait_send()

    def swap_mixed(batch):
        return to_pair(5 + batch, mixed.at[batch, lanes_at(1 - core, 512), :], mixed_pair.at[batch])

    def join(batch, carry):
        swap_mixed(batch).wait_recv()
        span = lanes_at(core, 512)
        own_wo = full[1, :, :, :, :, 256:768].reshape(1024, 512)
        result = rows_all[batch, core].astype(F32)
        result += contract(mixed[batch, span, :], own_wo, 1, 1)
        result += contract(mixed_pair[batch], wo_pair[...].reshape(1024, 512), 1, 1)
        attended[batch] = result
        scale = lax.rsqrt(jnp.mean(result * result, axis=1, keepdims=True) + EPS)
        rows_all[batch, core] = (result * scale * gain_rows[1:2]).astype(BF16)
        to_pair(7 + batch, rows_all.at[batch, core], rows_all.at[batch, core]).start()
        return carry

    lax.fori_loop(0, 2, join, 0)
    keep_ffn = keep(3, rows_all, ffn_out)

    def feed_forward(result, back, saved):
        last = CHUNKS - 3

        def save(chunk, batch, half):
            return keep(4 + batch, saved.at[batch], saved_out.at[chunk, batch, half])

        def lend(batch):
            return (
                to_pair(10 + batch, cots.at[batch, 1 - core], lent.at[0, batch]),
                to_pair(12 + batch, rows_all.at[batch, 1 - core], lent.at[1, batch]),
            )

        def chunk_step(chunk, carry):
            def block(part, inner):
                batch = part % 2
                own = (part < 2) != (chunk == last)
                half = jnp.where(own, core, 1 - core)
                for turn in range(2):

                    @pl.when((part == 2 * turn) & (chunk < LATER))
                    def _():
                        gather.tick(EAGER + SPREAD + chunk, ((0,), (1, 2))[turn])

                @pl.when((chunk == 0) & (part >= 2))
                def _():
                    to_pair(
                        7 + batch, rows_all.at[batch, core], rows_all.at[batch, 1 - core]
                    ).wait_recv()

                @pl.when((chunk == 1) & (part == 0))
                def _():
                    keep_ffn.start()

                @pl.when((chunk == last) & (part == 0))
                def _():
                    keep_w.wait()
                    keep_gain.wait()
                    for each in range(2):
                        swap_mixed(each).wait_send()
                    keep_ffn.wait()
                    keep_cot.wait()

                @pl.when((chunk > 0) | (part > 1))
                def _():
                    save(chunk, batch, half).wait()

                up_weights = full[chunk + 2, :, :, :, :, 0:512].reshape(1024, 512)
                down_weights = full[chunk + 2, :, :, :, :, 512:768].reshape(1024, 256)
                both = contract(rows_all[batch, half], up_weights, 1, 0)
                grad = contract(cots[batch, half], down_weights, 1, 0)
                gate, up = both[:, 0:256], both[:, 256:512]
                bend = 1.0 / (1.0 + jnp.exp(-gate))
                silu = gate * bend
                active = (silu * up).astype(BF16)
                grad_up = (grad * silu).astype(BF16)
                grad_gate = (grad * up * bend * (1.0 + gate * (1.0 - bend))).astype(BF16)
                saved[batch, :, 0:256] = grad_gate
                saved[batch, :, 256:512] = grad_up
                saved[batch, :, 512:768] = active
                save(chunk, batch, half).start()
                forward = contract(active, down_weights, 1, 1)
                backward = contract(saved[batch, :, 0:512], up_weights, 1, 1)

                @pl.when(chunk == 0)
                def _():
                    result[batch, half] = forward
                    back[batch, half] = backward

                @pl.when(chunk > 0)
                def _():
                    result[batch, half] += forward
                    back[batch, half] += backward

                @pl.when((chunk == last) & (part < 2))
                def _():
                    cots[batch, half] = result[batch, half].astype(BF16)
                    rows_all[batch, half] = back[batch, half].astype(BF16)
                    for copy in lend(batch):
                        copy.start()

                return inner

            lax.fori_loop(0, 4, block, 0)
            return carry

        lax.fori_loop(0, CHUNKS - 2, chunk_step, 0)

        def give_branch(batch, side):
            columns = pl.ds(512 * side, 512)
            return to_pair(
                14 + 2 * batch + side, cots.at[batch, core, :, columns], mixed.at[batch, columns, :]
            )

        def keep_branch(batch, side):
            columns = pl.ds(512 * side, 512)
            target = branch_out.at[batch, 1 - core, :, columns]
            return keep(8 + 2 * batch + side, mixed.at[batch, columns, :], target)

        def ends(batch):
            return (
                keep(batch, lent.at[0, batch], result_out.at[batch]),
                keep(2 + batch, attended.at[batch], kept_out.at[batch]),
                keep(6 + batch, cots.at[batch, core], branch_out.at[batch, core]),
            )

        def close(batch, carry):
            for copy in lend(batch):
                copy.wait_recv()
            joined = attended[batch]
            outputs = joined + result[batch, core] + lent[0, batch].astype(F32)
            lent[0, batch] = outputs.astype(BF16)
            scale = lax.rsqrt(jnp.mean(joined * joined, axis=1, keepdims=True) + EPS)
            unit = joined * scale
            pulled = (back[batch, core] + lent[1, batch].astype(F32)) * gain_rows[1:2]
            shared = jnp.mean(pulled * unit, axis=1, keepdims=True)
            total = cots[batch, core].astype(F32) + scale * (pulled - unit * shared)
            attended[batch] = total
            cots[batch, core] = total.astype(BF16)
            for side in range(2):
                give_branch(batch, side).start()
            for copy in ends(batch):
                copy.start()
            return carry

        lax.fori_loop(0, 2, close, 0)
        for batch in range(2):
            for side in range(2):
                give_branch(batch, side).wait_recv()
                keep_branch(batch, side).start()
        for batch in range(2):
            save(last, batch, core).wait()
            for copy in ends(batch):
                copy.wait()
            for side in range(2):
                keep_branch(batch, side).wait()
                give_branch(batch, side).wait_send()
            for copy in lend(batch):
                copy.wait_send()

    pl.run_scoped(
        feed_forward,
        pltpu.VMEM((2, 2, 512, 1024), F32),
        pltpu.VMEM((2, 2, 512, 1024), F32),
        pltpu.VMEM((2, 512, WIDE), BF16),
    )
    give_w.wait_send()
    give_seg.wait_send()
    for batch in range(2):
        to_pair(7 + batch, rows_all.at[batch, core], rows_all.at[batch, core]).wait_send()
    give_tile.wait_send()
    give_cot.wait_send()
    gather.drain()


def forward_call(packed, tile, inputs, cotangent, segments, gains):
    rows = inputs.shape[1]
    counter = np.arange(128) % 32
    inverse = jnp.asarray(THETA ** (-2.0 * counter / 64), F32)[None]
    shapes = [
        ((2, 4, 2, 2, 64, WIDE), BF16),
        ((2, SEQ, 1024), BF16),
        ((2, SEQ, WIDE), BF16),
        ((2, SEQ, 1024), BF16),
        ((2, SEQ, 256), F32),
        ((2, SEQ, SEQ), BF16),
        ((2, SEQ, 128), F32),
        ((2, SEQ, 512), BF16),
        ((2, 2, rows, 1024), BF16),
        ((2, 2, rows, 1024), BF16),
        ((CHUNKS - 2, 2, 2, rows, WIDE), BF16),
        ((2, rows, 1024), BF16),
        ((2, 2, rows, 1024), BF16),
        ((2, rows, 1024), F32),
        ((8, 1024), F32),
    ]
    anywhere = pl.BlockSpec(memory_space=pl.ANY)
    inside = pl.BlockSpec(memory_space=pltpu.VMEM)
    return pl.pallas_call(
        forward_kernel,
        out_shape=[jax.ShapeDtypeStruct(*shape) for shape in shapes],
        in_specs=[anywhere] * 5 + [inside] * 2,
        out_specs=[anywhere] * len(shapes),
        scratch_shapes=[
            pltpu.VMEM((CHUNKS, 4, 2, 2, 64, WIDE), BF16),
            pltpu.VMEM((4, 2, 2, 2, 8, 128), F32),
            pltpu.VMEM((8, 1024), F32),
            pltpu.VMEM((2, 2, rows, 1024), BF16),
            pltpu.VMEM((2, 2, rows, 1024), BF16),
            pltpu.VMEM((2, 2, 1, rows), F32),
            pltpu.VMEM((2, SEQ, 512), BF16),
            pltpu.VMEM((2, rows, 512), BF16),
            pltpu.VMEM((4, 2, 2, 64, 512), BF16),
            pltpu.VMEM((2, rows, 1024), F32),
            pltpu.VMEM((2, 2, rows, 1024), BF16),
            pltpu.SemaphoreType.DMA((12,)),
            pltpu.SemaphoreType.DMA((18,)),
            pltpu.SemaphoreType.DMA((18,)),
        ]
        + semaphores(),
        compiler_params=params(0),
        name="forward",
    )(packed, tile, inputs, cotangent, segments.astype(F32)[:, None, :], gains, inverse)


def pack_halves(w_query, w_key, w_value, output_t, w_gate, w_up, down_t):
    rows = w_query.shape[0]
    halves = [jnp.stack(jnp.split(w, 2, axis=1)) for w in (w_query, w_key, w_value, output_t)]
    first = jnp.concatenate(halves[:2], axis=2)[:, None]
    second = jnp.concatenate(halves[2:], axis=2)[:, None]
    wide = jnp.concatenate(
        [w.reshape(rows, 2, CHUNKS - 2, 256).transpose(1, 2, 0, 3) for w in (w_gate, w_up, down_t)],
        axis=3,
    )
    return jnp.concatenate([first, second, wide], axis=1)


def pack_gains(attn_gain, ffn_gain):
    count = attn_gain.shape[0]
    slot = lax.axis_index("fsdp") % (128 // count)
    pair = jnp.stack([attn_gain, ffn_gain]).astype(F32)
    place_of = (jnp.arange(128 // count) == slot).astype(F32)
    spread = (place_of[None, :, None] * pair[:, None, :]).reshape(2, 128)
    return jnp.concatenate([spread, jnp.zeros((6, 128), F32)])


def backward_kernel(*refs):
    (
        w_in, normed_in, raw_in, qkv_in, table_in, mask_in, total_in, mix_in, ffn_in, cot_in,
        saved_in, branch_in, kept_in, x_in, gain_rows, head_gains,
    ) = refs[:16]
    grad_out, sums_out, head_out = refs[16:19]
    sums = refs[19]
    lands = (refs[20:24], refs[24:28], refs[28:32])
    (
        totals, pair_land, rows_all, cots, saved, branch, grads, qkv, raw, table, total, mask, mixed,
        grad_mixed, wo, keys, values, key_sum, value_sum, head_sum, head_land, kept,
        local, pair_sent, pair_landed, head_sent, head_landed, sent, landed,
    ) = refs[32:]
    me, z, y, x, core = place()
    greet(me, z, 16)
    mine, other = pair_rows(core)
    scatter = Scatter(sums, lands, totals, sent, landed)

    def to_pair(number, source, target):
        return pltpu.make_async_remote_copy(
            src_ref=source,
            dst_ref=target,
            send_sem=pair_sent.at[number],
            recv_sem=pair_landed.at[number],
            device_id=(me ^ 1,),
            device_id_type=MESH,
        )

    def load(number, source, target):
        return pltpu.make_async_copy(source, target, local.at[number])

    loads = [
        load(0, ffn_in, rows_all),
        load(1, cot_in, cots),
        load(2, saved_in.at[0], saved),
        load(3, branch_in, branch),
        load(4, w_in.at[1, :, :, pl.ds(256, 512)], wo),
        load(5, mix_in, mixed),
    ]
    for copy in loads:
        copy.start()
    head_sum[...] = jnp.zeros_like(head_sum)
    for copy in loads[:3]:
        copy.wait()

    def put(slot, columns, left, right):
        product = contract(left, right, 0, 0).astype(BF16)
        sums[slot, :, :, :, :, columns] = product.reshape(4, 2, 2, 64, columns.size)

    def wide_terms(chunk):
        slot = lax.rem(chunk, SUM_SLOTS)
        flat = saved[...].reshape(2048, WIDE)
        put(slot, pl.ds(0, 512), rows_all[...].reshape(2048, 1024), flat[:, 0:512])
        put(slot, pl.ds(512, 256), cots[...].reshape(2048, 1024), flat[:, 512:768])

    wide_terms(0)
    load(2, saved_in.at[1], saved).start()
    for copy in loads[3:]:
        copy.wait()

    def mixed_back(half, carry):
        product = contract(branch[half].reshape(1024, 1024), wo[...].reshape(1024, 512), 1, 0)
        grad_mixed[half] = product.astype(BF16)
        return carry

    def batch_loads(batch):
        return (
            load(6, qkv_in.at[batch], qkv),
            load(7, raw_in.at[batch], raw),
            load(8, table_in.at[batch], table),
            load(9, total_in.at[batch], total),
            load(10, mask_in.at[batch], mask),
        )

    def pull_back(grad, span, columns, gain, number):
        plain = raw[span, columns].astype(F32)
        width = plain.shape[1]
        row = lax.broadcasted_iota(jnp.int32, (width, width), 0) // 64
        column = lax.broadcasted_iota(jnp.int32, (width, width), 1) // 64
        ones = jnp.where(row == column, 1.0 / 64.0, 0.0).astype(BF16)
        level = lax.rsqrt(contract((plain * plain).astype(BF16), ones, 1, 0) + EPS)
        unit = plain * level
        turned = grad * table[span, 0:128] - half_turn(grad) * table[span, 128:256]
        terms = turned * unit
        head_sum[number] += jnp.sum(terms.reshape(-1, 8, width), axis=0)
        scaled = terms * gain
        shared = contract(scaled.astype(BF16), ones, 1, 0)
        return level * (turned * gain - unit * shared)

    def sides(pair, parity):
        low = lane_index(pair.shape) < 64
        rows = pair.astype(F32)
        first, second = jnp.where(low, rows, 0.0), jnp.where(low, 0.0, rows)
        if parity == 0:
            second = pltpu.roll(second, 64, 1)
        else:
            first = pltpu.roll(first, 64, 1)
        return first.astype(BF16), second.astype(BF16)

    def attend_back(batch, couple, parity):
        key_pair = qkv[:, pl.ds(pl.multiple_of(512 + couple * 128, 128), 128)].astype(F32)
        value_pair = qkv[:, pl.ds(pl.multiple_of(768 + couple * 128, 128), 128)].astype(F32)
        for target, pair in ((keys, key_pair), (values, value_pair)):
            low, high = split_pair(pair, parity)
            target[0] = low.astype(BF16)
            target[1] = high.astype(BF16)
        if parity == 0:
            key_sum[...] = jnp.zeros_like(key_sum)
            value_sum[...] = jnp.zeros_like(value_sum)
        group = couple * 2 + parity
        lane = lane_index((256, 128))
        for quarter in range(4):
            span = pl.ds(quarter * 256, 256)
            width = (quarter + 1) * 256
            allowed = mask[span, 0:width].astype(F32)
            queries = qkv[span, lanes_at(group, 128)]
            pulled = grad_mixed[batch, span, lanes_at(group, 128)]
            product = pulled.astype(F32) * mixed[batch, span, lanes_at(group, 128)].astype(F32)
            inverse = total[span, :]
            query_sides, pulled_sides = sides(queries, parity), sides(pulled, parity)
            grad_query = jnp.zeros((256, 128), F32)
            grad_key = jnp.zeros((width, 128), F32)
            grad_value = jnp.zeros((width, 128), F32)
            for side in range(2):
                inside = lane < 64 if side == 0 else lane >= 64
                center = jnp.sum(jnp.where(inside, product, 0.0), axis=1, keepdims=True)
                level = jnp.sum(jnp.where(lane == 2 * group + side, inverse, 0.0), axis=1, keepdims=True)
                near_keys, near_values = keys[side, 0:width, :], values[side, 0:width, :]
                scores = contract(queries, near_keys, 1, 1)
                probs = jnp.exp(scores) * (allowed * level)
                grad_probs = contract(pulled, near_values, 1, 1)
                grad_scores = (probs * (grad_probs - center)).astype(BF16)
                grad_query += contract(grad_scores, near_keys, 1, 0)
                grad_key += contract(grad_scores, query_sides[side], 0, 0)
                grad_value += contract(probs.astype(BF16), pulled_sides[side], 0, 0)
            key_sum[0:width, :] += grad_key
            value_sum[0:width, :] += grad_value
            grad_raw = pull_back(
                grad_query * 0.125, span, lanes_at(group, 128), head_gains[:, 0:128], 0
            )
            grads[batch, span, lanes_at(group, 128)] = grad_raw.astype(BF16)
        if parity == 1:
            whole = pl.ds(0, SEQ)
            columns = pl.ds(pl.multiple_of(512 + couple * 128, 128), 128)
            grad_raw = pull_back(key_sum[...], whole, columns, head_gains[:, 512:640], 1)
            grads[batch, :, columns] = grad_raw.astype(BF16)
            columns = pl.ds(pl.multiple_of(768 + couple * 128, 128), 128)
            grads[batch, :, columns] = value_sum[...].astype(BF16)

    def head_copy(step):
        bit = (1, 2, 4, 8, 16)[step]
        return pltpu.make_async_remote_copy(
            src_ref=head_sum,
            dst_ref=head_land.at[step],
            send_sem=head_sent.at[step],
            recv_sem=head_landed.at[step],
            device_id=(me ^ bit,),
            device_id_type=MESH,
        )

    def send_heads(step):
        if step > 0:
            head_copy(step - 1).wait()
            head_sum[...] += head_land[step - 1]
        if step < 5:
            head_copy(step).start()

    def near_normed(batch, half):
        part = grads[batch, pl.ds(pl.multiple_of(half * 512, 512), 512), :]
        first = contract(part[:, 0:768], saved[0].reshape(1024, WIDE), 1, 1)
        value_weights = saved[1].reshape(1024, WIDE)[:, 0:256]
        return first + contract(part[:, 768:1024], value_weights, 1, 1)

    def work(time):
        @pl.when(time == 0)
        def _():
            lax.fori_loop(0, 2, mixed_back, 0)

        @pl.when((time >= 1) & (time <= 8))
        def _():
            unit = time - 1
            batch, couple, parity = unit // 4, (unit // 2) % 2, unit % 2

            @pl.when(unit % 4 == 0)
            def _():
                for copy in batch_loads(batch):
                    copy.start()
                for copy in batch_loads(batch):
                    copy.wait()

            for each in range(2):

                @pl.when(parity == each)
                def _():
                    attend_back(batch, couple, each)

        for step in range(6):

            @pl.when(time == 9 + step)
            def _():
                send_heads(step)

        @pl.when(time == 10)
        def _():
            load(2, w_in, saved).wait()

            def lend(batch, carry):
                cots[0, batch] = near_normed(batch, 1 - core).astype(BF16)
                return carry

            lax.fori_loop(0, 2, lend, 0)
            to_pair(1, cots.at[0], pair_land).start()
            load(7, x_in, cots.at[1]).start()
            load(6, kept_in.at[0], kept).start()

        @pl.when(time == 11)
        def _():
            to_pair(1, cots.at[0], pair_land).wait()
            load(7, x_in, cots.at[1]).wait()

            def close(batch, carry):
                load(6, kept_in.at[batch], kept).wait()
                rows = cots[1, batch].astype(F32)
                scale = lax.rsqrt(jnp.mean(rows * rows, axis=1, keepdims=True) + EPS)
                unit = rows * scale
                pulled = near_normed(batch, core) + pair_land[batch].astype(F32)
                pulled = pulled * gain_rows[0:1]
                shared = jnp.mean(pulled * unit, axis=1, keepdims=True)
                grad = kept[...] + scale * (pulled - unit * shared)
                cots[0, batch] = grad.astype(BF16)

                @pl.when(batch == 0)
                def _():
                    load(6, kept_in.at[1], kept).start()

                return carry

            lax.fori_loop(0, 2, close, 0)
            load(7, cots.at[0], grad_out).start()

    def next_terms(time):
        @pl.when(time + 1 < CHUNKS - 2)
        def _():
            load(2, saved_in.at[0], saved).wait()
            wide_terms(time + 1)

        @pl.when(time + 2 < CHUNKS - 2)
        def _():
            load(2, saved_in.at[time + 2], saved).start()

        @pl.when(time == CHUNKS - 4)
        def _():
            load(0, normed_in, rows_all).start()
            load(2, w_in, saved).start()

        @pl.when(time == CHUNKS - 3)
        def _():
            load(0, normed_in, rows_all).wait()
            slot = (CHUNKS - 2) % SUM_SLOTS
            put(slot, pl.ds(0, 768), rows_all[...].reshape(2048, 1024), grads[:, :, 0:768].reshape(2048, 768))

        @pl.when(time == CHUNKS - 2)
        def _():
            slot = (CHUNKS - 1) % SUM_SLOTS
            put(slot, pl.ds(0, 256), rows_all[...].reshape(2048, 1024), grads[:, :, 768:1024].reshape(2048, 256))
            put(slot, pl.ds(256, 512), branch[...].reshape(2048, 1024), mixed[...].reshape(2048, 512))

    def body(time, carry):
        scatter.tick(time, (0,))
        work(time)
        scatter.tick(time, (1, 2))
        next_terms(time)
        return carry

    lax.fori_loop(0, CHUNKS + 5, body, 0)
    load(7, cots.at[0], grad_out).wait()

    def hand(half):
        return to_pair(0, totals.at[:, other, :], sums_out.at[half])

    own = load(0, totals.at[:, mine, :], sums_out.at[core])
    own.start()
    hand(core).start()
    head_store = load(1, head_sum, head_out)
    head_store.start()
    hand(core).wait_send()
    hand(1 - core).wait_recv()
    head_store.wait()
    own.wait()


def backward_call(forward, inputs, gains):
    rows = inputs.shape[1]
    (
        w, normed, raw, qkv, table, mask, total, mix, ffn, cot, saved, _, branch, kept, gain_rows,
    ) = forward
    anywhere = pl.BlockSpec(memory_space=pl.ANY)
    inside = pl.BlockSpec(memory_space=pltpu.VMEM)
    return pl.pallas_call(
        backward_kernel,
        out_shape=[
            jax.ShapeDtypeStruct((2, rows, 1024), BF16),
            jax.ShapeDtypeStruct((2, CHUNKS, 32, WIDE), F32),
            jax.ShapeDtypeStruct((2, 8, 128), F32),
        ],
        in_specs=[anywhere] * 14 + [inside] * 2,
        out_specs=[anywhere] * 3,
        scratch_shapes=[pltpu.VMEM((SUM_SLOTS, 4, 2, 2, 64, WIDE), BF16)]
        + land_shapes()
        + [
            pltpu.VMEM((CHUNKS, 64, WIDE), F32),
            pltpu.VMEM((2, rows, 1024), BF16),
            pltpu.VMEM((2, 2, rows, 1024), BF16),
            pltpu.VMEM((2, 2, rows, 1024), BF16),
            pltpu.VMEM((2, 2, rows, WIDE), BF16),
            pltpu.VMEM((2, 2, rows, 1024), BF16),
            pltpu.VMEM((2, SEQ, 1024), BF16),
            pltpu.VMEM((SEQ, 1024), BF16),
            pltpu.VMEM((SEQ, WIDE), BF16),
            pltpu.VMEM((SEQ, 256), F32),
            pltpu.VMEM((SEQ, 128), F32),
            pltpu.VMEM((SEQ, SEQ), BF16),
            pltpu.VMEM((2, SEQ, 512), BF16),
            pltpu.VMEM((2, SEQ, 512), BF16),
            pltpu.VMEM((2, 512, 512), BF16),
            pltpu.VMEM((2, SEQ, 128), BF16),
            pltpu.VMEM((2, SEQ, 128), BF16),
            pltpu.VMEM((SEQ, 128), F32),
            pltpu.VMEM((SEQ, 128), F32),
            pltpu.VMEM((2, 8, 128), F32),
            pltpu.VMEM((5, 2, 8, 128), F32),
            pltpu.VMEM((rows, 1024), F32),
            pltpu.SemaphoreType.DMA((11,)),
            pltpu.SemaphoreType.DMA((2,)),
            pltpu.SemaphoreType.DMA((2,)),
            pltpu.SemaphoreType.DMA((5,)),
            pltpu.SemaphoreType.DMA((5,)),
        ]
        + semaphores(),
        compiler_params=params(1),
        name="backward",
    )(
        w.reshape(2, 2, rows, WIDE), normed.reshape(2, 2, rows, 1024), raw, qkv, table, mask, total,
        mix, ffn, cot, saved, branch, kept, inputs, gain_rows, gains,
    )


def unpack(out):
    def both(chunk, start, stop):
        return jnp.concatenate([out[0, chunk, :, start:stop], out[1, chunk, :, start:stop]], axis=1)

    def wide_of(start):
        return out[:, 2:, :, start : start + 256].transpose(2, 0, 1, 3).reshape(out.shape[2], -1)

    return (
        both(0, 0, 512),
        both(0, 512, 768),
        both(1, 0, 256),
        both(1, 256, 768),
        wide_of(0),
        wide_of(256),
        wide_of(512),
    )


def gain_terms(packed, sums, attn_gain, ffn_gain):
    terms = packed.astype(F32) * sums
    blocks = jnp.sum(terms.reshape(*terms.shape[:-1], 3, 256), axis=(0, 4))
    attn = jnp.sum(blocks[0], axis=1) + blocks[1, :, 0]
    ffn = jnp.sum(blocks[2:, :, 0:2], axis=(0, 2))
    return attn / attn_gain.astype(F32), ffn / ffn_gain.astype(F32)


def local_grid(
    inputs,
    segments,
    attn_gain,
    w_query,
    key_projection,
    value_projection,
    w_output,
    query_gain,
    key_norm_gain,
    ffn_gain,
    w_gate,
    w_up,
    w_down,
    cotangent,
):
    packed = pack_halves(
        w_query, key_projection, value_projection, w_output.T, w_gate, w_up, w_down.T
    )
    gains = [query_gain] * 8 + [key_norm_gain] * 4
    gains = jnp.concatenate(gains).astype(F32)[None]
    forward = forward_call(
        packed, pack_gains(attn_gain, ffn_gain), inputs, cotangent, segments, gains
    )
    input_grad, sums, heads = backward_call(forward, inputs, gains)
    query, key, value, output_t, gate, up, down_t = unpack(sums)
    heads = jnp.sum(heads, axis=1)
    heads = heads[:, :64] + heads[:, 64:]
    attn_gain_grad, ffn_gain_grad = gain_terms(packed, sums, attn_gain, ffn_gain)
    return (
        forward[11],
        input_grad,
        attn_gain_grad,
        query,
        key,
        value,
        output_t.T,
        heads[0],
        heads[1],
        ffn_gain_grad,
        gate,
        up,
        down_t.T,
    )


def from_behind(block, axis, distance):
    devices = range(lax.axis_size(axis))
    route = [(i - distance, i) for i in devices if i - distance in devices]
    return lax.ppermute(block, axis, route)


def row_norm(values, gain_row):
    return values * lax.rsqrt(jnp.mean(values * values, axis=-1, keepdims=True) + EPS) * gain_row


def angles(places, head_width):
    counter = jnp.arange(head_width // 2, dtype=jnp.float32)
    inverse = jnp.power(jnp.float32(THETA), -2.0 * counter / head_width)
    turned = places.astype(jnp.float32)[:, None] * inverse[None, :]
    return (jnp.cos(turned), jnp.sin(turned))


def prepare_inputs(raw_rows, gain_row, cosine_table, sine_table_rows, head_count):
    token_count = raw_rows.shape[0]
    head_width = gain_row.shape[0]
    split_rows = raw_rows.reshape(token_count, head_count, head_width)
    normed = row_norm(split_rows, gain_row)
    first_half = normed[..., : head_width // 2]
    second = normed[..., head_width // 2 :]
    cos_rows = cosine_table[:, None, :]
    sin_rows = sine_table_rows[:, None, :]
    turned = jnp.concatenate(
        [first_half * cos_rows - second * sin_rows, second * cos_rows + first_half * sin_rows],
        axis=-1,
    )
    return turned.reshape(token_count, head_count * head_width)


def plain_product(left_rows, right_rows):
    return jnp.dot(left_rows, right_rows, preferred_element_type=jnp.float32)


def rows_product(left_rows, right_rows):
    return lax.dot_general(
        left_rows, right_rows, (((0,), (0,)), ((), ())), preferred_element_type=jnp.float32
    )


def cols_product(left_rows, right_rows):
    return lax.dot_general(
        left_rows, right_rows, (((1,), (1,)), ((), ())), preferred_element_type=jnp.float32
    )


def silu_product(gate_raw, upward):
    return gate_raw * jax.nn.sigmoid(gate_raw) * upward


def add_sets(former_set, latter_set):
    if former_set is None:
        return latter_set
    return tuple((former + latter for former, latter in zip(former_set, latter_set)))


def local(
    inputs,
    segments,
    attn_gain,
    w_query,
    key_projection,
    value_projection,
    w_output,
    query_gain,
    key_norm_gain,
    ffn_gain,
    w_gate,
    w_up,
    w_down,
    cotangent,
):
    batches = inputs.shape[0]
    tokens = inputs.shape[1]
    head_width = query_gain.shape[0]
    query_width = w_query.shape[1]
    kv_width = key_projection.shape[1]
    query_head_rows = query_width // head_width
    kv_heads = kv_width // head_width
    heads_per_group = query_head_rows // kv_heads
    scale = 1.0 / math.sqrt(head_width)
    query_gain_f = query_gain.astype(jnp.float32)
    key_gain_f = key_norm_gain.astype(jnp.float32)
    device_index = lax.axis_index("fsdp")
    places_row = jnp.arange(tokens, dtype=jnp.int32)
    causal = places_row[None, :] <= places_row[:, None]
    same_run = device_index * tokens // SEQ == (device_index - 1) * tokens // SEQ
    outputs_list = []
    grads_list = []
    shard_sums = None
    gain_sums = None
    for batch_index in range(batches):
        gathered = (
            lax.all_gather(attn_gain, "fsdp", axis=0, tiled=True),
            lax.all_gather(w_query, "fsdp", axis=0, tiled=True),
            lax.all_gather(key_projection, "fsdp", axis=0, tiled=True),
            lax.all_gather(value_projection, "fsdp", axis=0, tiled=True),
            lax.all_gather(w_output, "fsdp", axis=1, tiled=True),
            lax.all_gather(ffn_gain, "fsdp", axis=0, tiled=True),
            lax.all_gather(w_gate, "fsdp", axis=0, tiled=True),
            lax.all_gather(w_up, "fsdp", axis=0, tiled=True),
            lax.all_gather(w_down, "fsdp", axis=1, tiled=True),
        )
        (
            gain_attn,
            full_query,
            full_key,
            full_value,
            full_output,
            gain_ffn,
            full_gate,
            full_up,
            full_down,
        ) = gathered
        hidden = inputs[batch_index].astype(jnp.float32)
        segment = segments[batch_index]
        normed_f, norm_pull = jax.vjp(row_norm, hidden, gain_attn.astype(jnp.float32))
        normed = normed_f.astype(jnp.bfloat16)
        query_raw = plain_product(normed, full_query)
        key_projected = plain_product(normed, full_key)
        value_reduced = plain_product(normed, full_value).astype(jnp.bfloat16)
        lower_count = jnp.sum((segment[None, :] < segment[:, None]).astype(jnp.int32), axis=1)
        local_places = places_row - lower_count
        cos_local, sin_local = angles(local_places, head_width)
        key_sent = prepare_inputs(key_projected, key_gain_f, cos_local, sin_local, kv_heads).astype(
            jnp.bfloat16
        )
        remote_key, remote_value, remote_segment = from_behind(
            (key_sent, value_reduced, segment.astype(jnp.bfloat16)), "fsdp", 1
        )
        remote_match = (remote_segment.astype(jnp.int32)[None, :] == segment[:, None]) & same_run
        places_all = local_places + jnp.sum(remote_match.astype(jnp.int32), axis=1)
        cosine_table, sine_table_rows = angles(places_all, head_width)
        query_f, query_pull = jax.vjp(
            lambda raw_rows, gain_row: prepare_inputs(
                raw_rows, gain_row, cosine_table, sine_table_rows, query_head_rows
            ),
            query_raw,
            query_gain_f,
        )
        key_f, key_pull = jax.vjp(
            lambda raw_rows, gain_row: prepare_inputs(
                raw_rows, gain_row, cosine_table, sine_table_rows, kv_heads
            ),
            key_projected,
            key_gain_f,
        )
        query_low = query_f.astype(jnp.bfloat16)
        key_low = key_f.astype(jnp.bfloat16)
        allowed = jnp.concatenate(
            [remote_match, causal & (segment[None, :] == segment[:, None])], axis=1
        )
        query_split = query_low.reshape(tokens, kv_heads, heads_per_group, head_width).transpose(
            1, 0, 2, 3
        )
        key_split = (
            jnp.concatenate([remote_key, key_low], axis=0)
            .reshape(2 * tokens, kv_heads, head_width)
            .transpose(1, 0, 2)
        )
        value_split = (
            jnp.concatenate([remote_value, value_reduced], axis=0)
            .reshape(2 * tokens, kv_heads, head_width)
            .transpose(1, 0, 2)
        )

        def head_forward(blocks):
            query_part, key_part, value_part = blocks
            scores = (
                jnp.einsum("tgd,ld->gtl", query_part, key_part, preferred_element_type=jnp.float32)
                * scale
            )
            scores = jnp.where(allowed[None], scores, NEG)
            row_peak = jnp.max(scores, axis=-1, keepdims=True)
            raised = jnp.exp(scores - row_peak)
            row_total = jnp.sum(raised, axis=-1, keepdims=True)
            prob_rows = (raised / row_total).astype(jnp.bfloat16)
            mixed_part = jnp.einsum(
                "gtl,ld->tgd", prob_rows, value_part, preferred_element_type=jnp.float32
            )
            return (mixed_part.astype(jnp.bfloat16), (row_peak + jnp.log(row_total))[..., 0])

        mixed_split, log_totals = lax.map(head_forward, (query_split, key_split, value_split))
        attn_mix = mixed_split.transpose(1, 0, 2, 3).reshape(tokens, query_width)
        attended = hidden + plain_product(attn_mix, full_output)
        ffn_f, ffn_pull = jax.vjp(row_norm, attended, gain_ffn.astype(jnp.float32))
        ffn_in = ffn_f.astype(jnp.bfloat16)
        gate_raw = plain_product(ffn_in, full_gate)
        upward = plain_product(ffn_in, full_up)
        active_f, active_pull = jax.vjp(silu_product, gate_raw, upward)
        active = active_f.astype(jnp.bfloat16)
        result = attended + plain_product(active, full_down)
        outputs_list.append(result.astype(jnp.bfloat16))
        back_query, back_key, back_value, back_output, back_gate, back_up, back_down = (
            lax.all_gather(w_query, "fsdp", axis=0, tiled=True),
            lax.all_gather(key_projection, "fsdp", axis=0, tiled=True),
            lax.all_gather(value_projection, "fsdp", axis=0, tiled=True),
            lax.all_gather(w_output, "fsdp", axis=1, tiled=True),
            lax.all_gather(w_gate, "fsdp", axis=0, tiled=True),
            lax.all_gather(w_up, "fsdp", axis=0, tiled=True),
            lax.all_gather(w_down, "fsdp", axis=1, tiled=True),
        )
        grad_result = cotangent[batch_index]
        grad_down_t = rows_product(grad_result, active)
        grad_active = cols_product(grad_result, back_down)
        grad_gate_f, grad_up_f = active_pull(grad_active)
        grad_gate_low = grad_gate_f.astype(jnp.bfloat16)
        grad_up_low = grad_up_f.astype(jnp.bfloat16)
        grad_gate_w = rows_product(ffn_in, grad_gate_low)
        grad_up_w = rows_product(ffn_in, grad_up_low)
        grad_ffn_in = cols_product(grad_gate_low, back_gate) + cols_product(grad_up_low, back_up)
        grad_attended_norm, grad_ffn_gain = ffn_pull(grad_ffn_in)
        grad_attended = grad_result.astype(jnp.float32) + grad_attended_norm
        grad_branch = grad_attended.astype(jnp.bfloat16)
        grad_output_t = rows_product(grad_branch, attn_mix)
        grad_mixed = cols_product(grad_branch, back_output).astype(jnp.bfloat16)
        grad_split = grad_mixed.reshape(tokens, kv_heads, heads_per_group, head_width).transpose(
            1, 0, 2, 3
        )

        def head_backward(blocks):
            query_part, key_part, value_part, grad_part, log_part = blocks
            scores = (
                jnp.einsum("tgd,ld->gtl", query_part, key_part, preferred_element_type=jnp.float32)
                * scale
            )
            scores = jnp.where(allowed[None], scores, NEG)
            prob_rows = jnp.exp(scores - log_part[..., None])
            grad_probs = jnp.einsum(
                "tgd,ld->gtl", grad_part, value_part, preferred_element_type=jnp.float32
            )
            center = jnp.sum(prob_rows * grad_probs, axis=-1, keepdims=True)
            grad_scores = (prob_rows * (grad_probs - center)).astype(jnp.bfloat16)
            grad_query_part = (
                jnp.einsum("gtl,ld->tgd", grad_scores, key_part, preferred_element_type=jnp.float32)
                * scale
            )
            grad_key_part = (
                jnp.einsum(
                    "gtl,tgd->ld", grad_scores, query_part, preferred_element_type=jnp.float32
                )
                * scale
            )
            grad_value_part = jnp.einsum(
                "gtl,tgd->ld",
                prob_rows.astype(jnp.bfloat16),
                grad_part,
                preferred_element_type=jnp.float32,
            )
            return (grad_query_part, grad_key_part, grad_value_part)

        grad_query_split, grad_key_split, grad_value_split = lax.map(
            head_backward, (query_split, key_split, value_split, grad_split, log_totals)
        )
        grad_query_rot = grad_query_split.transpose(1, 0, 2, 3).reshape(tokens, query_width)
        grad_key_all = grad_key_split.transpose(1, 0, 2).reshape(2 * tokens, kv_width)
        grad_value_all = grad_value_split.transpose(1, 0, 2).reshape(2 * tokens, kv_width)
        back_key_grad, back_value_grad = (
            from_behind(grad_key_all[:tokens].astype(jnp.bfloat16), "fsdp", -1).astype(jnp.float32),
            from_behind(grad_value_all[:tokens].astype(jnp.bfloat16), "fsdp", -1).astype(
                jnp.float32
            ),
        )
        grad_key_rot = grad_key_all[tokens:] + back_key_grad
        grad_value_low = (grad_value_all[tokens:] + back_value_grad).astype(jnp.bfloat16)
        grad_query_raw, grad_query_gain = query_pull(grad_query_rot)
        grad_key_raw, grad_key_gain = key_pull(grad_key_rot)
        grad_query_low = grad_query_raw.astype(jnp.bfloat16)
        grad_key_low = grad_key_raw.astype(jnp.bfloat16)
        grad_query_w = rows_product(normed, grad_query_low)
        grad_key_w = rows_product(normed, grad_key_low)
        grad_value_w = rows_product(normed, grad_value_low)
        grad_normed = (
            cols_product(grad_query_low, back_query)
            + cols_product(grad_key_low, back_key)
            + cols_product(grad_value_low, back_value)
        )
        grad_hidden_norm, grad_attn_gain = norm_pull(grad_normed)
        grads_list.append((grad_attended + grad_hidden_norm).astype(jnp.bfloat16))
        gain_sums = add_sets(gain_sums, (grad_query_gain, grad_key_gain))
        shard_terms = (
            lax.psum_scatter(grad_attn_gain, "fsdp", scatter_dimension=0, tiled=True),
            lax.psum_scatter(grad_query_w, "fsdp", scatter_dimension=0, tiled=True),
            lax.psum_scatter(grad_key_w, "fsdp", scatter_dimension=0, tiled=True),
            lax.psum_scatter(grad_value_w, "fsdp", scatter_dimension=0, tiled=True),
            lax.psum_scatter(grad_output_t, "fsdp", scatter_dimension=0, tiled=True),
            lax.psum_scatter(grad_ffn_gain, "fsdp", scatter_dimension=0, tiled=True),
            lax.psum_scatter(grad_gate_w, "fsdp", scatter_dimension=0, tiled=True),
            lax.psum_scatter(grad_up_w, "fsdp", scatter_dimension=0, tiled=True),
            lax.psum_scatter(grad_down_t, "fsdp", scatter_dimension=0, tiled=True),
        )
        shard_sums = add_sets(shard_sums, shard_terms)
    head_sums = lax.psum((gain_sums[0], gain_sums[1]), "fsdp")
    return (
        jnp.stack(outputs_list),
        jnp.stack(grads_list),
        shard_sums[0],
        shard_sums[1],
        shard_sums[2],
        shard_sums[3],
        shard_sums[4].T,
        head_sums[0],
        head_sums[1],
        shard_sums[5],
        shard_sums[6],
        shard_sums[7],
        shard_sums[8].T,
    )


def solution(mesh):
    return jax.shard_map(
        local_grid if mesh.shape["fsdp"] == 32 else local,
        mesh=mesh,
        in_specs=(
            P(None, "fsdp", None),
            P(None, "fsdp"),
            P("fsdp"),
            P("fsdp", None),
            P("fsdp", None),
            P("fsdp", None),
            P(None, "fsdp"),
            P(),
            P(),
            P("fsdp"),
            P("fsdp", None),
            P("fsdp", None),
            P(None, "fsdp"),
            P(None, "fsdp", None),
        ),
        out_specs=(
            P(None, "fsdp", None),
            P(None, "fsdp", None),
            P("fsdp"),
            P("fsdp", None),
            P("fsdp", None),
            P("fsdp", None),
            P(None, "fsdp"),
            P(),
            P(),
            P("fsdp"),
            P("fsdp", None),
            P("fsdp", None),
            P(None, "fsdp"),
        ),
        check_vma=False,
    )
```

```python
import math

import jax
import jax.numpy as jnp
import numpy as np
from jax import lax
from jax.experimental import pallas as pl
from jax.experimental.pallas import tpu as pltpu
from jax.sharding import PartitionSpec as P

SEQ = 1024


EPS = 1e-05
THETA = 1000000.0
NEG = -1e30


CHUNKS = 11
WIDE = 768
MESH = pl.DeviceIdType.MESH
ALL = slice(None)
F32 = jnp.float32
BF16 = jnp.bfloat16
PARTS = (
    ("A", pl.ds(0, 48), pl.ds(0, 384)),
    ("B", pl.ds(0, 48), pl.ds(384, 384)),
    ("C", pl.ds(48, 16), pl.ds(0, 768)),
)
GAINS = len(PARTS)
OUTWARD = {
    "A": ("z0", "z1", "z2", "y", "x"),
    "B": ("z0", "z1", "z2", "x", "y"),
    "C": ("x", "y", "z0", "z1", "z2"),
}
INWARD = {
    "A": ("x", "y", "z0", "z1", "z2"),
    "B": ("y", "x", "z0", "z1", "z2"),
    "C": ("z0", "z1", "z2", "y", "x"),
}
SUM_SLOTS = 6
HELD = 2
LAND_SLOTS = 3


def place():
    me = lax.axis_index("fsdp")
    return me, me // 8, (me // 4) % 2, (me // 2) % 2, me % 2


def guarded(condition, action):
    if condition is None:
        action()
    else:
        pl.when(condition)(action)


def greet(me, z, far=0):
    gate = pltpu.get_barrier_semaphore()
    for bit in (1, 2, 4):
        pl.semaphore_signal(gate, inc=1, device_id=(me ^ bit,), device_id_type=MESH)

    @pl.when(z > 0)
    def _():
        pl.semaphore_signal(gate, inc=1, device_id=(me - 8,), device_id_type=MESH)

    @pl.when(z < 3)
    def _():
        pl.semaphore_signal(gate, inc=1, device_id=(me + 8,), device_id_type=MESH)

    if far:
        pl.semaphore_signal(gate, inc=1, device_id=(me ^ far,), device_id_type=MESH)
    pl.semaphore_wait(gate, (4 if far else 3) + (z > 0).astype(jnp.int32) + (z < 3).astype(jnp.int32))


class Gather:
    def __init__(self, full, tiles, sent, landed):
        self.full, self.tiles, self.sent, self.landed = full, tiles, sent, landed
        self.me, self.z, self.y, self.x, self.core = place()

    def moves(self, part, step, chunk):
        kind, rows, columns = PARTS[0] if part == GAINS else PARTS[part]
        z, y, x, me = self.z, self.y, self.x, self.me

        def view(zz, yy, xx):
            if part == GAINS:
                return self.tiles.at[zz, yy, xx]
            return self.full.at[chunk, zz, yy, xx, rows, columns]

        axis = OUTWARD[kind][step]
        if axis[0] == "z":
            far = int(axis[1])
            yy, xx = (ALL, ALL) if kind == "C" else (y, x)
            return (
                ((z >= far) & (z < 3), z - far, me + 8, z >= far + 1, z - 1 - far),
                ((z <= 3 - far) & (z > 0), z + far, me - 8, z <= 2 - far, z + 1 + far),
            ), lambda zz: view(zz, yy, xx)
        zz = z if kind == "C" else ALL
        if axis == "y":
            xx = x if kind == "A" else ALL
            return ((None, y, me ^ 4, None, 1 - y),), lambda yy: view(zz, yy, xx)
        yy = ALL if kind == "A" else y
        return ((None, x, me ^ 2, None, 1 - x),), lambda xx: view(zz, yy, xx)

    def copy(self, ref, device, part, step, chunk, way):
        return pltpu.make_async_remote_copy(
            src_ref=ref,
            dst_ref=ref,
            send_sem=self.sent.at[chunk, part, step, way],
            recv_sem=self.landed.at[chunk, part, step, way],
            device_id=(device,),
            device_id_type=MESH,
        )

    def send(self, part, step, chunk):
        moves, view = self.moves(part, step, chunk)
        for way, (sends, mine, device, _, _) in enumerate(moves):
            guarded(
                sends,
                lambda: self.copy(view(mine), device, part, step, chunk, way).start(),
            )

    def receive(self, part, step, chunk):
        moves, view = self.moves(part, step, chunk)
        for way, (_, _, _, receives, other) in enumerate(moves):
            guarded(
                receives,
                lambda: self.copy(view(other), self.me ^ 2, part, step, chunk, way).wait_recv(),
            )

    def finish(self, part, step, chunk):
        moves, view = self.moves(part, step, chunk)
        for way, (sends, mine, device, _, _) in enumerate(moves):
            guarded(
                sends,
                lambda: self.copy(view(mine), device, part, step, chunk, way).wait_send(),
            )

    def tick(self, time, parts):
        for step in range(6):
            age = time - step
            chunk = jnp.where(age < 2, age, age - HELD)

            @pl.when((age >= 0) & (chunk < CHUNKS) & ((age < 2) | (chunk >= 2)))
            def _():
                for part in parts:
                    if step > 0:
                        self.receive(part, step - 1, chunk)
                    if step < 5:
                        self.send(part, step, chunk)

    def tick_gains(self, step):
        if step > 0:
            self.receive(GAINS, step - 1, 0)
        if step < 5:
            self.send(GAINS, step, 0)

    def drain(self):
        def body(chunk, carry):
            for part in range(len(PARTS)):
                for step in range(5):
                    self.finish(part, step, chunk)
            return carry

        lax.fori_loop(0, CHUNKS, body, 0)
        for step in range(5):
            self.finish(GAINS, step, 0)


class Scatter:
    def __init__(self, sums, lands, totals, sent, landed):
        self.sums, self.lands, self.totals = sums, lands, totals
        self.sent, self.landed = sent, landed
        self.me, self.z, self.y, self.x, self.core = place()

    def moves(self, part, step, chunk):
        kind, rows, columns = PARTS[part]
        z, y, x, me = self.z, self.y, self.x, self.me
        slot, land = lax.rem(chunk, SUM_SLOTS), lax.rem(chunk, LAND_SLOTS)
        first, second, up, down = self.lands[part]
        axis = INWARD[kind][step]

        def view(zz, yy, xx):
            return self.sums.at[slot, zz, yy, xx, rows, columns]

        if axis[0] == "z":
            far = int(axis[1])
            count = 3 - far
            yy, xx = (ALL, ALL) if kind == "C" else (y, x)
            above, below = pl.ds(far + 1, count), pl.ds(0, count)
            up_land, down_land = up.at[land, pl.ds(far, count)], down.at[land, pl.ds(0, count)]
            return (
                (z == far, view(above, yy, xx), up_land, me + 8, z == far + 1, view(above, yy, xx)),
                (z == 3 - far, view(below, yy, xx), down_land, me - 8, z == 2 - far, view(below, yy, xx)),
            )
        zz = z if kind == "C" else ALL
        ref = (first if step == 0 or (kind == "C" and step == 3) else second).at[land]
        if axis == "x":
            yy = ALL if kind == "A" else y
            return ((None, view(zz, yy, 1 - x), ref, me ^ 2, None, view(zz, yy, x)),)
        xx = x if kind == "A" else ALL
        return ((None, view(zz, 1 - y, xx), ref, me ^ 4, None, view(zz, y, xx)),)

    def copy(self, source, target, device, part, step, chunk, way):
        return pltpu.make_async_remote_copy(
            src_ref=source,
            dst_ref=target,
            send_sem=self.sent.at[chunk, part, step, way],
            recv_sem=self.landed.at[chunk, part, step, way],
            device_id=(device,),
            device_id_type=MESH,
        )

    def step(self, part, step, chunk):
        if step > 0:
            for way, move in enumerate(self.moves(part, step - 1, chunk)):
                sends, source, land, device, receives, target = move

                def add():
                    self.copy(land, land, self.me ^ 2, part, step - 1, chunk, way).wait_recv()
                    target[...] = (target[...].astype(F32) + land[...].astype(F32)).astype(BF16)

                guarded(receives, add)
                guarded(
                    sends,
                    lambda: self.copy(source, land, device, part, step - 1, chunk, way).wait_send(),
                )
        if step < 5:
            for way, move in enumerate(self.moves(part, step, chunk)):
                sends, source, land, device, _, _ = move
                guarded(
                    sends,
                    lambda: self.copy(source, land, device, part, step, chunk, way).start(),
                )
        else:
            _, rows, columns = PARTS[part]
            slot = lax.rem(chunk, SUM_SLOTS)
            self.totals[lax.rem(chunk + 2, CHUNKS), rows, columns] = self.sums[
                slot, self.z, self.y, self.x, rows, columns
            ].astype(F32)

    def tick(self, time, parts):
        for step in range(5, -1, -1):
            chunk = time - step

            @pl.when((chunk >= 0) & (chunk < CHUNKS))
            def _():
                for part in parts:
                    self.step(part, step, chunk)


def pair_rows(core):
    mine = pl.ds(pl.multiple_of(core * 32, 32), 32)
    other = pl.ds(pl.multiple_of((1 - core) * 32, 32), 32)
    return mine, other


def semaphores():
    return [pltpu.SemaphoreType.DMA((CHUNKS, len(PARTS) + 1, 5, 2))] * 2


def land_shapes():
    slots = LAND_SLOTS
    plain = [(slots, 4, 2, 48, 384), (slots, 4, 48, 384), (slots, 3, 48, 384), (slots, 3, 48, 384)]
    late = [(slots, 2, 16, 768), (slots, 16, 768), (slots, 3, 2, 2, 16, 768), (slots, 3, 2, 2, 16, 768)]
    return [pltpu.VMEM(shape, BF16) for shape in plain + plain + late]


def params(number):
    return pltpu.CompilerParams(
        collective_id=number, has_side_effects=True, vmem_limit_bytes=62 * 2**20
    )


EAGER = 7
SPREAD = 3
LATER = CHUNKS + 5 + HELD - EAGER - SPREAD


def contract(left, right, left_dim, right_dim):
    return lax.dot_general(
        left, right, (((left_dim,), (right_dim,)), ((), ())), preferred_element_type=F32
    )


def lane_index(shape):
    return lax.broadcasted_iota(jnp.int32, shape, 1)


def half_turn(rows):
    width = rows.shape[1]
    first = lane_index(rows.shape) % 64 < 32
    return jnp.where(first, pltpu.roll(rows, width - 32, 1), pltpu.roll(rows, 32, 1))


def head_means(rows, ones):
    parts = [
        contract(rows[:, k : k + 256].astype(BF16), ones, 1, 0)
        for k in range(0, rows.shape[1], 256)
    ]
    return jnp.concatenate(parts, axis=1)


def head_ones():
    row = lax.broadcasted_iota(jnp.int32, (256, 256), 0) // 64
    column = lax.broadcasted_iota(jnp.int32, (256, 256), 1) // 64
    return jnp.where(row == column, 1.0 / 64.0, 0.0).astype(BF16)


def tiled(table, copies):
    return jnp.concatenate([table] * copies, axis=1)


def split_pair(rows, group):
    pair = rows[:, 128 * (group // 2) : 128 * (group // 2) + 128]
    low = lane_index(pair.shape) < 64
    if group % 2 == 0:
        kept = jnp.where(low, pair, 0.0)
        return kept, pltpu.roll(kept, 64, 1)
    kept = jnp.where(low, 0.0, pair)
    return pltpu.roll(kept, 64, 1), kept


def lanes_at(block, width):
    return pl.ds(pl.multiple_of(block * width, width), width)


def forward_kernel(*refs):
    packed, tile_in, x_in, cot_in, seg_in, gains, inverse = refs[:7]
    (
        w_out, normed_out, raw_out, qkv_out, table_out, mask_out, total_out, mix_out,
        ffn_out, cot_out, saved_out, result_out, branch_out, kept_out, gain_out,
    ) = refs[7:22]
    (
        full, tiles, gain_rows, rows_all, cots, seg_rows, mixed, mixed_pair, wo_pair, attended,
        lent, local, pair_sent, pair_landed, sent, landed,
    ) = refs[22:]
    me, z, y, x, core = place()
    pair = (me ^ 1,)
    greet(me, z)
    mine, other = pair_rows(core)

    def to_pair(number, source, target):
        return pltpu.make_async_remote_copy(
            src_ref=source,
            dst_ref=target,
            send_sem=pair_sent.at[number],
            recv_sem=pair_landed.at[number],
            device_id=pair,
            device_id_type=MESH,
        )

    def keep(number, source, target):
        return pltpu.make_async_copy(source, target, local.at[number])

    own_w = keep(0, packed.at[core], full.at[:, z, y, x, mine, :])
    own_x = keep(1, x_in, rows_all.at[:, core])
    own_cot = keep(2, cot_in, cots.at[:, core])
    own_seg = keep(3, seg_in, seg_rows.at[core])
    give_w = to_pair(0, packed.at[1 - core], full.at[:, z, y, x, mine, :])
    take_w = to_pair(0, packed.at[1 - core], full.at[:, z, y, x, other, :])
    give_x = to_pair(1, x_in, rows_all.at[:, core])
    take_x = to_pair(1, x_in, rows_all.at[:, 1 - core])
    give_cot = to_pair(2, cot_in, cots.at[:, core])
    take_cot = to_pair(2, cot_in, cots.at[:, 1 - core])
    give_seg = to_pair(3, seg_in, seg_rows.at[core])
    take_seg = to_pair(3, seg_in, seg_rows.at[1 - core])
    own_tile = keep(4, tile_in, tiles.at[z, y, x, core])
    give_tile = to_pair(9, tile_in, tiles.at[z, y, x, core])
    own_tile.start()
    give_tile.start()
    own_w.start()
    give_w.start()
    own_seg.start()
    give_seg.start()
    own_x.start()
    give_x.start()
    own_cot.start()
    give_cot.start()
    own_w.wait()
    take_w.wait_recv()
    own_tile.wait()
    to_pair(9, tile_in, tiles.at[z, y, x, 1 - core]).wait_recv()
    gather = Gather(full, tiles, sent, landed)
    give_wo = to_pair(4, full.at[1, :, :, :, :, pl.ds(256, 512)], wo_pair)
    keep_w = keep(0, full.at[pl.ds(0, 2)], w_out)
    keep_gain = keep(11, gain_rows, gain_out)
    keep_cot = keep(2, cots, cot_out)
    def attention(normed, raw, qkv, table, mask, mask_turned, total, total_turned, keys, values):
        def early_copies(batch):
            return (
                keep(4, normed, normed_out.at[batch]),
                keep(5, raw, raw_out.at[batch]),
                keep(6, qkv, qkv_out.at[batch]),
                keep(7, table.at[batch], table_out.at[batch]),
                keep(8, mask_turned.at[batch], mask_out.at[batch]),
            )

        def late_copies(batch):
            return (
                keep(9, total_turned, total_out.at[batch]),
                keep(10, mixed.at[batch], mix_out.at[batch]),
            )

        def prepare(batch):
            segment = jnp.concatenate([seg_rows[0, batch], seg_rows[1, batch]], axis=1)
            column = jnp.broadcast_to(segment, (128, SEQ)).T
            below = jnp.zeros((SEQ, 128), F32)
            for k in range(0, SEQ, 128):
                below += (segment[:, k : k + 128] < column).astype(F32)
            before = jnp.sum(below, axis=1, keepdims=True)
            spot = lax.broadcasted_iota(jnp.int32, (SEQ, 128), 0).astype(F32) - before
            angle = spot * inverse[...]
            sine = jnp.sin(angle)
            first = lane_index((SEQ, 128)) % 64 < 32
            table[batch, :, 0:128] = jnp.cos(angle)
            table[batch, :, 128:256] = jnp.where(first, -sine, sine)
            for quarter in range(4):
                span = pl.ds(quarter * 256, 256)
                width = (quarter + 1) * 256
                same = segment[:, :width] == column[quarter * 256 : quarter * 256 + 256, 0:1]
                spots = lax.broadcasted_iota(jnp.int32, (256, width), 0) + quarter * 256
                behind = lane_index((256, width)) <= spots
                mask[batch, span, 0:width] = jnp.where(same & behind, 1.0, 0.0).astype(BF16)
                first_key = quarter * 256
                same = segment[:, first_key:] == column[first_key : first_key + 256, 0:1]
                spots = lax.broadcasted_iota(jnp.int32, same.shape, 0)
                behind = spots <= lane_index(same.shape)
                turned = jnp.where(same & behind, 1.0, 0.0).astype(BF16)
                mask_turned[batch, span, first_key:] = turned

        def project(batch):
            total[...] = jnp.zeros_like(total)
            ones = head_ones()

            def value_block(half, carry):
                span = pl.ds(pl.multiple_of(half * 512, 512), 512)
                value_weights = full[1, :, :, :, :, 0:256].reshape(1024, 256)
                value = contract(normed[span, :], value_weights, 1, 0).astype(BF16)
                qkv[span, 768:1024] = value
                value = value.astype(F32)
                for group in range(4):
                    low, high = split_pair(value, group)
                    values[group, 0, span, :] = low.astype(BF16)
                    values[group, 1, span, :] = high.astype(BF16)
                return carry

            def block(half, carry):
                span = pl.ds(pl.multiple_of(half * 512, 512), 512)
                rows = rows_all[batch, half].astype(F32)
                scale = lax.rsqrt(jnp.mean(rows * rows, axis=1, keepdims=True) + EPS)
                unit = (rows * scale * gain_rows[0:1]).astype(BF16)
                normed[span, :] = unit
                weights = full[0].reshape(1024, WIDE)
                product = contract(unit, weights, 1, 0)
                raw[span, :] = product.astype(BF16)
                level = lax.rsqrt(head_means(product * product, ones) + EPS)
                turned = product * level * gains[...]
                cosine = tiled(table[batch, span, 0:128], 6)
                sine_signed = tiled(table[batch, span, 128:256], 6)
                turned = turned * cosine + half_turn(turned) * sine_signed
                query = turned[:, 0:512] * 0.125
                key = turned[:, 512:768].astype(BF16).astype(F32)
                qkv[span, 0:512] = query.astype(BF16)
                qkv[span, 512:768] = key.astype(BF16)
                for group in range(4):
                    low, high = split_pair(key, group)
                    keys[group, 0, span, :] = low.astype(BF16)
                    keys[group, 1, span, :] = high.astype(BF16)
                return carry

            lax.fori_loop(0, 2, block, 0)

            @pl.when(batch == 0)
            def _():
                gather.tick(EAGER - 1, (0, 1, 2))
                give_wo.start()
                keep_w.start()

            lax.fori_loop(0, 2, value_block, 0)

        def attend(batch, quarter):
            span = pl.ds(quarter * 256, 256)
            width = (quarter + 1) * 256
            allowed = mask[batch, span, 0:width].astype(F32)
            lane = lane_index((256, 128))

            def group_step(group, carry):
                queries = qkv[span, lanes_at(group, 128)]
                parts, sums = [], []
                for side in range(2):
                    scores = contract(queries, keys[group, side, 0:width, :], 1, 1)
                    raised = jnp.exp(scores) * allowed
                    sums.append(1.0 / jnp.sum(raised, axis=1, keepdims=True))
                    parts.append(
                        contract(raised.astype(BF16), values[group, side, 0:width, :], 1, 0)
                    )
                result = (parts[0] + parts[1]) * jnp.where(lane < 64, sums[0], sums[1])
                mixed[batch, span, lanes_at(group, 128)] = result.astype(BF16)
                old = total[span, :]
                old = jnp.where(lane == 2 * group, sums[0], old)
                total[span, :] = jnp.where(lane == 2 * group + 1, sums[1], old)
                return carry

            lax.fori_loop(0, 4, group_step, 0)

        def piece(number, carry):
            batch, part = number // 4, number % 4

            @pl.when(part == 0)
            def _():
                @pl.when(batch > 0)
                def _():
                    for copy in early_copies(0) + late_copies(0):
                        copy.wait()

                project(batch)
                for copy in early_copies(batch):
                    copy.start()

            for turn in range(2):

                @pl.when((number % 2 == turn) & (number < 2 * SPREAD))
                def _():
                    gather.tick(EAGER + number // 2, ((0,), (1, 2))[turn])

            for quarter in range(4):

                @pl.when(part == quarter)
                def _():
                    attend(batch, quarter)

            @pl.when(part == 3)
            def _():
                total_turned[...] = total[...].T[0:8, :]
                for copy in late_copies(batch):
                    copy.start()
                to_pair(5 + batch, mixed.at[batch, lanes_at(1 - core, 512), :], mixed_pair.at[batch]).start()

            return carry

        own_seg.wait()
        take_seg.wait_recv()
        def early(time, carry):
            for step in range(6):

                @pl.when(time == step)
                def _():
                    gather.tick_gains(step)

            gather.tick(time, (0, 1, 2))
            for batch in range(2):

                @pl.when(time == 1 + 2 * batch)
                def _():
                    prepare(batch)

            return carry

        lax.fori_loop(0, EAGER - 1, early, 0)
        for block in range(8):
            quad = tiles[block // 2, block % 2]
            quad = quad[0, 0] + quad[0, 1] + quad[1, 0] + quad[1, 1]
            gain_rows[:, 128 * block : 128 * block + 128] = quad
        keep_gain.start()
        own_x.wait()
        own_cot.wait()
        take_x.wait_recv()
        take_cot.wait_recv()
        keep_cot.start()
        lax.fori_loop(0, 8, piece, 0)
        for copy in early_copies(1) + late_copies(1):
            copy.wait()

    pl.run_scoped(
        attention,
        pltpu.VMEM((SEQ, 1024), BF16),
        pltpu.VMEM((SEQ, WIDE), BF16),
        pltpu.VMEM((SEQ, 1024), BF16),
        pltpu.VMEM((2, SEQ, 256), F32),
        pltpu.VMEM((2, SEQ, SEQ), BF16),
        pltpu.VMEM((2, SEQ, SEQ), BF16),
        pltpu.VMEM((SEQ, 128), F32),
        pltpu.VMEM((8, SEQ), F32),
        pltpu.VMEM((4, 2, SEQ, 128), BF16),
        pltpu.VMEM((4, 2, SEQ, 128), BF16),
    )
    give_wo.wait_send()
    give_wo.wait_recv()
    give_x.wait_send()

    def swap_mixed(batch):
        return to_pair(5 + batch, mixed.at[batch, lanes_at(1 - core, 512), :], mixed_pair.at[batch])

    def join(batch, carry):
        swap_mixed(batch).wait_recv()
        span = lanes_at(core, 512)
        own_wo = full[1, :, :, :, :, 256:768].reshape(1024, 512)
        result = rows_all[batch, core].astype(F32)
        result += contract(mixed[batch, span, :], own_wo, 1, 1)
        result += contract(mixed_pair[batch], wo_pair[...].reshape(1024, 512), 1, 1)
        attended[batch] = result
        scale = lax.rsqrt(jnp.mean(result * result, axis=1, keepdims=True) + EPS)
        rows_all[batch, core] = (result * scale * gain_rows[1:2]).astype(BF16)
        to_pair(7 + batch, rows_all.at[batch, core], rows_all.at[batch, core]).start()
        return carry

    lax.fori_loop(0, 2, join, 0)
    keep_ffn = keep(3, rows_all, ffn_out)

    def feed_forward(result, back, saved):
        last = CHUNKS - 3

        def save(chunk, batch, half):
            return keep(4 + batch, saved.at[batch], saved_out.at[chunk, batch, half])

        def lend(batch):
            return (
                to_pair(10 + batch, cots.at[batch, 1 - core], lent.at[0, batch]),
                to_pair(12 + batch, rows_all.at[batch, 1 - core], lent.at[1, batch]),
            )

        result[...] = jnp.zeros_like(result)
        back[...] = jnp.zeros_like(back)

        def chunk_step(chunk, carry):
            def block(part, inner):
                batch = part % 2
                own = (part < 2) != (chunk == last)
                half = jnp.where(own, core, 1 - core)
                for turn in range(2):

                    @pl.when((part == 2 * turn) & (chunk < LATER))
                    def _():
                        gather.tick(EAGER + SPREAD + chunk, ((0,), (1, 2))[turn])

                @pl.when((chunk == 0) & (part >= 2))
                def _():
                    to_pair(
                        7 + batch, rows_all.at[batch, core], rows_all.at[batch, 1 - core]
                    ).wait_recv()

                @pl.when((chunk == 1) & (part == 0))
                def _():
                    keep_ffn.start()

                @pl.when((chunk == last) & (part == 0))
                def _():
                    keep_w.wait()
                    keep_gain.wait()
                    for each in range(2):
                        swap_mixed(each).wait_send()
                    keep_ffn.wait()
                    keep_cot.wait()

                @pl.when((chunk > 0) | (part > 1))
                def _():
                    save(chunk, batch, half).wait()

                up_weights = full[chunk + 2, :, :, :, :, 0:512].reshape(1024, 512)
                down_weights = full[chunk + 2, :, :, :, :, 512:768].reshape(1024, 256)
                for piece in range(2):
                    rows = pl.ds(256 * piece, 256)
                    both = contract(rows_all[batch, half, rows, :], up_weights, 1, 0)
                    grad = contract(cots[batch, half, rows, :], down_weights, 1, 0)
                    gate, up = both[:, 0:256], both[:, 256:512]
                    bend = 1.0 / (1.0 + jnp.exp(-gate))
                    silu = gate * bend
                    active = (silu * up).astype(BF16)
                    grad_up = (grad * silu).astype(BF16)
                    grad_gate = (grad * up * bend * (1.0 + gate * (1.0 - bend))).astype(BF16)
                    saved[batch, rows, 0:256] = grad_gate
                    saved[batch, rows, 256:512] = grad_up
                    saved[batch, rows, 512:768] = active
                    result[batch, half, rows, :] += contract(active, down_weights, 1, 1)
                    pulled = jnp.concatenate([grad_gate, grad_up], axis=1)
                    back[batch, half, rows, :] += contract(pulled, up_weights, 1, 1)
                save(chunk, batch, half).start()

                @pl.when((chunk == last) & (part < 2))
                def _():
                    cots[batch, half] = result[batch, half].astype(BF16)
                    rows_all[batch, half] = back[batch, half].astype(BF16)
                    for copy in lend(batch):
                        copy.start()

                return inner

            lax.fori_loop(0, 4, block, 0)
            return carry

        lax.fori_loop(0, CHUNKS - 2, chunk_step, 0)

        def give_branch(batch, side):
            columns = pl.ds(512 * side, 512)
            return to_pair(
                14 + 2 * batch + side, cots.at[batch, core, :, columns], mixed.at[batch, columns, :]
            )

        def keep_branch(batch, side):
            columns = pl.ds(512 * side, 512)
            target = branch_out.at[batch, 1 - core, :, columns]
            return keep(8 + 2 * batch + side, mixed.at[batch, columns, :], target)

        def ends(batch):
            return (
                keep(batch, lent.at[0, batch], result_out.at[batch]),
                keep(2 + batch, attended.at[batch], kept_out.at[batch]),
                keep(6 + batch, cots.at[batch, core], branch_out.at[batch, core]),
            )

        def close(batch, carry):
            for copy in lend(batch):
                copy.wait_recv()
            joined = attended[batch]
            outputs = joined + result[batch, core] + lent[0, batch].astype(F32)
            lent[0, batch] = outputs.astype(BF16)
            scale = lax.rsqrt(jnp.mean(joined * joined, axis=1, keepdims=True) + EPS)
            unit = joined * scale
            pulled = (back[batch, core] + lent[1, batch].astype(F32)) * gain_rows[1:2]
            shared = jnp.mean(pulled * unit, axis=1, keepdims=True)
            total = cots[batch, core].astype(F32) + scale * (pulled - unit * shared)
            attended[batch] = total
            cots[batch, core] = total.astype(BF16)
            for side in range(2):
                give_branch(batch, side).start()
            for copy in ends(batch):
                copy.start()
            return carry

        lax.fori_loop(0, 2, close, 0)
        for batch in range(2):
            for side in range(2):
                give_branch(batch, side).wait_recv()
                keep_branch(batch, side).start()
        for batch in range(2):
            save(last, batch, core).wait()
            for copy in ends(batch):
                copy.wait()
            for side in range(2):
                keep_branch(batch, side).wait()
                give_branch(batch, side).wait_send()
            for copy in lend(batch):
                copy.wait_send()

    pl.run_scoped(
        feed_forward,
        pltpu.VMEM((2, 2, 512, 1024), F32),
        pltpu.VMEM((2, 2, 512, 1024), F32),
        pltpu.VMEM((2, 512, WIDE), BF16),
    )
    give_w.wait_send()
    give_seg.wait_send()
    for batch in range(2):
        to_pair(7 + batch, rows_all.at[batch, core], rows_all.at[batch, core]).wait_send()
    give_tile.wait_send()
    give_cot.wait_send()
    gather.drain()


def forward_call(packed, tile, inputs, cotangent, segments, gains):
    rows = inputs.shape[1]
    counter = np.arange(128) % 32
    inverse = jnp.asarray(THETA ** (-2.0 * counter / 64), F32)[None]
    shapes = [
        ((2, 4, 2, 2, 64, WIDE), BF16),
        ((2, SEQ, 1024), BF16),
        ((2, SEQ, WIDE), BF16),
        ((2, SEQ, 1024), BF16),
        ((2, SEQ, 256), F32),
        ((2, SEQ, SEQ), BF16),
        ((2, 8, SEQ), F32),
        ((2, SEQ, 512), BF16),
        ((2, 2, rows, 1024), BF16),
        ((2, 2, rows, 1024), BF16),
        ((CHUNKS - 2, 2, 2, rows, WIDE), BF16),
        ((2, rows, 1024), BF16),
        ((2, 2, rows, 1024), BF16),
        ((2, rows, 1024), F32),
        ((8, 1024), F32),
    ]
    anywhere = pl.BlockSpec(memory_space=pl.ANY)
    inside = pl.BlockSpec(memory_space=pltpu.VMEM)
    return pl.pallas_call(
        forward_kernel,
        out_shape=[jax.ShapeDtypeStruct(*shape) for shape in shapes],
        in_specs=[anywhere] * 5 + [inside] * 2,
        out_specs=[anywhere] * len(shapes),
        scratch_shapes=[
            pltpu.VMEM((CHUNKS, 4, 2, 2, 64, WIDE), BF16),
            pltpu.VMEM((4, 2, 2, 2, 8, 128), F32),
            pltpu.VMEM((8, 1024), F32),
            pltpu.VMEM((2, 2, rows, 1024), BF16),
            pltpu.VMEM((2, 2, rows, 1024), BF16),
            pltpu.VMEM((2, 2, 1, rows), F32),
            pltpu.VMEM((2, SEQ, 512), BF16),
            pltpu.VMEM((2, rows, 512), BF16),
            pltpu.VMEM((4, 2, 2, 64, 512), BF16),
            pltpu.VMEM((2, rows, 1024), F32),
            pltpu.VMEM((2, 2, rows, 1024), BF16),
            pltpu.SemaphoreType.DMA((12,)),
            pltpu.SemaphoreType.DMA((18,)),
            pltpu.SemaphoreType.DMA((18,)),
        ]
        + semaphores(),
        compiler_params=params(0),
        name="forward",
    )(packed, tile, inputs, cotangent, segments.astype(F32)[:, None, :], gains, inverse)


def pack_halves(w_query, w_key, w_value, output_t, w_gate, w_up, down_t):
    rows = w_query.shape[0]
    halves = [jnp.stack(jnp.split(w, 2, axis=1)) for w in (w_query, w_key, w_value, output_t)]
    first = jnp.concatenate(halves[:2], axis=2)[:, None]
    second = jnp.concatenate(halves[2:], axis=2)[:, None]
    wide = jnp.concatenate(
        [w.reshape(rows, 2, CHUNKS - 2, 256).transpose(1, 2, 0, 3) for w in (w_gate, w_up, down_t)],
        axis=3,
    )
    return jnp.concatenate([first, second, wide], axis=1)


def pack_gains(attn_gain, ffn_gain):
    count = attn_gain.shape[0]
    slot = lax.axis_index("fsdp") % (128 // count)
    pair = jnp.stack([attn_gain, ffn_gain]).astype(F32)
    place_of = (jnp.arange(128 // count) == slot).astype(F32)
    spread = (place_of[None, :, None] * pair[:, None, :]).reshape(2, 128)
    return jnp.concatenate([spread, jnp.zeros((6, 128), F32)])


def backward_kernel(*refs):
    (
        w_in, normed_in, raw_in, qkv_in, table_in, mask_in, total_in, mix_in, ffn_in, cot_in,
        saved_in, branch_in, kept_in, x_in, gain_rows, head_gains,
    ) = refs[:16]
    grad_out, sums_out, head_out = refs[16:19]
    sums = refs[19]
    lands = (refs[20:24], refs[24:28], refs[28:32])
    (
        totals, pair_land, rows_all, cots, saved, branch, grads, qkv, raw, table, total, mask, mixed,
        grad_mixed, wo, keys, values, key_sum, value_sum, head_sum, head_land, kept,
        local, pair_sent, pair_landed, head_sent, head_landed, sent, landed,
    ) = refs[32:]
    me, z, y, x, core = place()
    mine, other = pair_rows(core)
    scatter = Scatter(sums, lands, totals, sent, landed)

    def to_pair(number, source, target):
        return pltpu.make_async_remote_copy(
            src_ref=source,
            dst_ref=target,
            send_sem=pair_sent.at[number],
            recv_sem=pair_landed.at[number],
            device_id=(me ^ 1,),
            device_id_type=MESH,
        )

    def load(number, source, target):
        return pltpu.make_async_copy(source, target, local.at[number])

    loads = [
        load(2, saved_in.at[0], saved),
        load(0, ffn_in, rows_all),
        load(1, cot_in, cots),
        load(3, branch_in, branch),
        load(4, w_in.at[1, :, :, pl.ds(256, 512)], wo),
        load(5, mix_in, mixed),
    ]
    def batch_loads(batch):
        return (
            load(6, qkv_in.at[batch], qkv),
            load(7, raw_in.at[batch], raw),
            load(8, table_in.at[batch], table),
            load(9, total_in.at[batch], total),
            load(10, mask_in.at[batch], mask),
        )

    for copy in loads[:3]:
        copy.start()
    greet(me, z, 16)
    head_sum[...] = jnp.zeros_like(head_sum)

    def put(slot, columns, left, right):
        product = contract(left, right, 0, 0).astype(BF16)
        sums[slot, :, :, :, :, columns] = product.reshape(4, 2, 2, 64, columns.size)

    def up_terms(chunk):
        slot = lax.rem(chunk, SUM_SLOTS)
        flat = saved[:, :, :, 0:512].reshape(2048, 512)
        put(slot, pl.ds(0, 512), rows_all[...].reshape(2048, 1024), flat)

    def down_terms(chunk):
        slot = lax.rem(chunk, SUM_SLOTS)
        flat = saved[:, :, :, 512:768].reshape(2048, 256)
        put(slot, pl.ds(512, 256), cots[...].reshape(2048, 1024), flat)

    loads[0].wait()
    loads[1].wait()
    up_terms(0)
    loads[2].wait()
    down_terms(0)
    load(2, saved_in.at[1], saved).start()
    for copy in loads[3:]:
        copy.start()
    for copy in batch_loads(0):
        copy.start()
    def mixed_back(half, carry):
        product = contract(branch[half].reshape(1024, 1024), wo[...].reshape(1024, 512), 1, 0)
        grad_mixed[half] = product.astype(BF16)
        return carry

    def pull_back(grad, span, columns, gain, number):
        plain = raw[span, columns].astype(F32)
        width = plain.shape[1]
        row = lax.broadcasted_iota(jnp.int32, (width, width), 0) // 64
        column = lax.broadcasted_iota(jnp.int32, (width, width), 1) // 64
        ones = jnp.where(row == column, 1.0 / 64.0, 0.0).astype(BF16)
        level = lax.rsqrt(contract((plain * plain).astype(BF16), ones, 1, 0) + EPS)
        unit = plain * level
        turned = grad * table[span, 0:128] - half_turn(grad) * table[span, 128:256]
        terms = turned * unit
        head_sum[number] += jnp.sum(terms.reshape(-1, 8, width), axis=0)
        scaled = terms * gain
        shared = contract(scaled.astype(BF16), ones, 1, 0)
        return level * (turned * gain - unit * shared)

    def sides(pair, parity):
        low = lane_index(pair.shape) < 64
        rows = pair.astype(F32)
        first, second = jnp.where(low, rows, 0.0), jnp.where(low, 0.0, rows)
        if parity == 0:
            second = pltpu.roll(second, 64, 1)
        else:
            first = pltpu.roll(first, 64, 1)
        return first.astype(BF16), second.astype(BF16)

    def attend_back(batch, couple, parity):
        key_pair = qkv[:, pl.ds(pl.multiple_of(512 + couple * 128, 128), 128)].astype(F32)
        value_pair = qkv[:, pl.ds(pl.multiple_of(768 + couple * 128, 128), 128)].astype(F32)
        for target, pair in ((keys, key_pair), (values, value_pair)):
            low, high = split_pair(pair, parity)
            target[0] = low.astype(BF16)
            target[1] = high.astype(BF16)
        if parity == 0:
            key_sum[...] = jnp.zeros_like(key_sum)
            value_sum[...] = jnp.zeros_like(value_sum)
        group = couple * 2 + parity
        picks = lax.broadcasted_iota(jnp.int32, (8, 128), 0) == lane_index((8, 128)) // 64
        picks = jnp.where(picks, 1.0, 0.0).astype(BF16)
        for quarter in range(4):
            span = pl.ds(quarter * 256, 256)
            width = (quarter + 1) * 256
            allowed = mask[0:width, span].astype(F32)
            queries = qkv[span, lanes_at(group, 128)]
            pulled = grad_mixed[batch, span, lanes_at(group, 128)]
            product = pulled.astype(F32) * mixed[batch, span, lanes_at(group, 128)].astype(F32)
            coarse = product.astype(BF16)
            rest = (product - coarse.astype(F32)).astype(BF16)
            centers = contract(picks, coarse, 1, 1) + contract(picks, rest, 1, 1)
            query_sides, pulled_sides = sides(queries, parity), sides(pulled, parity)
            levels = [total[pl.ds(2 * group + side, 1), span] for side in range(2)]
            scores = contract(keys[:, 0:width, :].reshape(2 * width, 128), queries, 1, 1)
            grad_probs = contract(values[:, 0:width, :].reshape(2 * width, 128), pulled, 1, 1)
            low_probs, grad_scores = [], []
            for side in range(2):
                rows = slice(side * width, side * width + width)
                probs = jnp.exp(scores[rows]) * allowed * levels[side]
                low_probs.append(probs.astype(BF16))
                grad_scores.append((probs * (grad_probs[rows] - centers[side : side + 1])).astype(BF16))
            stacked = jnp.concatenate(grad_scores, axis=0)
            grad_query = contract(stacked, keys[:, 0:width, :].reshape(2 * width, 128), 0, 0)
            wide = jnp.concatenate(grad_scores, axis=1)
            grad_key = contract(wide, jnp.concatenate(query_sides, axis=0), 1, 0)
            wide = jnp.concatenate(low_probs, axis=1)
            grad_value = contract(wide, jnp.concatenate(pulled_sides, axis=0), 1, 0)
            key_sum[0:width, :] += grad_key
            value_sum[0:width, :] += grad_value
            grad_raw = pull_back(
                grad_query * 0.125, span, lanes_at(group, 128), head_gains[:, 0:128], 0
            )
            grads[batch, span, lanes_at(group, 128)] = grad_raw.astype(BF16)
        if parity == 1:
            whole = pl.ds(0, SEQ)
            columns = pl.ds(pl.multiple_of(512 + couple * 128, 128), 128)
            grad_raw = pull_back(key_sum[...], whole, columns, head_gains[:, 512:640], 1)
            grads[batch, :, columns] = grad_raw.astype(BF16)
            columns = pl.ds(pl.multiple_of(768 + couple * 128, 128), 128)
            grads[batch, :, columns] = value_sum[...].astype(BF16)

    def head_copy(step):
        bit = (1, 2, 4, 8, 16)[step]
        return pltpu.make_async_remote_copy(
            src_ref=head_sum,
            dst_ref=head_land.at[step],
            send_sem=head_sent.at[step],
            recv_sem=head_landed.at[step],
            device_id=(me ^ bit,),
            device_id_type=MESH,
        )

    def send_heads(step):
        if step > 0:
            head_copy(step - 1).wait()
            head_sum[...] += head_land[step - 1]
        if step < 5:
            head_copy(step).start()

    def near_normed(batch, half):
        part = grads[batch, pl.ds(pl.multiple_of(half * 512, 512), 512), :]
        first = contract(part[:, 0:768], saved[0].reshape(1024, WIDE), 1, 1)
        value_weights = saved[1].reshape(1024, WIDE)[:, 0:256]
        return first + contract(part[:, 768:1024], value_weights, 1, 1)

    def work(time):
        @pl.when(time == 0)
        def _():
            for copy in loads[3:]:
                copy.wait()
            lax.fori_loop(0, 2, mixed_back, 0)

        @pl.when((time >= 1) & (time <= 8))
        def _():
            unit = time - 1
            batch, couple, parity = unit // 4, (unit // 2) % 2, unit % 2

            @pl.when(unit % 4 == 0)
            def _():
                for copy in batch_loads(batch):
                    copy.wait()

            for each in range(2):

                @pl.when(parity == each)
                def _():
                    attend_back(batch, couple, each)

            @pl.when(unit == 3)
            def _():
                for copy in batch_loads(1):
                    copy.start()

        for step in range(6):

            @pl.when(time == 9 + step)
            def _():
                send_heads(step)

        @pl.when(time == 10)
        def _():
            load(2, w_in, saved).wait()
            load(7, x_in, cots.at[1]).start()
            load(6, kept_in.at[0], kept).start()
            lend(0)

        @pl.when((time == 12) | (time == 13))
        def _():
            batch = time - 12
            swap(batch).wait()
            load(6, kept_in.at[batch], kept).wait()

            @pl.when(batch == 0)
            def _():
                load(7, x_in, cots.at[1]).wait()

            rows = cots[1, batch].astype(F32)
            scale = lax.rsqrt(jnp.mean(rows * rows, axis=1, keepdims=True) + EPS)
            unit = rows * scale
            pulled = near_normed(batch, core) + pair_land[batch].astype(F32)
            pulled = pulled * gain_rows[0:1]
            shared = jnp.mean(pulled * unit, axis=1, keepdims=True)
            grad = kept[...] + scale * (pulled - unit * shared)
            cots[0, batch] = grad.astype(BF16)
            store_grad(batch).start()

            @pl.when(batch == 0)
            def _():
                load(6, kept_in.at[1], kept).start()

    def swap(batch):
        return to_pair(1 + batch, cots.at[0, batch], pair_land.at[batch])

    def lend(batch):
        cots[0, batch] = near_normed(batch, 1 - core).astype(BF16)
        swap(batch).start()

    def store_grad(batch):
        return load(8 + batch, cots.at[0, batch], grad_out.at[batch])

    def hand(number, chunks, half):
        return to_pair(
            3 + number, totals.at[chunks, other, :], sums_out.at[half, chunks]
        )

    def own_sums(number, chunks):
        return load(3 + number, totals.at[chunks, mine, :], sums_out.at[core, chunks])

    def next_terms(time):
        @pl.when(time + 1 < CHUNKS - 2)
        def _():
            load(2, saved_in.at[0], saved).wait()
            up_terms(time + 1)
            down_terms(time + 1)

        @pl.when(time + 2 < CHUNKS - 2)
        def _():
            load(2, saved_in.at[time + 2], saved).start()

        @pl.when(time == CHUNKS - 4)
        def _():
            load(0, normed_in, rows_all).start()
            load(2, w_in, saved).start()

        @pl.when(time == CHUNKS - 3)
        def _():
            load(0, normed_in, rows_all).wait()
            slot = (CHUNKS - 2) % SUM_SLOTS
            put(slot, pl.ds(0, 768), rows_all[...].reshape(2048, 1024), grads[:, :, 0:768].reshape(2048, 768))

        @pl.when(time == CHUNKS - 2)
        def _():
            slot = (CHUNKS - 1) % SUM_SLOTS
            put(slot, pl.ds(0, 256), rows_all[...].reshape(2048, 1024), grads[:, :, 768:1024].reshape(2048, 256))
            put(slot, pl.ds(256, 512), branch[...].reshape(2048, 1024), mixed[...].reshape(2048, 512))

        @pl.when(time == 10)
        def _():
            lend(1)

        @pl.when(time == CHUNKS + 3)
        def _():
            hand(0, pl.ds(2, CHUNKS - 2), core).start()
            own_sums(0, pl.ds(2, CHUNKS - 2)).start()

    def body(time, carry):
        scatter.tick(time, (0,))
        work(time)
        scatter.tick(time, (1, 2))
        next_terms(time)
        return carry

    lax.fori_loop(0, CHUNKS + 5, body, 0)
    head_store = load(7, head_sum, head_out)
    head_store.start()
    hand(1, pl.ds(0, 2), core).start()
    own_sums(1, pl.ds(0, 2)).start()
    for number, chunks in ((0, pl.ds(2, CHUNKS - 2)), (1, pl.ds(0, 2))):
        hand(number, chunks, core).wait_send()
        hand(number, chunks, 1 - core).wait_recv()
        own_sums(number, chunks).wait()
    for batch in range(2):
        store_grad(batch).wait()
    head_store.wait()


def backward_call(forward, inputs, gains):
    rows = inputs.shape[1]
    (
        w, normed, raw, qkv, table, mask, total, mix, ffn, cot, saved, _, branch, kept, gain_rows,
    ) = forward
    anywhere = pl.BlockSpec(memory_space=pl.ANY)
    inside = pl.BlockSpec(memory_space=pltpu.VMEM)
    return pl.pallas_call(
        backward_kernel,
        out_shape=[
            jax.ShapeDtypeStruct((2, rows, 1024), BF16),
            jax.ShapeDtypeStruct((2, CHUNKS, 32, WIDE), F32),
            jax.ShapeDtypeStruct((2, 8, 128), F32),
        ],
        in_specs=[anywhere] * 14 + [inside] * 2,
        out_specs=[anywhere] * 3,
        scratch_shapes=[pltpu.VMEM((SUM_SLOTS, 4, 2, 2, 64, WIDE), BF16)]
        + land_shapes()
        + [
            pltpu.VMEM((CHUNKS, 64, WIDE), F32),
            pltpu.VMEM((2, rows, 1024), BF16),
            pltpu.VMEM((2, 2, rows, 1024), BF16),
            pltpu.VMEM((2, 2, rows, 1024), BF16),
            pltpu.VMEM((2, 2, rows, WIDE), BF16),
            pltpu.VMEM((2, 2, rows, 1024), BF16),
            pltpu.VMEM((2, SEQ, 1024), BF16),
            pltpu.VMEM((SEQ, 1024), BF16),
            pltpu.VMEM((SEQ, WIDE), BF16),
            pltpu.VMEM((SEQ, 256), F32),
            pltpu.VMEM((8, SEQ), F32),
            pltpu.VMEM((SEQ, SEQ), BF16),
            pltpu.VMEM((2, SEQ, 512), BF16),
            pltpu.VMEM((2, SEQ, 512), BF16),
            pltpu.VMEM((2, 512, 512), BF16),
            pltpu.VMEM((2, SEQ, 128), BF16),
            pltpu.VMEM((2, SEQ, 128), BF16),
            pltpu.VMEM((SEQ, 128), F32),
            pltpu.VMEM((SEQ, 128), F32),
            pltpu.VMEM((2, 8, 128), F32),
            pltpu.VMEM((5, 2, 8, 128), F32),
            pltpu.VMEM((rows, 1024), F32),
            pltpu.SemaphoreType.DMA((11,)),
            pltpu.SemaphoreType.DMA((5,)),
            pltpu.SemaphoreType.DMA((5,)),
            pltpu.SemaphoreType.DMA((5,)),
            pltpu.SemaphoreType.DMA((5,)),
        ]
        + semaphores(),
        compiler_params=params(1),
        name="backward",
    )(
        w.reshape(2, 2, rows, WIDE), normed.reshape(2, 2, rows, 1024), raw, qkv, table, mask, total,
        mix, ffn, cot, saved, branch, kept, inputs, gain_rows, gains,
    )


def unpack(out):
    def both(chunk, start, stop):
        return jnp.concatenate([out[0, chunk, :, start:stop], out[1, chunk, :, start:stop]], axis=1)

    def wide_of(start):
        return out[:, 2:, :, start : start + 256].transpose(2, 0, 1, 3).reshape(out.shape[2], -1)

    return (
        both(0, 0, 512),
        both(0, 512, 768),
        both(1, 0, 256),
        both(1, 256, 768),
        wide_of(0),
        wide_of(256),
        wide_of(512),
    )


def gain_terms(packed, sums, attn_gain, ffn_gain):
    terms = packed.astype(F32) * sums
    blocks = jnp.sum(terms.reshape(*terms.shape[:-1], 3, 256), axis=(0, 4))
    attn = jnp.sum(blocks[0], axis=1) + blocks[1, :, 0]
    ffn = jnp.sum(blocks[2:, :, 0:2], axis=(0, 2))
    return attn / attn_gain.astype(F32), ffn / ffn_gain.astype(F32)


def local_grid(
    inputs,
    segments,
    attn_gain,
    w_query,
    key_projection,
    value_projection,
    w_output,
    query_gain,
    key_norm_gain,
    ffn_gain,
    w_gate,
    w_up,
    w_down,
    cotangent,
):
    packed = pack_halves(
        w_query, key_projection, value_projection, w_output.T, w_gate, w_up, w_down.T
    )
    gains = [query_gain] * 8 + [key_norm_gain] * 4
    gains = jnp.concatenate(gains).astype(F32)[None]
    forward = forward_call(
        packed, pack_gains(attn_gain, ffn_gain), inputs, cotangent, segments, gains
    )
    input_grad, sums, heads = backward_call(forward, inputs, gains)
    query, key, value, output_t, gate, up, down_t = unpack(sums)
    heads = jnp.sum(heads, axis=1)
    heads = heads[:, :64] + heads[:, 64:]
    attn_gain_grad, ffn_gain_grad = gain_terms(packed, sums, attn_gain, ffn_gain)
    return (
        forward[11],
        input_grad,
        attn_gain_grad,
        query,
        key,
        value,
        output_t.T,
        heads[0],
        heads[1],
        ffn_gain_grad,
        gate,
        up,
        down_t.T,
    )


def from_behind(block, axis, distance):
    devices = range(lax.axis_size(axis))
    route = [(i - distance, i) for i in devices if i - distance in devices]
    return lax.ppermute(block, axis, route)


def row_norm(values, gain_row):
    return values * lax.rsqrt(jnp.mean(values * values, axis=-1, keepdims=True) + EPS) * gain_row


def angles(places, head_width):
    counter = jnp.arange(head_width // 2, dtype=jnp.float32)
    inverse = jnp.power(jnp.float32(THETA), -2.0 * counter / head_width)
    turned = places.astype(jnp.float32)[:, None] * inverse[None, :]
    return (jnp.cos(turned), jnp.sin(turned))


def prepare_inputs(raw_rows, gain_row, cosine_table, sine_table_rows, head_count):
    token_count = raw_rows.shape[0]
    head_width = gain_row.shape[0]
    split_rows = raw_rows.reshape(token_count, head_count, head_width)
    normed = row_norm(split_rows, gain_row)
    first_half = normed[..., : head_width // 2]
    second = normed[..., head_width // 2 :]
    cos_rows = cosine_table[:, None, :]
    sin_rows = sine_table_rows[:, None, :]
    turned = jnp.concatenate(
        [first_half * cos_rows - second * sin_rows, second * cos_rows + first_half * sin_rows],
        axis=-1,
    )
    return turned.reshape(token_count, head_count * head_width)


def plain_product(left_rows, right_rows):
    return jnp.dot(left_rows, right_rows, preferred_element_type=jnp.float32)


def rows_product(left_rows, right_rows):
    return lax.dot_general(
        left_rows, right_rows, (((0,), (0,)), ((), ())), preferred_element_type=jnp.float32
    )


def cols_product(left_rows, right_rows):
    return lax.dot_general(
        left_rows, right_rows, (((1,), (1,)), ((), ())), preferred_element_type=jnp.float32
    )


def silu_product(gate_raw, upward):
    return gate_raw * jax.nn.sigmoid(gate_raw) * upward


def add_sets(former_set, latter_set):
    if former_set is None:
        return latter_set
    return tuple((former + latter for former, latter in zip(former_set, latter_set)))


def local(
    inputs,
    segments,
    attn_gain,
    w_query,
    key_projection,
    value_projection,
    w_output,
    query_gain,
    key_norm_gain,
    ffn_gain,
    w_gate,
    w_up,
    w_down,
    cotangent,
):
    batches = inputs.shape[0]
    tokens = inputs.shape[1]
    head_width = query_gain.shape[0]
    query_width = w_query.shape[1]
    kv_width = key_projection.shape[1]
    query_head_rows = query_width // head_width
    kv_heads = kv_width // head_width
    heads_per_group = query_head_rows // kv_heads
    scale = 1.0 / math.sqrt(head_width)
    query_gain_f = query_gain.astype(jnp.float32)
    key_gain_f = key_norm_gain.astype(jnp.float32)
    device_index = lax.axis_index("fsdp")
    places_row = jnp.arange(tokens, dtype=jnp.int32)
    causal = places_row[None, :] <= places_row[:, None]
    same_run = device_index * tokens // SEQ == (device_index - 1) * tokens // SEQ
    outputs_list = []
    grads_list = []
    shard_sums = None
    gain_sums = None
    for batch_index in range(batches):
        gathered = (
            lax.all_gather(attn_gain, "fsdp", axis=0, tiled=True),
            lax.all_gather(w_query, "fsdp", axis=0, tiled=True),
            lax.all_gather(key_projection, "fsdp", axis=0, tiled=True),
            lax.all_gather(value_projection, "fsdp", axis=0, tiled=True),
            lax.all_gather(w_output, "fsdp", axis=1, tiled=True),
            lax.all_gather(ffn_gain, "fsdp", axis=0, tiled=True),
            lax.all_gather(w_gate, "fsdp", axis=0, tiled=True),
            lax.all_gather(w_up, "fsdp", axis=0, tiled=True),
            lax.all_gather(w_down, "fsdp", axis=1, tiled=True),
        )
        (
            gain_attn,
            full_query,
            full_key,
            full_value,
            full_output,
            gain_ffn,
            full_gate,
            full_up,
            full_down,
        ) = gathered
        hidden = inputs[batch_index].astype(jnp.float32)
        segment = segments[batch_index]
        normed_f, norm_pull = jax.vjp(row_norm, hidden, gain_attn.astype(jnp.float32))
        normed = normed_f.astype(jnp.bfloat16)
        query_raw = plain_product(normed, full_query)
        key_projected = plain_product(normed, full_key)
        value_reduced = plain_product(normed, full_value).astype(jnp.bfloat16)
        lower_count = jnp.sum((segment[None, :] < segment[:, None]).astype(jnp.int32), axis=1)
        local_places = places_row - lower_count
        cos_local, sin_local = angles(local_places, head_width)
        key_sent = prepare_inputs(key_projected, key_gain_f, cos_local, sin_local, kv_heads).astype(
            jnp.bfloat16
        )
        remote_key, remote_value, remote_segment = from_behind(
            (key_sent, value_reduced, segment.astype(jnp.bfloat16)), "fsdp", 1
        )
        remote_match = (remote_segment.astype(jnp.int32)[None, :] == segment[:, None]) & same_run
        places_all = local_places + jnp.sum(remote_match.astype(jnp.int32), axis=1)
        cosine_table, sine_table_rows = angles(places_all, head_width)
        query_f, query_pull = jax.vjp(
            lambda raw_rows, gain_row: prepare_inputs(
                raw_rows, gain_row, cosine_table, sine_table_rows, query_head_rows
            ),
            query_raw,
            query_gain_f,
        )
        key_f, key_pull = jax.vjp(
            lambda raw_rows, gain_row: prepare_inputs(
                raw_rows, gain_row, cosine_table, sine_table_rows, kv_heads
            ),
            key_projected,
            key_gain_f,
        )
        query_low = query_f.astype(jnp.bfloat16)
        key_low = key_f.astype(jnp.bfloat16)
        allowed = jnp.concatenate(
            [remote_match, causal & (segment[None, :] == segment[:, None])], axis=1
        )
        query_split = query_low.reshape(tokens, kv_heads, heads_per_group, head_width).transpose(
            1, 0, 2, 3
        )
        key_split = (
            jnp.concatenate([remote_key, key_low], axis=0)
            .reshape(2 * tokens, kv_heads, head_width)
            .transpose(1, 0, 2)
        )
        value_split = (
            jnp.concatenate([remote_value, value_reduced], axis=0)
            .reshape(2 * tokens, kv_heads, head_width)
            .transpose(1, 0, 2)
        )

        def head_forward(blocks):
            query_part, key_part, value_part = blocks
            scores = (
                jnp.einsum("tgd,ld->gtl", query_part, key_part, preferred_element_type=jnp.float32)
                * scale
            )
            scores = jnp.where(allowed[None], scores, NEG)
            row_peak = jnp.max(scores, axis=-1, keepdims=True)
            raised = jnp.exp(scores - row_peak)
            row_total = jnp.sum(raised, axis=-1, keepdims=True)
            prob_rows = (raised / row_total).astype(jnp.bfloat16)
            mixed_part = jnp.einsum(
                "gtl,ld->tgd", prob_rows, value_part, preferred_element_type=jnp.float32
            )
            return (mixed_part.astype(jnp.bfloat16), (row_peak + jnp.log(row_total))[..., 0])

        mixed_split, log_totals = lax.map(head_forward, (query_split, key_split, value_split))
        attn_mix = mixed_split.transpose(1, 0, 2, 3).reshape(tokens, query_width)
        attended = hidden + plain_product(attn_mix, full_output)
        ffn_f, ffn_pull = jax.vjp(row_norm, attended, gain_ffn.astype(jnp.float32))
        ffn_in = ffn_f.astype(jnp.bfloat16)
        gate_raw = plain_product(ffn_in, full_gate)
        upward = plain_product(ffn_in, full_up)
        active_f, active_pull = jax.vjp(silu_product, gate_raw, upward)
        active = active_f.astype(jnp.bfloat16)
        result = attended + plain_product(active, full_down)
        outputs_list.append(result.astype(jnp.bfloat16))
        back_query, back_key, back_value, back_output, back_gate, back_up, back_down = (
            lax.all_gather(w_query, "fsdp", axis=0, tiled=True),
            lax.all_gather(key_projection, "fsdp", axis=0, tiled=True),
            lax.all_gather(value_projection, "fsdp", axis=0, tiled=True),
            lax.all_gather(w_output, "fsdp", axis=1, tiled=True),
            lax.all_gather(w_gate, "fsdp", axis=0, tiled=True),
            lax.all_gather(w_up, "fsdp", axis=0, tiled=True),
            lax.all_gather(w_down, "fsdp", axis=1, tiled=True),
        )
        grad_result = cotangent[batch_index]
        grad_down_t = rows_product(grad_result, active)
        grad_active = cols_product(grad_result, back_down)
        grad_gate_f, grad_up_f = active_pull(grad_active)
        grad_gate_low = grad_gate_f.astype(jnp.bfloat16)
        grad_up_low = grad_up_f.astype(jnp.bfloat16)
        grad_gate_w = rows_product(ffn_in, grad_gate_low)
        grad_up_w = rows_product(ffn_in, grad_up_low)
        grad_ffn_in = cols_product(grad_gate_low, back_gate) + cols_product(grad_up_low, back_up)
        grad_attended_norm, grad_ffn_gain = ffn_pull(grad_ffn_in)
        grad_attended = grad_result.astype(jnp.float32) + grad_attended_norm
        grad_branch = grad_attended.astype(jnp.bfloat16)
        grad_output_t = rows_product(grad_branch, attn_mix)
        grad_mixed = cols_product(grad_branch, back_output).astype(jnp.bfloat16)
        grad_split = grad_mixed.reshape(tokens, kv_heads, heads_per_group, head_width).transpose(
            1, 0, 2, 3
        )

        def head_backward(blocks):
            query_part, key_part, value_part, grad_part, log_part = blocks
            scores = (
                jnp.einsum("tgd,ld->gtl", query_part, key_part, preferred_element_type=jnp.float32)
                * scale
            )
            scores = jnp.where(allowed[None], scores, NEG)
            prob_rows = jnp.exp(scores - log_part[..., None])
            grad_probs = jnp.einsum(
                "tgd,ld->gtl", grad_part, value_part, preferred_element_type=jnp.float32
            )
            center = jnp.sum(prob_rows * grad_probs, axis=-1, keepdims=True)
            grad_scores = (prob_rows * (grad_probs - center)).astype(jnp.bfloat16)
            grad_query_part = (
                jnp.einsum("gtl,ld->tgd", grad_scores, key_part, preferred_element_type=jnp.float32)
                * scale
            )
            grad_key_part = (
                jnp.einsum(
                    "gtl,tgd->ld", grad_scores, query_part, preferred_element_type=jnp.float32
                )
                * scale
            )
            grad_value_part = jnp.einsum(
                "gtl,tgd->ld",
                prob_rows.astype(jnp.bfloat16),
                grad_part,
                preferred_element_type=jnp.float32,
            )
            return (grad_query_part, grad_key_part, grad_value_part)

        grad_query_split, grad_key_split, grad_value_split = lax.map(
            head_backward, (query_split, key_split, value_split, grad_split, log_totals)
        )
        grad_query_rot = grad_query_split.transpose(1, 0, 2, 3).reshape(tokens, query_width)
        grad_key_all = grad_key_split.transpose(1, 0, 2).reshape(2 * tokens, kv_width)
        grad_value_all = grad_value_split.transpose(1, 0, 2).reshape(2 * tokens, kv_width)
        back_key_grad, back_value_grad = (
            from_behind(grad_key_all[:tokens].astype(jnp.bfloat16), "fsdp", -1).astype(jnp.float32),
            from_behind(grad_value_all[:tokens].astype(jnp.bfloat16), "fsdp", -1).astype(
                jnp.float32
            ),
        )
        grad_key_rot = grad_key_all[tokens:] + back_key_grad
        grad_value_low = (grad_value_all[tokens:] + back_value_grad).astype(jnp.bfloat16)
        grad_query_raw, grad_query_gain = query_pull(grad_query_rot)
        grad_key_raw, grad_key_gain = key_pull(grad_key_rot)
        grad_query_low = grad_query_raw.astype(jnp.bfloat16)
        grad_key_low = grad_key_raw.astype(jnp.bfloat16)
        grad_query_w = rows_product(normed, grad_query_low)
        grad_key_w = rows_product(normed, grad_key_low)
        grad_value_w = rows_product(normed, grad_value_low)
        grad_normed = (
            cols_product(grad_query_low, back_query)
            + cols_product(grad_key_low, back_key)
            + cols_product(grad_value_low, back_value)
        )
        grad_hidden_norm, grad_attn_gain = norm_pull(grad_normed)
        grads_list.append((grad_attended + grad_hidden_norm).astype(jnp.bfloat16))
        gain_sums = add_sets(gain_sums, (grad_query_gain, grad_key_gain))
        shard_terms = (
            lax.psum_scatter(grad_attn_gain, "fsdp", scatter_dimension=0, tiled=True),
            lax.psum_scatter(grad_query_w, "fsdp", scatter_dimension=0, tiled=True),
            lax.psum_scatter(grad_key_w, "fsdp", scatter_dimension=0, tiled=True),
            lax.psum_scatter(grad_value_w, "fsdp", scatter_dimension=0, tiled=True),
            lax.psum_scatter(grad_output_t, "fsdp", scatter_dimension=0, tiled=True),
            lax.psum_scatter(grad_ffn_gain, "fsdp", scatter_dimension=0, tiled=True),
            lax.psum_scatter(grad_gate_w, "fsdp", scatter_dimension=0, tiled=True),
            lax.psum_scatter(grad_up_w, "fsdp", scatter_dimension=0, tiled=True),
            lax.psum_scatter(grad_down_t, "fsdp", scatter_dimension=0, tiled=True),
        )
        shard_sums = add_sets(shard_sums, shard_terms)
    head_sums = lax.psum((gain_sums[0], gain_sums[1]), "fsdp")
    return (
        jnp.stack(outputs_list),
        jnp.stack(grads_list),
        shard_sums[0],
        shard_sums[1],
        shard_sums[2],
        shard_sums[3],
        shard_sums[4].T,
        head_sums[0],
        head_sums[1],
        shard_sums[5],
        shard_sums[6],
        shard_sums[7],
        shard_sums[8].T,
    )


def solution(mesh):
    return jax.shard_map(
        local_grid if mesh.shape["fsdp"] == 32 else local,
        mesh=mesh,
        in_specs=(
            P(None, "fsdp", None),
            P(None, "fsdp"),
            P("fsdp"),
            P("fsdp", None),
            P("fsdp", None),
            P("fsdp", None),
            P(None, "fsdp"),
            P(),
            P(),
            P("fsdp"),
            P("fsdp", None),
            P("fsdp", None),
            P(None, "fsdp"),
            P(None, "fsdp", None),
        ),
        out_specs=(
            P(None, "fsdp", None),
            P(None, "fsdp", None),
            P("fsdp"),
            P("fsdp", None),
            P("fsdp", None),
            P("fsdp", None),
            P(None, "fsdp"),
            P(),
            P(),
            P("fsdp"),
            P("fsdp", None),
            P("fsdp", None),
            P(None, "fsdp"),
        ),
        check_vma=False,
    )
```

```python
import math

import jax
import jax.numpy as jnp
import numpy as np
from jax import lax
from jax.experimental import pallas as pl
from jax.experimental.pallas import tpu as pltpu
from jax.sharding import PartitionSpec as P

SEQ = 1024


EPS = 1e-05
THETA = 1000000.0
NEG = -1e30


CHUNKS = 11
WIDE = 768
MESH = pl.DeviceIdType.MESH
ALL = slice(None)
F32 = jnp.float32
BF16 = jnp.bfloat16
PARTS = (
    ("A", pl.ds(0, 48), pl.ds(0, 384)),
    ("B", pl.ds(0, 48), pl.ds(384, 384)),
    ("C", pl.ds(48, 16), pl.ds(0, 768)),
)
GAINS = len(PARTS)
OUTWARD = {
    "A": ("z0", "z1", "z2", "y", "x"),
    "B": ("z0", "z1", "z2", "x", "y"),
    "C": ("x", "y", "z0", "z1", "z2"),
}
INWARD = {
    "A": ("x", "y", "z0", "z1", "z2"),
    "B": ("y", "x", "z0", "z1", "z2"),
    "C": ("z0", "z1", "z2", "y", "x"),
}
SUM_SLOTS = 6
HELD = 2
LAND_SLOTS = 3


def place():
    me = lax.axis_index("fsdp")
    return me, me // 8, (me // 4) % 2, (me // 2) % 2, me % 2


def guarded(condition, action):
    if condition is None:
        action()
    else:
        pl.when(condition)(action)


def greet(me, z, far=0):
    gate = pltpu.get_barrier_semaphore()
    for bit in (1, 2, 4):
        pl.semaphore_signal(gate, inc=1, device_id=(me ^ bit,), device_id_type=MESH)

    @pl.when(z > 0)
    def _():
        pl.semaphore_signal(gate, inc=1, device_id=(me - 8,), device_id_type=MESH)

    @pl.when(z < 3)
    def _():
        pl.semaphore_signal(gate, inc=1, device_id=(me + 8,), device_id_type=MESH)

    if far:
        pl.semaphore_signal(gate, inc=1, device_id=(me ^ far,), device_id_type=MESH)
    pl.semaphore_wait(gate, (4 if far else 3) + (z > 0).astype(jnp.int32) + (z < 3).astype(jnp.int32))


class Gather:
    def __init__(self, full, tiles, sent, landed):
        self.full, self.tiles, self.sent, self.landed = full, tiles, sent, landed
        self.me, self.z, self.y, self.x, self.core = place()

    def moves(self, part, step, chunk):
        kind, rows, columns = PARTS[0] if part == GAINS else PARTS[part]
        z, y, x, me = self.z, self.y, self.x, self.me

        def view(zz, yy, xx):
            if part == GAINS:
                return self.tiles.at[zz, yy, xx]
            return self.full.at[chunk, zz, yy, xx, rows, columns]

        axis = OUTWARD[kind][step]
        if axis[0] == "z":
            far = int(axis[1])
            yy, xx = (ALL, ALL) if kind == "C" else (y, x)
            return (
                ((z >= far) & (z < 3), z - far, me + 8, z >= far + 1, z - 1 - far),
                ((z <= 3 - far) & (z > 0), z + far, me - 8, z <= 2 - far, z + 1 + far),
            ), lambda zz: view(zz, yy, xx)
        zz = z if kind == "C" else ALL
        if axis == "y":
            xx = x if kind == "A" else ALL
            return ((None, y, me ^ 4, None, 1 - y),), lambda yy: view(zz, yy, xx)
        yy = ALL if kind == "A" else y
        return ((None, x, me ^ 2, None, 1 - x),), lambda xx: view(zz, yy, xx)

    def copy(self, ref, device, part, step, chunk, way):
        return pltpu.make_async_remote_copy(
            src_ref=ref,
            dst_ref=ref,
            send_sem=self.sent.at[chunk, part, step, way],
            recv_sem=self.landed.at[chunk, part, step, way],
            device_id=(device,),
            device_id_type=MESH,
        )

    def send(self, part, step, chunk):
        moves, view = self.moves(part, step, chunk)
        for way, (sends, mine, device, _, _) in enumerate(moves):
            guarded(
                sends,
                lambda: self.copy(view(mine), device, part, step, chunk, way).start(),
            )

    def receive(self, part, step, chunk):
        moves, view = self.moves(part, step, chunk)
        for way, (_, _, _, receives, other) in enumerate(moves):
            guarded(
                receives,
                lambda: self.copy(view(other), self.me ^ 2, part, step, chunk, way).wait_recv(),
            )

    def finish(self, part, step, chunk):
        moves, view = self.moves(part, step, chunk)
        for way, (sends, mine, device, _, _) in enumerate(moves):
            guarded(
                sends,
                lambda: self.copy(view(mine), device, part, step, chunk, way).wait_send(),
            )

    def tick(self, time, parts):
        for step in range(6):
            age = time - step
            chunk = jnp.where(age < 2, age, age - HELD)

            @pl.when((age >= 0) & (chunk < CHUNKS) & ((age < 2) | (chunk >= 2)))
            def _():
                for part in parts:
                    if step > 0:
                        self.receive(part, step - 1, chunk)
                    if step < 5:
                        self.send(part, step, chunk)

    def tick_gains(self, step):
        if step > 0:
            self.receive(GAINS, step - 1, 0)
        if step < 5:
            self.send(GAINS, step, 0)

    def drain(self):
        def body(chunk, carry):
            for part in range(len(PARTS)):
                for step in range(5):
                    self.finish(part, step, chunk)
            return carry

        lax.fori_loop(0, CHUNKS, body, 0)
        for step in range(5):
            self.finish(GAINS, step, 0)


class Scatter:
    def __init__(self, sums, lands, totals, sent, landed):
        self.sums, self.lands, self.totals = sums, lands, totals
        self.sent, self.landed = sent, landed
        self.me, self.z, self.y, self.x, self.core = place()

    def moves(self, part, step, chunk):
        kind, rows, columns = PARTS[part]
        z, y, x, me = self.z, self.y, self.x, self.me
        slot, land = lax.rem(chunk, SUM_SLOTS), lax.rem(chunk, LAND_SLOTS)
        first, second, up, down = self.lands[part]
        axis = INWARD[kind][step]

        def view(zz, yy, xx):
            return self.sums.at[slot, zz, yy, xx, rows, columns]

        if axis[0] == "z":
            far = int(axis[1])
            count = 3 - far
            yy, xx = (ALL, ALL) if kind == "C" else (y, x)
            above, below = pl.ds(far + 1, count), pl.ds(0, count)
            up_land, down_land = up.at[land, pl.ds(far, count)], down.at[land, pl.ds(0, count)]
            return (
                (z == far, view(above, yy, xx), up_land, me + 8, z == far + 1, view(above, yy, xx)),
                (z == 3 - far, view(below, yy, xx), down_land, me - 8, z == 2 - far, view(below, yy, xx)),
            )
        zz = z if kind == "C" else ALL
        ref = (first if step == 0 or (kind == "C" and step == 3) else second).at[land]
        if axis == "x":
            yy = ALL if kind == "A" else y
            return ((None, view(zz, yy, 1 - x), ref, me ^ 2, None, view(zz, yy, x)),)
        xx = x if kind == "A" else ALL
        return ((None, view(zz, 1 - y, xx), ref, me ^ 4, None, view(zz, y, xx)),)

    def copy(self, source, target, device, part, step, chunk, way):
        return pltpu.make_async_remote_copy(
            src_ref=source,
            dst_ref=target,
            send_sem=self.sent.at[chunk, part, step, way],
            recv_sem=self.landed.at[chunk, part, step, way],
            device_id=(device,),
            device_id_type=MESH,
        )

    def step(self, part, step, chunk):
        if step > 0:
            for way, move in enumerate(self.moves(part, step - 1, chunk)):
                sends, source, land, device, receives, target = move

                def add():
                    self.copy(land, land, self.me ^ 2, part, step - 1, chunk, way).wait_recv()
                    target[...] = (target[...].astype(F32) + land[...].astype(F32)).astype(BF16)

                guarded(receives, add)
                guarded(
                    sends,
                    lambda: self.copy(source, land, device, part, step - 1, chunk, way).wait_send(),
                )
        if step < 5:
            for way, move in enumerate(self.moves(part, step, chunk)):
                sends, source, land, device, _, _ = move
                guarded(
                    sends,
                    lambda: self.copy(source, land, device, part, step, chunk, way).start(),
                )
        else:
            _, rows, columns = PARTS[part]
            slot = lax.rem(chunk, SUM_SLOTS)
            self.totals[lax.rem(chunk + 2, CHUNKS), rows, columns] = self.sums[
                slot, self.z, self.y, self.x, rows, columns
            ].astype(F32)

    def tick(self, time, parts):
        for step in range(5, -1, -1):
            chunk = time - step

            @pl.when((chunk >= 0) & (chunk < CHUNKS))
            def _():
                for part in parts:
                    self.step(part, step, chunk)


def pair_rows(core):
    mine = pl.ds(pl.multiple_of(core * 32, 32), 32)
    other = pl.ds(pl.multiple_of((1 - core) * 32, 32), 32)
    return mine, other


def semaphores():
    return [pltpu.SemaphoreType.DMA((CHUNKS, len(PARTS) + 1, 5, 2))] * 2


def land_shapes():
    slots = LAND_SLOTS
    plain = [(slots, 4, 2, 48, 384), (slots, 4, 48, 384), (slots, 3, 48, 384), (slots, 3, 48, 384)]
    late = [(slots, 2, 16, 768), (slots, 16, 768), (slots, 3, 2, 2, 16, 768), (slots, 3, 2, 2, 16, 768)]
    return [pltpu.VMEM(shape, BF16) for shape in plain + plain + late]


def params(number):
    return pltpu.CompilerParams(
        collective_id=number, has_side_effects=True, vmem_limit_bytes=62 * 2**20
    )


EAGER = 7
SPREAD = 3
LATER = CHUNKS + 5 + HELD - EAGER - SPREAD


def contract(left, right, left_dim, right_dim):
    return lax.dot_general(
        left, right, (((left_dim,), (right_dim,)), ((), ())), preferred_element_type=F32
    )


def lane_index(shape):
    return lax.broadcasted_iota(jnp.int32, shape, 1)


def half_turn(rows):
    width = rows.shape[1]
    first = lane_index(rows.shape) % 64 < 32
    return jnp.where(first, pltpu.roll(rows, width - 32, 1), pltpu.roll(rows, 32, 1))


def head_means(rows, ones):
    parts = [
        contract(rows[:, k : k + 256].astype(BF16), ones, 1, 0)
        for k in range(0, rows.shape[1], 256)
    ]
    return jnp.concatenate(parts, axis=1)


def head_ones():
    row = lax.broadcasted_iota(jnp.int32, (256, 256), 0) // 64
    column = lax.broadcasted_iota(jnp.int32, (256, 256), 1) // 64
    return jnp.where(row == column, 1.0 / 64.0, 0.0).astype(BF16)


def tiled(table, copies):
    return jnp.concatenate([table] * copies, axis=1)


def split_pair(rows, group):
    pair = rows[:, 128 * (group // 2) : 128 * (group // 2) + 128]
    low = lane_index(pair.shape) < 64
    if group % 2 == 0:
        kept = jnp.where(low, pair, 0.0)
        return kept, pltpu.roll(kept, 64, 1)
    kept = jnp.where(low, 0.0, pair)
    return pltpu.roll(kept, 64, 1), kept


def lanes_at(block, width):
    return pl.ds(pl.multiple_of(block * width, width), width)


def forward_kernel(*refs):
    weights = refs[:7]
    tile_in, x_in, cot_in, seg_in, gains, inverse = refs[7:13]
    (
        w_out, normed_out, raw_out, qkv_out, table_out, mask_out, total_out, mix_out,
        ffn_out, cot_out, saved_out, result_out, branch_out, kept_out, gain_out,
    ) = refs[13:28]
    (
        full, tiles, gain_rows, rows_all, cots, seg_rows, mixed, mixed_pair, wo_pair, attended,
        lent, local, pair_sent, pair_landed, sent, landed,
    ) = refs[28:]
    me, z, y, x, core = place()
    pair = (me ^ 1,)
    mine, other = pair_rows(core)

    def to_pair(number, source, target):
        return pltpu.make_async_remote_copy(
            src_ref=source,
            dst_ref=target,
            send_sem=pair_sent.at[number],
            recv_sem=pair_landed.at[number],
            device_id=pair,
            device_id_type=MESH,
        )

    def keep(number, source, target):
        return pltpu.make_async_copy(source, target, local.at[number])

    own_x = keep(1, x_in, rows_all.at[:, core])
    own_cot = keep(2, cot_in, cots.at[:, core])
    own_seg = keep(3, seg_in, seg_rows.at[core])
    first, later = pl.ds(0, 2), pl.ds(2, CHUNKS - 2)

    def piece_of(number, half, at, width, chunk, column):
        source = weights[number].at[:, pl.ds(pl.multiple_of(half * (weights[number].shape[1] // 2) + at, 256), width)]
        return source, full.at[chunk, z, y, x, mine, pl.ds(column, width)]

    def first_pieces(half):
        return (
            piece_of(0, half, 0, 512, 0, 0),
            piece_of(1, half, 0, 256, 0, 512),
            piece_of(2, half, 0, 256, 1, 0),
            piece_of(3, half, 0, 512, 1, 256),
        )

    def later_pieces(half, chunk):
        return tuple(piece_of(4 + k, half, 256 * chunk, 256, chunk + 2, 256 * k) for k in range(3))

    def place_later(chunk, carry):
        for source, target in later_pieces(1 - core, chunk):
            to_pair(18, source, target).start()
        for source, target in later_pieces(core, chunk):
            keep(4, source, target).start()
        return carry

    def placed(number, local_number, chunks):
        keep(local_number, full.at[chunks, z, y, x, mine, :], full.at[chunks, z, y, x, mine, :]).wait()
        whole = full.at[chunks, z, y, x, other, :]
        to_pair(number, whole, whole).wait_recv()

    give_x = to_pair(1, x_in, rows_all.at[:, core])
    take_x = to_pair(1, x_in, rows_all.at[:, 1 - core])
    give_cot = to_pair(2, cot_in, cots.at[:, core])
    take_cot = to_pair(2, cot_in, cots.at[:, 1 - core])
    give_seg = to_pair(3, seg_in, seg_rows.at[core])
    take_seg = to_pair(3, seg_in, seg_rows.at[1 - core])
    for source, target in first_pieces(core):
        keep(0, source, target).start()
    greet(me, z)
    for source, target in first_pieces(1 - core):
        to_pair(0, source, target).start()
    own_tile = keep(5, tile_in, tiles.at[z, y, x, core])
    give_tile = to_pair(9, tile_in, tiles.at[z, y, x, core])
    own_tile.start()
    give_tile.start()
    own_seg.start()
    give_seg.start()
    own_x.start()
    give_x.start()
    lax.fori_loop(0, CHUNKS - 2, place_later, 0)
    own_cot.start()
    give_cot.start()
    placed(0, 0, first)
    own_tile.wait()
    to_pair(9, tile_in, tiles.at[z, y, x, 1 - core]).wait_recv()
    gather = Gather(full, tiles, sent, landed)
    give_wo = to_pair(4, full.at[1, :, :, :, :, pl.ds(256, 512)], wo_pair)
    keep_w = keep(0, full.at[pl.ds(0, 2)], w_out)
    keep_gain = keep(11, gain_rows, gain_out)
    keep_cot = keep(2, cots, cot_out)
    def attention(normed, raw, qkv, table, mask, mask_turned, total, total_turned, keys, values):
        def early_copies(batch):
            return (
                keep(4, normed, normed_out.at[batch]),
                keep(5, raw, raw_out.at[batch]),
                keep(6, qkv, qkv_out.at[batch]),
                keep(7, table.at[batch], table_out.at[batch]),
                keep(8, mask_turned.at[batch], mask_out.at[batch]),
            )

        def late_copies(batch):
            return (
                keep(9, total_turned, total_out.at[batch]),
                keep(10, mixed.at[batch], mix_out.at[batch]),
            )

        def prepare(batch):
            segment = jnp.concatenate([seg_rows[0, batch], seg_rows[1, batch]], axis=1)
            column = jnp.broadcast_to(segment, (128, SEQ)).T
            below = jnp.zeros((SEQ, 128), F32)
            for k in range(0, SEQ, 128):
                below += (segment[:, k : k + 128] < column).astype(F32)
            before = jnp.sum(below, axis=1, keepdims=True)
            spot = lax.broadcasted_iota(jnp.int32, (SEQ, 128), 0).astype(F32) - before
            angle = spot * inverse[...]
            sine = jnp.sin(angle)
            first = lane_index((SEQ, 128)) % 64 < 32
            table[batch, :, 0:128] = jnp.cos(angle)
            table[batch, :, 128:256] = jnp.where(first, -sine, sine)
            for quarter in range(4):
                span = pl.ds(quarter * 256, 256)
                width = (quarter + 1) * 256
                same = segment[:, :width] == column[quarter * 256 : quarter * 256 + 256, 0:1]
                spots = lax.broadcasted_iota(jnp.int32, (256, width), 0) + quarter * 256
                behind = lane_index((256, width)) <= spots
                mask[batch, span, 0:width] = jnp.where(same & behind, 1.0, 0.0).astype(BF16)
                first_key = quarter * 256
                same = segment[:, first_key:] == column[first_key : first_key + 256, 0:1]
                spots = lax.broadcasted_iota(jnp.int32, same.shape, 0)
                behind = spots <= lane_index(same.shape)
                turned = jnp.where(same & behind, 1.0, 0.0).astype(BF16)
                mask_turned[batch, span, first_key:] = turned

        def project(batch):
            total[...] = jnp.zeros_like(total)
            ones = head_ones()

            def value_block(half, carry):
                span = pl.ds(pl.multiple_of(half * 512, 512), 512)
                value_weights = full[1, :, :, :, :, 0:256].reshape(1024, 256)
                value = contract(normed[span, :], value_weights, 1, 0).astype(BF16)
                qkv[span, 768:1024] = value
                value = value.astype(F32)
                for group in range(4):
                    low, high = split_pair(value, group)
                    values[group, 0, span, :] = low.astype(BF16)
                    values[group, 1, span, :] = high.astype(BF16)
                return carry

            def block(half, carry):
                span = pl.ds(pl.multiple_of(half * 512, 512), 512)
                rows = rows_all[batch, half].astype(F32)
                scale = lax.rsqrt(jnp.mean(rows * rows, axis=1, keepdims=True) + EPS)
                unit = (rows * scale * gain_rows[0:1]).astype(BF16)
                normed[span, :] = unit
                weights = full[0].reshape(1024, WIDE)
                product = contract(unit, weights, 1, 0)
                raw[span, :] = product.astype(BF16)
                level = lax.rsqrt(head_means(product * product, ones) + EPS)
                turned = product * level * gains[...]
                cosine = tiled(table[batch, span, 0:128], 6)
                sine_signed = tiled(table[batch, span, 128:256], 6)
                turned = turned * cosine + half_turn(turned) * sine_signed
                query = turned[:, 0:512] * 0.125
                key = turned[:, 512:768].astype(BF16).astype(F32)
                qkv[span, 0:512] = query.astype(BF16)
                qkv[span, 512:768] = key.astype(BF16)
                for group in range(4):
                    low, high = split_pair(key, group)
                    keys[group, 0, span, :] = low.astype(BF16)
                    keys[group, 1, span, :] = high.astype(BF16)
                return carry

            lax.fori_loop(0, 2, block, 0)

            @pl.when(batch == 0)
            def _():
                gather.tick(EAGER - 1, (0, 1, 2))
                give_wo.start()
                keep_w.start()

            lax.fori_loop(0, 2, value_block, 0)

        def attend(batch, quarter):
            span = pl.ds(quarter * 256, 256)
            width = (quarter + 1) * 256
            allowed = mask[batch, span, 0:width].astype(F32)
            lane = lane_index((256, 128))

            def group_step(group, carry):
                queries = qkv[span, lanes_at(group, 128)]
                parts, sums = [], []
                for side in range(2):
                    scores = contract(queries, keys[group, side, 0:width, :], 1, 1)
                    raised = jnp.exp(scores) * allowed
                    sums.append(1.0 / jnp.sum(raised, axis=1, keepdims=True))
                    parts.append(
                        contract(raised.astype(BF16), values[group, side, 0:width, :], 1, 0)
                    )
                result = (parts[0] + parts[1]) * jnp.where(lane < 64, sums[0], sums[1])
                mixed[batch, span, lanes_at(group, 128)] = result.astype(BF16)
                old = total[span, :]
                old = jnp.where(lane == 2 * group, sums[0], old)
                total[span, :] = jnp.where(lane == 2 * group + 1, sums[1], old)
                return carry

            lax.fori_loop(0, 4, group_step, 0)

        def piece(number, carry):
            batch, part = number // 4, number % 4

            @pl.when(part == 0)
            def _():
                @pl.when(batch > 0)
                def _():
                    for copy in early_copies(0) + late_copies(0):
                        copy.wait()

                project(batch)
                for copy in early_copies(batch):
                    copy.start()

            for turn in range(2):

                @pl.when((number % 2 == turn) & (number < 2 * SPREAD))
                def _():
                    gather.tick(EAGER + number // 2, ((0, 2), (1,))[turn])

            for quarter in range(4):

                @pl.when(part == quarter)
                def _():
                    attend(batch, quarter)

            @pl.when(part == 3)
            def _():
                total_turned[...] = total[...].T[0:8, :]
                for copy in late_copies(batch):
                    copy.start()
                to_pair(5 + batch, mixed.at[batch, lanes_at(1 - core, 512), :], mixed_pair.at[batch]).start()

            return carry

        own_seg.wait()
        take_seg.wait_recv()
        def early(time, carry):
            for step in range(6):

                @pl.when(time == step)
                def _():
                    gather.tick_gains(step)

            @pl.when(time == 2)
            def _():
                placed(18, 4, later)

            gather.tick(time, (0, 1, 2))
            for batch in range(2):

                @pl.when(time == 1 + 2 * batch)
                def _():
                    prepare(batch)

            return carry

        lax.fori_loop(0, EAGER - 1, early, 0)
        for block in range(8):
            quad = tiles[block // 2, block % 2]
            quad = quad[0, 0] + quad[0, 1] + quad[1, 0] + quad[1, 1]
            gain_rows[:, 128 * block : 128 * block + 128] = quad
        keep_gain.start()
        own_x.wait()
        own_cot.wait()
        take_x.wait_recv()
        take_cot.wait_recv()
        keep_cot.start()
        lax.fori_loop(0, 8, piece, 0)
        for copy in early_copies(1) + late_copies(1):
            copy.wait()

    pl.run_scoped(
        attention,
        pltpu.VMEM((SEQ, 1024), BF16),
        pltpu.VMEM((SEQ, WIDE), BF16),
        pltpu.VMEM((SEQ, 1024), BF16),
        pltpu.VMEM((2, SEQ, 256), F32),
        pltpu.VMEM((2, SEQ, SEQ), BF16),
        pltpu.VMEM((2, SEQ, SEQ), BF16),
        pltpu.VMEM((SEQ, 128), F32),
        pltpu.VMEM((8, SEQ), F32),
        pltpu.VMEM((4, 2, SEQ, 128), BF16),
        pltpu.VMEM((4, 2, SEQ, 128), BF16),
    )
    give_wo.wait_send()
    give_wo.wait_recv()
    give_x.wait_send()

    def swap_mixed(batch):
        return to_pair(5 + batch, mixed.at[batch, lanes_at(1 - core, 512), :], mixed_pair.at[batch])

    def join(batch, carry):
        swap_mixed(batch).wait_recv()
        span = lanes_at(core, 512)
        own_wo = full[1, :, :, :, :, 256:768].reshape(1024, 512)
        result = rows_all[batch, core].astype(F32)
        result += contract(mixed[batch, span, :], own_wo, 1, 1)
        result += contract(mixed_pair[batch], wo_pair[...].reshape(1024, 512), 1, 1)
        attended[batch] = result
        scale = lax.rsqrt(jnp.mean(result * result, axis=1, keepdims=True) + EPS)
        rows_all[batch, core] = (result * scale * gain_rows[1:2]).astype(BF16)
        to_pair(7 + batch, rows_all.at[batch, core], rows_all.at[batch, core]).start()
        return carry

    lax.fori_loop(0, 2, join, 0)
    keep_ffn = keep(3, rows_all, ffn_out)

    def feed_forward(result, back, saved):
        last = CHUNKS - 3

        def save(chunk, batch, half):
            return keep(4 + batch, saved.at[batch], saved_out.at[chunk, batch, half])

        def lend(batch):
            return (
                to_pair(10 + batch, cots.at[batch, 1 - core], lent.at[0, batch]),
                to_pair(12 + batch, rows_all.at[batch, 1 - core], lent.at[1, batch]),
            )

        result[...] = jnp.zeros_like(result)
        back[...] = jnp.zeros_like(back)

        def chunk_step(chunk, carry):
            def block(part, inner):
                batch = part % 2
                own = (part < 2) != (chunk == last)
                half = jnp.where(own, core, 1 - core)
                for turn in range(2):

                    @pl.when((part == 2 * turn) & (chunk < LATER))
                    def _():
                        gather.tick(EAGER + SPREAD + chunk, ((0, 2), (1,))[turn])

                @pl.when((chunk == 0) & (part >= 2))
                def _():
                    to_pair(
                        7 + batch, rows_all.at[batch, core], rows_all.at[batch, 1 - core]
                    ).wait_recv()

                @pl.when((chunk == 1) & (part == 0))
                def _():
                    keep_ffn.start()

                @pl.when((chunk == last) & (part == 0))
                def _():
                    keep_w.wait()
                    keep_gain.wait()
                    for each in range(2):
                        swap_mixed(each).wait_send()
                    keep_ffn.wait()
                    keep_cot.wait()

                @pl.when((chunk > 0) | (part > 1))
                def _():
                    save(chunk, batch, half).wait()

                up_weights = full[chunk + 2, :, :, :, :, 0:512].reshape(1024, 512)
                down_weights = full[chunk + 2, :, :, :, :, 512:768].reshape(1024, 256)
                for piece in range(2):
                    rows = pl.ds(256 * piece, 256)
                    both = contract(rows_all[batch, half, rows, :], up_weights, 1, 0)
                    grad = contract(cots[batch, half, rows, :], down_weights, 1, 0)
                    gate, up = both[:, 0:256], both[:, 256:512]
                    bend = 1.0 / (1.0 + jnp.exp(-gate))
                    silu = gate * bend
                    active = (silu * up).astype(BF16)
                    grad_up = (grad * silu).astype(BF16)
                    grad_gate = (grad * up * bend * (1.0 + gate * (1.0 - bend))).astype(BF16)
                    saved[batch, rows, 0:256] = grad_gate
                    saved[batch, rows, 256:512] = grad_up
                    saved[batch, rows, 512:768] = active
                    result[batch, half, rows, :] += contract(active, down_weights, 1, 1)
                    pulled = jnp.concatenate([grad_gate, grad_up], axis=1)
                    back[batch, half, rows, :] += contract(pulled, up_weights, 1, 1)
                save(chunk, batch, half).start()

                @pl.when((chunk == last) & (part < 2))
                def _():
                    cots[batch, half] = result[batch, half].astype(BF16)
                    rows_all[batch, half] = back[batch, half].astype(BF16)
                    for copy in lend(batch):
                        copy.start()

                return inner

            lax.fori_loop(0, 4, block, 0)
            return carry

        lax.fori_loop(0, CHUNKS - 2, chunk_step, 0)

        def give_branch(batch, side):
            columns = pl.ds(512 * side, 512)
            return to_pair(
                14 + 2 * batch + side, cots.at[batch, core, :, columns], mixed.at[batch, columns, :]
            )

        def keep_branch(batch, side):
            columns = pl.ds(512 * side, 512)
            target = branch_out.at[batch, 1 - core, :, columns]
            return keep(8 + 2 * batch + side, mixed.at[batch, columns, :], target)

        def ends(batch):
            return (
                keep(batch, lent.at[0, batch], result_out.at[batch]),
                keep(2 + batch, attended.at[batch], kept_out.at[batch]),
                keep(6 + batch, cots.at[batch, core], branch_out.at[batch, core]),
            )

        def close(batch, carry):
            for copy in lend(batch):
                copy.wait_recv()
            joined = attended[batch]
            outputs = joined + result[batch, core] + lent[0, batch].astype(F32)
            lent[0, batch] = outputs.astype(BF16)
            scale = lax.rsqrt(jnp.mean(joined * joined, axis=1, keepdims=True) + EPS)
            unit = joined * scale
            pulled = (back[batch, core] + lent[1, batch].astype(F32)) * gain_rows[1:2]
            shared = jnp.mean(pulled * unit, axis=1, keepdims=True)
            total = cots[batch, core].astype(F32) + scale * (pulled - unit * shared)
            attended[batch] = total
            cots[batch, core] = total.astype(BF16)
            for side in range(2):
                give_branch(batch, side).start()
            for copy in ends(batch):
                copy.start()
            return carry

        lax.fori_loop(0, 2, close, 0)
        for batch in range(2):
            for side in range(2):
                give_branch(batch, side).wait_recv()
                keep_branch(batch, side).start()
        for batch in range(2):
            save(last, batch, core).wait()
            for copy in ends(batch):
                copy.wait()
            for side in range(2):
                keep_branch(batch, side).wait()
                give_branch(batch, side).wait_send()
            for copy in lend(batch):
                copy.wait_send()

    pl.run_scoped(
        feed_forward,
        pltpu.VMEM((2, 2, 512, 1024), F32),
        pltpu.VMEM((2, 2, 512, 1024), F32),
        pltpu.VMEM((2, 512, WIDE), BF16),
    )
    for number, chunks in ((0, first), (18, later)):
        whole = full.at[chunks, z, y, x, mine, :]
        to_pair(number, whole, whole).wait_send()
    give_seg.wait_send()
    for batch in range(2):
        to_pair(7 + batch, rows_all.at[batch, core], rows_all.at[batch, core]).wait_send()
    give_tile.wait_send()
    give_cot.wait_send()
    gather.drain()


def forward_call(weights, tile, inputs, cotangent, segments, gains):
    rows = inputs.shape[1]
    counter = np.arange(128) % 32
    inverse = jnp.asarray(THETA ** (-2.0 * counter / 64), F32)[None]
    shapes = [
        ((2, 4, 2, 2, 64, WIDE), BF16),
        ((2, SEQ, 1024), BF16),
        ((2, SEQ, WIDE), BF16),
        ((2, SEQ, 1024), BF16),
        ((2, SEQ, 256), F32),
        ((2, SEQ, SEQ), BF16),
        ((2, 8, SEQ), F32),
        ((2, SEQ, 512), BF16),
        ((2, 2, rows, 1024), BF16),
        ((2, 2, rows, 1024), BF16),
        ((CHUNKS - 2, 2, 2, rows, WIDE), BF16),
        ((2, rows, 1024), BF16),
        ((2, 2, rows, 1024), BF16),
        ((2, rows, 1024), F32),
        ((8, 1024), F32),
    ]
    anywhere = pl.BlockSpec(memory_space=pl.ANY)
    inside = pl.BlockSpec(memory_space=pltpu.VMEM)
    return pl.pallas_call(
        forward_kernel,
        out_shape=[jax.ShapeDtypeStruct(*shape) for shape in shapes],
        in_specs=[anywhere] * (len(weights) + 4) + [inside] * 2,
        out_specs=[anywhere] * len(shapes),
        scratch_shapes=[
            pltpu.VMEM((CHUNKS, 4, 2, 2, 64, WIDE), BF16),
            pltpu.VMEM((4, 2, 2, 2, 8, 128), F32),
            pltpu.VMEM((8, 1024), F32),
            pltpu.VMEM((2, 2, rows, 1024), BF16),
            pltpu.VMEM((2, 2, rows, 1024), BF16),
            pltpu.VMEM((2, 2, 1, rows), F32),
            pltpu.VMEM((2, SEQ, 512), BF16),
            pltpu.VMEM((2, rows, 512), BF16),
            pltpu.VMEM((4, 2, 2, 64, 512), BF16),
            pltpu.VMEM((2, rows, 1024), F32),
            pltpu.VMEM((2, 2, rows, 1024), BF16),
            pltpu.SemaphoreType.DMA((12,)),
            pltpu.SemaphoreType.DMA((19,)),
            pltpu.SemaphoreType.DMA((19,)),
        ]
        + semaphores(),
        compiler_params=params(0),
        name="forward",
    )(*weights, tile, inputs, cotangent, segments.astype(F32)[:, None, :], gains, inverse)


def pack_gains(attn_gain, ffn_gain):
    count = attn_gain.shape[0]
    slot = lax.axis_index("fsdp") % (128 // count)
    pair = jnp.stack([attn_gain, ffn_gain]).astype(F32)
    place_of = (jnp.arange(128 // count) == slot).astype(F32)
    spread = (place_of[None, :, None] * pair[:, None, :]).reshape(2, 128)
    return jnp.concatenate([spread, jnp.zeros((6, 128), F32)])


def backward_kernel(*refs):
    (
        w_in, normed_in, raw_in, qkv_in, table_in, mask_in, total_in, mix_in, ffn_in, cot_in,
        saved_in, branch_in, kept_in, x_in, gain_rows, head_gains,
    ) = refs[:16]
    grad_out, sums_out, head_out = refs[16:19]
    sums = refs[19]
    lands = (refs[20:24], refs[24:28], refs[28:32])
    (
        totals, pair_land, rows_all, cots, saved, branch, grads, qkv, raw, table, total, mask, mixed,
        grad_mixed, wo, keys, values, key_sum, value_sum, head_sum, head_land, kept,
        local, pair_sent, pair_landed, head_sent, head_landed, sent, landed,
    ) = refs[32:]
    me, z, y, x, core = place()
    mine, other = pair_rows(core)
    scatter = Scatter(sums, lands, totals, sent, landed)

    def to_pair(number, source, target):
        return pltpu.make_async_remote_copy(
            src_ref=source,
            dst_ref=target,
            send_sem=pair_sent.at[number],
            recv_sem=pair_landed.at[number],
            device_id=(me ^ 1,),
            device_id_type=MESH,
        )

    def load(number, source, target):
        return pltpu.make_async_copy(source, target, local.at[number])

    loads = [
        load(2, saved_in.at[0], saved),
        load(0, ffn_in, rows_all),
        load(1, cot_in, cots),
        load(3, branch_in, branch),
        load(4, w_in.at[1, :, :, pl.ds(256, 512)], wo),
        load(5, mix_in, mixed),
    ]
    def batch_loads(batch):
        return (
            load(6, qkv_in.at[batch], qkv),
            load(7, raw_in.at[batch], raw),
            load(8, table_in.at[batch], table),
            load(9, total_in.at[batch], total),
            load(10, mask_in.at[batch], mask),
        )

    for copy in loads[:3]:
        copy.start()
    greet(me, z, 16)
    head_sum[...] = jnp.zeros_like(head_sum)

    def put(slot, columns, left, right):
        product = contract(left, right, 0, 0).astype(BF16)
        sums[slot, :, :, :, :, columns] = product.reshape(4, 2, 2, 64, columns.size)

    def up_terms(chunk):
        slot = lax.rem(chunk, SUM_SLOTS)
        flat = saved[:, :, :, 0:512].reshape(2048, 512)
        put(slot, pl.ds(0, 512), rows_all[...].reshape(2048, 1024), flat)

    def down_terms(chunk):
        slot = lax.rem(chunk, SUM_SLOTS)
        flat = saved[:, :, :, 512:768].reshape(2048, 256)
        put(slot, pl.ds(512, 256), cots[...].reshape(2048, 1024), flat)

    loads[0].wait()
    loads[1].wait()
    up_terms(0)
    loads[2].wait()
    down_terms(0)
    load(2, saved_in.at[1], saved).start()
    for copy in loads[3:]:
        copy.start()
    for copy in batch_loads(0):
        copy.start()
    def mixed_back(half, carry):
        product = contract(branch[half].reshape(1024, 1024), wo[...].reshape(1024, 512), 1, 0)
        grad_mixed[half] = product.astype(BF16)
        return carry

    def pull_back(grad, span, columns, gain, number):
        plain = raw[span, columns].astype(F32)
        width = plain.shape[1]
        row = lax.broadcasted_iota(jnp.int32, (width, width), 0) // 64
        column = lax.broadcasted_iota(jnp.int32, (width, width), 1) // 64
        ones = jnp.where(row == column, 1.0 / 64.0, 0.0).astype(BF16)
        level = lax.rsqrt(contract((plain * plain).astype(BF16), ones, 1, 0) + EPS)
        unit = plain * level
        turned = grad * table[span, 0:128] - half_turn(grad) * table[span, 128:256]
        terms = turned * unit
        head_sum[number] += jnp.sum(terms.reshape(-1, 8, width), axis=0)
        scaled = terms * gain
        shared = contract(scaled.astype(BF16), ones, 1, 0)
        return level * (turned * gain - unit * shared)

    def sides(pair, parity):
        low = lane_index(pair.shape) < 64
        rows = pair.astype(F32)
        first, second = jnp.where(low, rows, 0.0), jnp.where(low, 0.0, rows)
        if parity == 0:
            second = pltpu.roll(second, 64, 1)
        else:
            first = pltpu.roll(first, 64, 1)
        return first.astype(BF16), second.astype(BF16)

    def attend_back(batch, couple, parity):
        key_pair = qkv[:, pl.ds(pl.multiple_of(512 + couple * 128, 128), 128)].astype(F32)
        value_pair = qkv[:, pl.ds(pl.multiple_of(768 + couple * 128, 128), 128)].astype(F32)
        for target, pair in ((keys, key_pair), (values, value_pair)):
            low, high = split_pair(pair, parity)
            target[0] = low.astype(BF16)
            target[1] = high.astype(BF16)
        if parity == 0:
            key_sum[...] = jnp.zeros_like(key_sum)
            value_sum[...] = jnp.zeros_like(value_sum)
        group = couple * 2 + parity
        picks = lax.broadcasted_iota(jnp.int32, (8, 128), 0) == lane_index((8, 128)) // 64
        picks = jnp.where(picks, 1.0, 0.0).astype(BF16)
        for quarter in range(4):
            span = pl.ds(quarter * 256, 256)
            width = (quarter + 1) * 256
            allowed = mask[0:width, span].astype(F32)
            queries = qkv[span, lanes_at(group, 128)]
            pulled = grad_mixed[batch, span, lanes_at(group, 128)]
            product = pulled.astype(F32) * mixed[batch, span, lanes_at(group, 128)].astype(F32)
            coarse = product.astype(BF16)
            rest = (product - coarse.astype(F32)).astype(BF16)
            centers = contract(picks, coarse, 1, 1) + contract(picks, rest, 1, 1)
            query_sides, pulled_sides = sides(queries, parity), sides(pulled, parity)
            levels = [total[pl.ds(2 * group + side, 1), span] for side in range(2)]
            scores = contract(keys[:, 0:width, :].reshape(2 * width, 128), queries, 1, 1)
            grad_probs = contract(values[:, 0:width, :].reshape(2 * width, 128), pulled, 1, 1)
            low_probs, grad_scores = [], []
            for side in range(2):
                rows = slice(side * width, side * width + width)
                probs = jnp.exp(scores[rows]) * allowed * levels[side]
                low_probs.append(probs.astype(BF16))
                grad_scores.append((probs * (grad_probs[rows] - centers[side : side + 1])).astype(BF16))
            stacked = jnp.concatenate(grad_scores, axis=0)
            grad_query = contract(stacked, keys[:, 0:width, :].reshape(2 * width, 128), 0, 0)
            wide = jnp.concatenate(grad_scores, axis=1)
            grad_key = contract(wide, jnp.concatenate(query_sides, axis=0), 1, 0)
            wide = jnp.concatenate(low_probs, axis=1)
            grad_value = contract(wide, jnp.concatenate(pulled_sides, axis=0), 1, 0)
            key_sum[0:width, :] += grad_key
            value_sum[0:width, :] += grad_value
            grad_raw = pull_back(
                grad_query * 0.125, span, lanes_at(group, 128), head_gains[:, 0:128], 0
            )
            grads[batch, span, lanes_at(group, 128)] = grad_raw.astype(BF16)
        if parity == 1:
            whole = pl.ds(0, SEQ)
            columns = pl.ds(pl.multiple_of(512 + couple * 128, 128), 128)
            grad_raw = pull_back(key_sum[...], whole, columns, head_gains[:, 512:640], 1)
            grads[batch, :, columns] = grad_raw.astype(BF16)
            columns = pl.ds(pl.multiple_of(768 + couple * 128, 128), 128)
            grads[batch, :, columns] = value_sum[...].astype(BF16)

    def head_copy(step):
        bit = (1, 2, 4, 8, 16)[step]
        return pltpu.make_async_remote_copy(
            src_ref=head_sum,
            dst_ref=head_land.at[step],
            send_sem=head_sent.at[step],
            recv_sem=head_landed.at[step],
            device_id=(me ^ bit,),
            device_id_type=MESH,
        )

    def send_heads(step):
        if step > 0:
            head_copy(step - 1).wait()
            head_sum[...] += head_land[step - 1]
        if step < 5:
            head_copy(step).start()

    def near_normed(batch, half):
        part = grads[batch, pl.ds(pl.multiple_of(half * 512, 512), 512), :]
        first = contract(part[:, 0:768], saved[0].reshape(1024, WIDE), 1, 1)
        value_weights = saved[1].reshape(1024, WIDE)[:, 0:256]
        return first + contract(part[:, 768:1024], value_weights, 1, 1)

    def work(time):
        @pl.when(time == 0)
        def _():
            for copy in loads[3:]:
                copy.wait()
            lax.fori_loop(0, 2, mixed_back, 0)

        @pl.when((time >= 1) & (time <= 8))
        def _():
            unit = time - 1
            batch, couple, parity = unit // 4, (unit // 2) % 2, unit % 2

            @pl.when(unit % 4 == 0)
            def _():
                for copy in batch_loads(batch):
                    copy.wait()

            for each in range(2):

                @pl.when(parity == each)
                def _():
                    attend_back(batch, couple, each)

            @pl.when(unit == 3)
            def _():
                for copy in batch_loads(1):
                    copy.start()

        for step in range(6):

            @pl.when(time == 9 + step)
            def _():
                send_heads(step)

        @pl.when(time == 10)
        def _():
            load(2, w_in, saved).wait()
            load(7, x_in, cots.at[1]).start()
            load(6, kept_in.at[0], kept).start()
            lend(0)

        @pl.when((time == 12) | (time == 13))
        def _():
            batch = time - 12
            swap(batch).wait()
            load(6, kept_in.at[batch], kept).wait()

            @pl.when(batch == 0)
            def _():
                load(7, x_in, cots.at[1]).wait()

            rows = cots[1, batch].astype(F32)
            scale = lax.rsqrt(jnp.mean(rows * rows, axis=1, keepdims=True) + EPS)
            unit = rows * scale
            pulled = near_normed(batch, core) + pair_land[batch].astype(F32)
            pulled = pulled * gain_rows[0:1]
            shared = jnp.mean(pulled * unit, axis=1, keepdims=True)
            grad = kept[...] + scale * (pulled - unit * shared)
            cots[0, batch] = grad.astype(BF16)
            store_grad(batch).start()

            @pl.when(batch == 0)
            def _():
                load(6, kept_in.at[1], kept).start()

    def swap(batch):
        return to_pair(1 + batch, cots.at[0, batch], pair_land.at[batch])

    def lend(batch):
        cots[0, batch] = near_normed(batch, 1 - core).astype(BF16)
        swap(batch).start()

    def store_grad(batch):
        return load(8 + batch, cots.at[0, batch], grad_out.at[batch])

    def hand(number, chunks, half):
        return to_pair(
            3 + number, totals.at[chunks, other, :], sums_out.at[half, chunks]
        )

    def own_sums(number, chunks):
        return load(3 + number, totals.at[chunks, mine, :], sums_out.at[core, chunks])

    def next_terms(time):
        @pl.when(time + 1 < CHUNKS - 2)
        def _():
            load(2, saved_in.at[0], saved).wait()
            up_terms(time + 1)
            down_terms(time + 1)

        @pl.when(time + 2 < CHUNKS - 2)
        def _():
            load(2, saved_in.at[time + 2], saved).start()

        @pl.when(time == CHUNKS - 4)
        def _():
            load(0, normed_in, rows_all).start()
            load(2, w_in, saved).start()

        @pl.when(time == CHUNKS - 3)
        def _():
            load(0, normed_in, rows_all).wait()
            slot = (CHUNKS - 2) % SUM_SLOTS
            put(slot, pl.ds(0, 768), rows_all[...].reshape(2048, 1024), grads[:, :, 0:768].reshape(2048, 768))

        @pl.when(time == CHUNKS - 2)
        def _():
            slot = (CHUNKS - 1) % SUM_SLOTS
            put(slot, pl.ds(0, 256), rows_all[...].reshape(2048, 1024), grads[:, :, 768:1024].reshape(2048, 256))
            put(slot, pl.ds(256, 512), branch[...].reshape(2048, 1024), mixed[...].reshape(2048, 512))

        @pl.when(time == 10)
        def _():
            lend(1)

        @pl.when(time == CHUNKS + 3)
        def _():
            hand(0, pl.ds(2, CHUNKS - 2), core).start()
            own_sums(0, pl.ds(2, CHUNKS - 2)).start()

    def body(time, carry):
        scatter.tick(time, (0, 2))
        work(time)
        scatter.tick(time, (1,))
        next_terms(time)
        return carry

    lax.fori_loop(0, CHUNKS + 5, body, 0)
    head_store = load(7, head_sum, head_out)
    head_store.start()
    hand(1, pl.ds(0, 2), core).start()
    own_sums(1, pl.ds(0, 2)).start()
    for number, chunks in ((0, pl.ds(2, CHUNKS - 2)), (1, pl.ds(0, 2))):
        hand(number, chunks, core).wait_send()
        hand(number, chunks, 1 - core).wait_recv()
        own_sums(number, chunks).wait()
    for batch in range(2):
        store_grad(batch).wait()
    head_store.wait()


def backward_call(forward, inputs, gains):
    rows = inputs.shape[1]
    (
        w, normed, raw, qkv, table, mask, total, mix, ffn, cot, saved, _, branch, kept, gain_rows,
    ) = forward
    anywhere = pl.BlockSpec(memory_space=pl.ANY)
    inside = pl.BlockSpec(memory_space=pltpu.VMEM)
    return pl.pallas_call(
        backward_kernel,
        out_shape=[
            jax.ShapeDtypeStruct((2, rows, 1024), BF16),
            jax.ShapeDtypeStruct((2, CHUNKS, 32, WIDE), F32),
            jax.ShapeDtypeStruct((2, 8, 128), F32),
        ],
        in_specs=[anywhere] * 14 + [inside] * 2,
        out_specs=[anywhere] * 3,
        scratch_shapes=[pltpu.VMEM((SUM_SLOTS, 4, 2, 2, 64, WIDE), BF16)]
        + land_shapes()
        + [
            pltpu.VMEM((CHUNKS, 64, WIDE), F32),
            pltpu.VMEM((2, rows, 1024), BF16),
            pltpu.VMEM((2, 2, rows, 1024), BF16),
            pltpu.VMEM((2, 2, rows, 1024), BF16),
            pltpu.VMEM((2, 2, rows, WIDE), BF16),
            pltpu.VMEM((2, 2, rows, 1024), BF16),
            pltpu.VMEM((2, SEQ, 1024), BF16),
            pltpu.VMEM((SEQ, 1024), BF16),
            pltpu.VMEM((SEQ, WIDE), BF16),
            pltpu.VMEM((SEQ, 256), F32),
            pltpu.VMEM((8, SEQ), F32),
            pltpu.VMEM((SEQ, SEQ), BF16),
            pltpu.VMEM((2, SEQ, 512), BF16),
            pltpu.VMEM((2, SEQ, 512), BF16),
            pltpu.VMEM((2, 512, 512), BF16),
            pltpu.VMEM((2, SEQ, 128), BF16),
            pltpu.VMEM((2, SEQ, 128), BF16),
            pltpu.VMEM((SEQ, 128), F32),
            pltpu.VMEM((SEQ, 128), F32),
            pltpu.VMEM((2, 8, 128), F32),
            pltpu.VMEM((5, 2, 8, 128), F32),
            pltpu.VMEM((rows, 1024), F32),
            pltpu.SemaphoreType.DMA((11,)),
            pltpu.SemaphoreType.DMA((5,)),
            pltpu.SemaphoreType.DMA((5,)),
            pltpu.SemaphoreType.DMA((5,)),
            pltpu.SemaphoreType.DMA((5,)),
        ]
        + semaphores(),
        compiler_params=params(1),
        name="backward",
    )(
        w.reshape(2, 2, rows, WIDE), normed.reshape(2, 2, rows, 1024), raw, qkv, table, mask, total,
        mix, ffn, cot, saved, branch, kept, inputs, gain_rows, gains,
    )


def unpack(out):
    def both(chunk, start, stop):
        return jnp.concatenate([out[0, chunk, :, start:stop], out[1, chunk, :, start:stop]], axis=1)

    def wide_of(start):
        return out[:, 2:, :, start : start + 256].transpose(2, 0, 1, 3).reshape(out.shape[2], -1)

    return (
        both(0, 0, 512),
        both(0, 512, 768),
        both(1, 0, 256),
        both(1, 256, 768),
        wide_of(0),
        wide_of(256),
        wide_of(512),
    )


def gain_terms(gain, weights, grads):
    total = sum(jnp.sum(w.astype(F32) * g, axis=1) for w, g in zip(weights, grads))
    return total / gain.astype(F32)


def local_grid(
    inputs,
    segments,
    attn_gain,
    w_query,
    key_projection,
    value_projection,
    w_output,
    query_gain,
    key_norm_gain,
    ffn_gain,
    w_gate,
    w_up,
    w_down,
    cotangent,
):
    attn_weights = (w_query, key_projection, value_projection)
    weights = attn_weights + (w_output.T, w_gate, w_up, w_down.T)
    gains = [query_gain] * 8 + [key_norm_gain] * 4
    gains = jnp.concatenate(gains).astype(F32)[None]
    forward = forward_call(
        weights, pack_gains(attn_gain, ffn_gain), inputs, cotangent, segments, gains
    )
    input_grad, sums, heads = backward_call(forward, inputs, gains)
    query, key, value, output_t, gate, up, down_t = unpack(sums)
    heads = jnp.sum(heads, axis=1)
    heads = heads[:, :64] + heads[:, 64:]
    return (
        forward[11],
        input_grad,
        gain_terms(attn_gain, attn_weights, (query, key, value)),
        query,
        key,
        value,
        output_t.T,
        heads[0],
        heads[1],
        gain_terms(ffn_gain, (w_gate, w_up), (gate, up)),
        gate,
        up,
        down_t.T,
    )


def from_behind(block, axis, distance):
    devices = range(lax.axis_size(axis))
    route = [(i - distance, i) for i in devices if i - distance in devices]
    return lax.ppermute(block, axis, route)


def row_norm(values, gain_row):
    return values * lax.rsqrt(jnp.mean(values * values, axis=-1, keepdims=True) + EPS) * gain_row


def angles(places, head_width):
    counter = jnp.arange(head_width // 2, dtype=jnp.float32)
    inverse = jnp.power(jnp.float32(THETA), -2.0 * counter / head_width)
    turned = places.astype(jnp.float32)[:, None] * inverse[None, :]
    return (jnp.cos(turned), jnp.sin(turned))


def prepare_inputs(raw_rows, gain_row, cosine_table, sine_table_rows, head_count):
    token_count = raw_rows.shape[0]
    head_width = gain_row.shape[0]
    split_rows = raw_rows.reshape(token_count, head_count, head_width)
    normed = row_norm(split_rows, gain_row)
    first_half = normed[..., : head_width // 2]
    second = normed[..., head_width // 2 :]
    cos_rows = cosine_table[:, None, :]
    sin_rows = sine_table_rows[:, None, :]
    turned = jnp.concatenate(
        [first_half * cos_rows - second * sin_rows, second * cos_rows + first_half * sin_rows],
        axis=-1,
    )
    return turned.reshape(token_count, head_count * head_width)


def plain_product(left_rows, right_rows):
    return jnp.dot(left_rows, right_rows, preferred_element_type=jnp.float32)


def rows_product(left_rows, right_rows):
    return lax.dot_general(
        left_rows, right_rows, (((0,), (0,)), ((), ())), preferred_element_type=jnp.float32
    )


def cols_product(left_rows, right_rows):
    return lax.dot_general(
        left_rows, right_rows, (((1,), (1,)), ((), ())), preferred_element_type=jnp.float32
    )


def silu_product(gate_raw, upward):
    return gate_raw * jax.nn.sigmoid(gate_raw) * upward


def add_sets(former_set, latter_set):
    if former_set is None:
        return latter_set
    return tuple((former + latter for former, latter in zip(former_set, latter_set)))


def local(
    inputs,
    segments,
    attn_gain,
    w_query,
    key_projection,
    value_projection,
    w_output,
    query_gain,
    key_norm_gain,
    ffn_gain,
    w_gate,
    w_up,
    w_down,
    cotangent,
):
    batches = inputs.shape[0]
    tokens = inputs.shape[1]
    head_width = query_gain.shape[0]
    query_width = w_query.shape[1]
    kv_width = key_projection.shape[1]
    query_head_rows = query_width // head_width
    kv_heads = kv_width // head_width
    heads_per_group = query_head_rows // kv_heads
    scale = 1.0 / math.sqrt(head_width)
    query_gain_f = query_gain.astype(jnp.float32)
    key_gain_f = key_norm_gain.astype(jnp.float32)
    device_index = lax.axis_index("fsdp")
    places_row = jnp.arange(tokens, dtype=jnp.int32)
    causal = places_row[None, :] <= places_row[:, None]
    same_run = device_index * tokens // SEQ == (device_index - 1) * tokens // SEQ
    outputs_list = []
    grads_list = []
    shard_sums = None
    gain_sums = None
    for batch_index in range(batches):
        gathered = (
            lax.all_gather(attn_gain, "fsdp", axis=0, tiled=True),
            lax.all_gather(w_query, "fsdp", axis=0, tiled=True),
            lax.all_gather(key_projection, "fsdp", axis=0, tiled=True),
            lax.all_gather(value_projection, "fsdp", axis=0, tiled=True),
            lax.all_gather(w_output, "fsdp", axis=1, tiled=True),
            lax.all_gather(ffn_gain, "fsdp", axis=0, tiled=True),
            lax.all_gather(w_gate, "fsdp", axis=0, tiled=True),
            lax.all_gather(w_up, "fsdp", axis=0, tiled=True),
            lax.all_gather(w_down, "fsdp", axis=1, tiled=True),
        )
        (
            gain_attn,
            full_query,
            full_key,
            full_value,
            full_output,
            gain_ffn,
            full_gate,
            full_up,
            full_down,
        ) = gathered
        hidden = inputs[batch_index].astype(jnp.float32)
        segment = segments[batch_index]
        normed_f, norm_pull = jax.vjp(row_norm, hidden, gain_attn.astype(jnp.float32))
        normed = normed_f.astype(jnp.bfloat16)
        query_raw = plain_product(normed, full_query)
        key_projected = plain_product(normed, full_key)
        value_reduced = plain_product(normed, full_value).astype(jnp.bfloat16)
        lower_count = jnp.sum((segment[None, :] < segment[:, None]).astype(jnp.int32), axis=1)
        local_places = places_row - lower_count
        cos_local, sin_local = angles(local_places, head_width)
        key_sent = prepare_inputs(key_projected, key_gain_f, cos_local, sin_local, kv_heads).astype(
            jnp.bfloat16
        )
        remote_key, remote_value, remote_segment = from_behind(
            (key_sent, value_reduced, segment.astype(jnp.bfloat16)), "fsdp", 1
        )
        remote_match = (remote_segment.astype(jnp.int32)[None, :] == segment[:, None]) & same_run
        places_all = local_places + jnp.sum(remote_match.astype(jnp.int32), axis=1)
        cosine_table, sine_table_rows = angles(places_all, head_width)
        query_f, query_pull = jax.vjp(
            lambda raw_rows, gain_row: prepare_inputs(
                raw_rows, gain_row, cosine_table, sine_table_rows, query_head_rows
            ),
            query_raw,
            query_gain_f,
        )
        key_f, key_pull = jax.vjp(
            lambda raw_rows, gain_row: prepare_inputs(
                raw_rows, gain_row, cosine_table, sine_table_rows, kv_heads
            ),
            key_projected,
            key_gain_f,
        )
        query_low = query_f.astype(jnp.bfloat16)
        key_low = key_f.astype(jnp.bfloat16)
        allowed = jnp.concatenate(
            [remote_match, causal & (segment[None, :] == segment[:, None])], axis=1
        )
        query_split = query_low.reshape(tokens, kv_heads, heads_per_group, head_width).transpose(
            1, 0, 2, 3
        )
        key_split = (
            jnp.concatenate([remote_key, key_low], axis=0)
            .reshape(2 * tokens, kv_heads, head_width)
            .transpose(1, 0, 2)
        )
        value_split = (
            jnp.concatenate([remote_value, value_reduced], axis=0)
            .reshape(2 * tokens, kv_heads, head_width)
            .transpose(1, 0, 2)
        )

        def head_forward(blocks):
            query_part, key_part, value_part = blocks
            scores = (
                jnp.einsum("tgd,ld->gtl", query_part, key_part, preferred_element_type=jnp.float32)
                * scale
            )
            scores = jnp.where(allowed[None], scores, NEG)
            row_peak = jnp.max(scores, axis=-1, keepdims=True)
            raised = jnp.exp(scores - row_peak)
            row_total = jnp.sum(raised, axis=-1, keepdims=True)
            prob_rows = (raised / row_total).astype(jnp.bfloat16)
            mixed_part = jnp.einsum(
                "gtl,ld->tgd", prob_rows, value_part, preferred_element_type=jnp.float32
            )
            return (mixed_part.astype(jnp.bfloat16), (row_peak + jnp.log(row_total))[..., 0])

        mixed_split, log_totals = lax.map(head_forward, (query_split, key_split, value_split))
        attn_mix = mixed_split.transpose(1, 0, 2, 3).reshape(tokens, query_width)
        attended = hidden + plain_product(attn_mix, full_output)
        ffn_f, ffn_pull = jax.vjp(row_norm, attended, gain_ffn.astype(jnp.float32))
        ffn_in = ffn_f.astype(jnp.bfloat16)
        gate_raw = plain_product(ffn_in, full_gate)
        upward = plain_product(ffn_in, full_up)
        active_f, active_pull = jax.vjp(silu_product, gate_raw, upward)
        active = active_f.astype(jnp.bfloat16)
        result = attended + plain_product(active, full_down)
        outputs_list.append(result.astype(jnp.bfloat16))
        back_query, back_key, back_value, back_output, back_gate, back_up, back_down = (
            lax.all_gather(w_query, "fsdp", axis=0, tiled=True),
            lax.all_gather(key_projection, "fsdp", axis=0, tiled=True),
            lax.all_gather(value_projection, "fsdp", axis=0, tiled=True),
            lax.all_gather(w_output, "fsdp", axis=1, tiled=True),
            lax.all_gather(w_gate, "fsdp", axis=0, tiled=True),
            lax.all_gather(w_up, "fsdp", axis=0, tiled=True),
            lax.all_gather(w_down, "fsdp", axis=1, tiled=True),
        )
        grad_result = cotangent[batch_index]
        grad_down_t = rows_product(grad_result, active)
        grad_active = cols_product(grad_result, back_down)
        grad_gate_f, grad_up_f = active_pull(grad_active)
        grad_gate_low = grad_gate_f.astype(jnp.bfloat16)
        grad_up_low = grad_up_f.astype(jnp.bfloat16)
        grad_gate_w = rows_product(ffn_in, grad_gate_low)
        grad_up_w = rows_product(ffn_in, grad_up_low)
        grad_ffn_in = cols_product(grad_gate_low, back_gate) + cols_product(grad_up_low, back_up)
        grad_attended_norm, grad_ffn_gain = ffn_pull(grad_ffn_in)
        grad_attended = grad_result.astype(jnp.float32) + grad_attended_norm
        grad_branch = grad_attended.astype(jnp.bfloat16)
        grad_output_t = rows_product(grad_branch, attn_mix)
        grad_mixed = cols_product(grad_branch, back_output).astype(jnp.bfloat16)
        grad_split = grad_mixed.reshape(tokens, kv_heads, heads_per_group, head_width).transpose(
            1, 0, 2, 3
        )

        def head_backward(blocks):
            query_part, key_part, value_part, grad_part, log_part = blocks
            scores = (
                jnp.einsum("tgd,ld->gtl", query_part, key_part, preferred_element_type=jnp.float32)
                * scale
            )
            scores = jnp.where(allowed[None], scores, NEG)
            prob_rows = jnp.exp(scores - log_part[..., None])
            grad_probs = jnp.einsum(
                "tgd,ld->gtl", grad_part, value_part, preferred_element_type=jnp.float32
            )
            center = jnp.sum(prob_rows * grad_probs, axis=-1, keepdims=True)
            grad_scores = (prob_rows * (grad_probs - center)).astype(jnp.bfloat16)
            grad_query_part = (
                jnp.einsum("gtl,ld->tgd", grad_scores, key_part, preferred_element_type=jnp.float32)
                * scale
            )
            grad_key_part = (
                jnp.einsum(
                    "gtl,tgd->ld", grad_scores, query_part, preferred_element_type=jnp.float32
                )
                * scale
            )
            grad_value_part = jnp.einsum(
                "gtl,tgd->ld",
                prob_rows.astype(jnp.bfloat16),
                grad_part,
                preferred_element_type=jnp.float32,
            )
            return (grad_query_part, grad_key_part, grad_value_part)

        grad_query_split, grad_key_split, grad_value_split = lax.map(
            head_backward, (query_split, key_split, value_split, grad_split, log_totals)
        )
        grad_query_rot = grad_query_split.transpose(1, 0, 2, 3).reshape(tokens, query_width)
        grad_key_all = grad_key_split.transpose(1, 0, 2).reshape(2 * tokens, kv_width)
        grad_value_all = grad_value_split.transpose(1, 0, 2).reshape(2 * tokens, kv_width)
        back_key_grad, back_value_grad = (
            from_behind(grad_key_all[:tokens].astype(jnp.bfloat16), "fsdp", -1).astype(jnp.float32),
            from_behind(grad_value_all[:tokens].astype(jnp.bfloat16), "fsdp", -1).astype(
                jnp.float32
            ),
        )
        grad_key_rot = grad_key_all[tokens:] + back_key_grad
        grad_value_low = (grad_value_all[tokens:] + back_value_grad).astype(jnp.bfloat16)
        grad_query_raw, grad_query_gain = query_pull(grad_query_rot)
        grad_key_raw, grad_key_gain = key_pull(grad_key_rot)
        grad_query_low = grad_query_raw.astype(jnp.bfloat16)
        grad_key_low = grad_key_raw.astype(jnp.bfloat16)
        grad_query_w = rows_product(normed, grad_query_low)
        grad_key_w = rows_product(normed, grad_key_low)
        grad_value_w = rows_product(normed, grad_value_low)
        grad_normed = (
            cols_product(grad_query_low, back_query)
            + cols_product(grad_key_low, back_key)
            + cols_product(grad_value_low, back_value)
        )
        grad_hidden_norm, grad_attn_gain = norm_pull(grad_normed)
        grads_list.append((grad_attended + grad_hidden_norm).astype(jnp.bfloat16))
        gain_sums = add_sets(gain_sums, (grad_query_gain, grad_key_gain))
        shard_terms = (
            lax.psum_scatter(grad_attn_gain, "fsdp", scatter_dimension=0, tiled=True),
            lax.psum_scatter(grad_query_w, "fsdp", scatter_dimension=0, tiled=True),
            lax.psum_scatter(grad_key_w, "fsdp", scatter_dimension=0, tiled=True),
            lax.psum_scatter(grad_value_w, "fsdp", scatter_dimension=0, tiled=True),
            lax.psum_scatter(grad_output_t, "fsdp", scatter_dimension=0, tiled=True),
            lax.psum_scatter(grad_ffn_gain, "fsdp", scatter_dimension=0, tiled=True),
            lax.psum_scatter(grad_gate_w, "fsdp", scatter_dimension=0, tiled=True),
            lax.psum_scatter(grad_up_w, "fsdp", scatter_dimension=0, tiled=True),
            lax.psum_scatter(grad_down_t, "fsdp", scatter_dimension=0, tiled=True),
        )
        shard_sums = add_sets(shard_sums, shard_terms)
    head_sums = lax.psum((gain_sums[0], gain_sums[1]), "fsdp")
    return (
        jnp.stack(outputs_list),
        jnp.stack(grads_list),
        shard_sums[0],
        shard_sums[1],
        shard_sums[2],
        shard_sums[3],
        shard_sums[4].T,
        head_sums[0],
        head_sums[1],
        shard_sums[5],
        shard_sums[6],
        shard_sums[7],
        shard_sums[8].T,
    )


def solution(mesh):
    return jax.shard_map(
        local_grid if mesh.shape["fsdp"] == 32 else local,
        mesh=mesh,
        in_specs=(
            P(None, "fsdp", None),
            P(None, "fsdp"),
            P("fsdp"),
            P("fsdp", None),
            P("fsdp", None),
            P("fsdp", None),
            P(None, "fsdp"),
            P(),
            P(),
            P("fsdp"),
            P("fsdp", None),
            P("fsdp", None),
            P(None, "fsdp"),
            P(None, "fsdp", None),
        ),
        out_specs=(
            P(None, "fsdp", None),
            P(None, "fsdp", None),
            P("fsdp"),
            P("fsdp", None),
            P("fsdp", None),
            P("fsdp", None),
            P(None, "fsdp"),
            P(),
            P(),
            P("fsdp"),
            P("fsdp", None),
            P("fsdp", None),
            P(None, "fsdp"),
        ),
        check_vma=False,
    )
```

```python
import math

import jax
import jax.numpy as jnp
import numpy as np
from jax import lax
from jax.experimental import pallas as pl
from jax.experimental.pallas import tpu as pltpu
from jax.sharding import PartitionSpec as P

SEQ = 1024


EPS = 1e-05
THETA = 1000000.0
NEG = -1e30


CHUNKS = 11
WIDE = 768
MESH = pl.DeviceIdType.MESH
ALL = slice(None)
F32 = jnp.float32
BF16 = jnp.bfloat16
PARTS = (
    ("A", pl.ds(0, 48), pl.ds(0, 384)),
    ("B", pl.ds(0, 48), pl.ds(384, 384)),
    ("C", pl.ds(48, 16), pl.ds(0, 768)),
)
GAINS = len(PARTS)
OUTWARD = {
    "A": ("z0", "z1", "z2", "y", "x"),
    "B": ("z0", "z1", "z2", "x", "y"),
    "C": ("x", "y", "z0", "z1", "z2"),
}
INWARD = {
    "A": ("x", "y", "z0", "z1", "z2"),
    "B": ("y", "x", "z0", "z1", "z2"),
    "C": ("z0", "z1", "z2", "y", "x"),
}
SUM_SLOTS = 6
HELD = 2
LAND_SLOTS = 3


def place():
    me = lax.axis_index("fsdp")
    return me, me // 8, (me // 4) % 2, (me // 2) % 2, me % 2


def guarded(condition, action):
    if condition is None:
        action()
    else:
        pl.when(condition)(action)


def greet(me, z, far=0):
    gate = pltpu.get_barrier_semaphore()
    for bit in (1, 2, 4):
        pl.semaphore_signal(gate, inc=1, device_id=(me ^ bit,), device_id_type=MESH)

    @pl.when(z > 0)
    def _():
        pl.semaphore_signal(gate, inc=1, device_id=(me - 8,), device_id_type=MESH)

    @pl.when(z < 3)
    def _():
        pl.semaphore_signal(gate, inc=1, device_id=(me + 8,), device_id_type=MESH)

    if far:
        pl.semaphore_signal(gate, inc=1, device_id=(me ^ far,), device_id_type=MESH)
    pl.semaphore_wait(gate, (4 if far else 3) + (z > 0).astype(jnp.int32) + (z < 3).astype(jnp.int32))


class Gather:
    def __init__(self, full, tiles, sent, landed):
        self.full, self.tiles, self.sent, self.landed = full, tiles, sent, landed
        self.me, self.z, self.y, self.x, self.core = place()

    def moves(self, part, step, chunk):
        kind, rows, columns = PARTS[0] if part == GAINS else PARTS[part]
        z, y, x, me = self.z, self.y, self.x, self.me

        def view(zz, yy, xx):
            if part == GAINS:
                return self.tiles.at[zz, yy, xx]
            return self.full.at[chunk, zz, yy, xx, rows, columns]

        axis = OUTWARD[kind][step]
        if axis[0] == "z":
            far = int(axis[1])
            yy, xx = (ALL, ALL) if kind == "C" else (y, x)
            return (
                ((z >= far) & (z < 3), z - far, me + 8, z >= far + 1, z - 1 - far),
                ((z <= 3 - far) & (z > 0), z + far, me - 8, z <= 2 - far, z + 1 + far),
            ), lambda zz: view(zz, yy, xx)
        zz = z if kind == "C" else ALL
        if axis == "y":
            xx = x if kind == "A" else ALL
            return ((None, y, me ^ 4, None, 1 - y),), lambda yy: view(zz, yy, xx)
        yy = ALL if kind == "A" else y
        return ((None, x, me ^ 2, None, 1 - x),), lambda xx: view(zz, yy, xx)

    def copy(self, ref, device, part, step, chunk, way):
        return pltpu.make_async_remote_copy(
            src_ref=ref,
            dst_ref=ref,
            send_sem=self.sent.at[chunk, part, step, way],
            recv_sem=self.landed.at[chunk, part, step, way],
            device_id=(device,),
            device_id_type=MESH,
        )

    def send(self, part, step, chunk):
        moves, view = self.moves(part, step, chunk)
        for way, (sends, mine, device, _, _) in enumerate(moves):
            guarded(
                sends,
                lambda: self.copy(view(mine), device, part, step, chunk, way).start(),
            )

    def receive(self, part, step, chunk):
        moves, view = self.moves(part, step, chunk)
        for way, (_, _, _, receives, other) in enumerate(moves):
            guarded(
                receives,
                lambda: self.copy(view(other), self.me ^ 2, part, step, chunk, way).wait_recv(),
            )

    def finish(self, part, step, chunk):
        moves, view = self.moves(part, step, chunk)
        for way, (sends, mine, device, _, _) in enumerate(moves):
            guarded(
                sends,
                lambda: self.copy(view(mine), device, part, step, chunk, way).wait_send(),
            )

    def tick(self, time, parts):
        for step in range(6):
            age = time - step
            chunk = jnp.where(age < 2, age, age - HELD)

            @pl.when((age >= 0) & (chunk < CHUNKS) & ((age < 2) | (chunk >= 2)))
            def _():
                for part in parts:
                    if step > 0:
                        self.receive(part, step - 1, chunk)
                    if step < 5:
                        self.send(part, step, chunk)

    def tick_gains(self, step):
        if step > 0:
            self.receive(GAINS, step - 1, 0)
        if step < 5:
            self.send(GAINS, step, 0)

    def drain(self):
        def body(chunk, carry):
            for part in range(len(PARTS)):
                for step in range(5):
                    self.finish(part, step, chunk)
            return carry

        lax.fori_loop(0, CHUNKS, body, 0)
        for step in range(5):
            self.finish(GAINS, step, 0)


class Scatter:
    def __init__(self, sums, lands, totals, sent, landed):
        self.sums, self.lands, self.totals = sums, lands, totals
        self.sent, self.landed = sent, landed
        self.me, self.z, self.y, self.x, self.core = place()

    def moves(self, part, step, chunk):
        kind, rows, columns = PARTS[part]
        z, y, x, me = self.z, self.y, self.x, self.me
        slot, land = lax.rem(chunk, SUM_SLOTS), lax.rem(chunk, LAND_SLOTS)
        first, second, up, down = self.lands[part]
        axis = INWARD[kind][step]

        def view(zz, yy, xx):
            return self.sums.at[slot, zz, yy, xx, rows, columns]

        if axis[0] == "z":
            far = int(axis[1])
            count = 3 - far
            yy, xx = (ALL, ALL) if kind == "C" else (y, x)
            above, below = pl.ds(far + 1, count), pl.ds(0, count)
            up_land, down_land = up.at[land, pl.ds(far, count)], down.at[land, pl.ds(0, count)]
            return (
                (z == far, view(above, yy, xx), up_land, me + 8, z == far + 1, view(above, yy, xx)),
                (z == 3 - far, view(below, yy, xx), down_land, me - 8, z == 2 - far, view(below, yy, xx)),
            )
        zz = z if kind == "C" else ALL
        ref = (first if step == 0 or (kind == "C" and step == 3) else second).at[land]
        if axis == "x":
            yy = ALL if kind == "A" else y
            return ((None, view(zz, yy, 1 - x), ref, me ^ 2, None, view(zz, yy, x)),)
        xx = x if kind == "A" else ALL
        return ((None, view(zz, 1 - y, xx), ref, me ^ 4, None, view(zz, y, xx)),)

    def copy(self, source, target, device, part, step, chunk, way):
        return pltpu.make_async_remote_copy(
            src_ref=source,
            dst_ref=target,
            send_sem=self.sent.at[chunk, part, step, way],
            recv_sem=self.landed.at[chunk, part, step, way],
            device_id=(device,),
            device_id_type=MESH,
        )

    def step(self, part, step, chunk):
        if step > 0:
            for way, move in enumerate(self.moves(part, step - 1, chunk)):
                sends, source, land, device, receives, target = move

                def add():
                    self.copy(land, land, self.me ^ 2, part, step - 1, chunk, way).wait_recv()
                    target[...] = (target[...].astype(F32) + land[...].astype(F32)).astype(BF16)

                guarded(receives, add)
                guarded(
                    sends,
                    lambda: self.copy(source, land, device, part, step - 1, chunk, way).wait_send(),
                )
        if step < 5:
            for way, move in enumerate(self.moves(part, step, chunk)):
                sends, source, land, device, _, _ = move
                guarded(
                    sends,
                    lambda: self.copy(source, land, device, part, step, chunk, way).start(),
                )
        else:
            _, rows, columns = PARTS[part]
            slot = lax.rem(chunk, SUM_SLOTS)
            self.totals[lax.rem(chunk + 2, CHUNKS), rows, columns] = self.sums[
                slot, self.z, self.y, self.x, rows, columns
            ].astype(F32)

    def tick(self, time, parts):
        for step in range(5, -1, -1):
            chunk = time - step

            @pl.when((chunk >= 0) & (chunk < CHUNKS))
            def _():
                for part in parts:
                    self.step(part, step, chunk)


def pair_rows(core):
    mine = pl.ds(pl.multiple_of(core * 32, 32), 32)
    other = pl.ds(pl.multiple_of((1 - core) * 32, 32), 32)
    return mine, other


def semaphores():
    return [pltpu.SemaphoreType.DMA((CHUNKS, len(PARTS) + 1, 5, 2))] * 2


def land_shapes():
    slots = LAND_SLOTS
    plain = [(slots, 4, 2, 48, 384), (slots, 4, 48, 384), (slots, 3, 48, 384), (slots, 3, 48, 384)]
    late = [(slots, 2, 16, 768), (slots, 16, 768), (slots, 3, 2, 2, 16, 768), (slots, 3, 2, 2, 16, 768)]
    return [pltpu.VMEM(shape, BF16) for shape in plain + plain + late]


def params(number):
    return pltpu.CompilerParams(
        collective_id=number, has_side_effects=True, vmem_limit_bytes=62 * 2**20
    )


EAGER = 7
SPREAD = 3
LATER = CHUNKS + 5 + HELD - EAGER - SPREAD


def contract(left, right, left_dim, right_dim):
    return lax.dot_general(
        left, right, (((left_dim,), (right_dim,)), ((), ())), preferred_element_type=F32
    )


def lane_index(shape):
    return lax.broadcasted_iota(jnp.int32, shape, 1)


def half_turn(rows):
    width = rows.shape[1]
    first = lane_index(rows.shape) % 64 < 32
    return jnp.where(first, pltpu.roll(rows, width - 32, 1), pltpu.roll(rows, 32, 1))


def head_means(rows, ones):
    parts = [
        contract(rows[:, k : k + 256].astype(BF16), ones, 1, 0)
        for k in range(0, rows.shape[1], 256)
    ]
    return jnp.concatenate(parts, axis=1)


def head_ones():
    row = lax.broadcasted_iota(jnp.int32, (256, 256), 0) // 64
    column = lax.broadcasted_iota(jnp.int32, (256, 256), 1) // 64
    return jnp.where(row == column, 1.0 / 64.0, 0.0).astype(BF16)


def tiled(table, copies):
    return jnp.concatenate([table] * copies, axis=1)


def split_pair(rows, group):
    pair = rows[:, 128 * (group // 2) : 128 * (group // 2) + 128]
    low = lane_index(pair.shape) < 64
    if group % 2 == 0:
        kept = jnp.where(low, pair, 0.0)
        return kept, pltpu.roll(kept, 64, 1)
    kept = jnp.where(low, 0.0, pair)
    return pltpu.roll(kept, 64, 1), kept


def lanes_at(block, width):
    return pl.ds(pl.multiple_of(block * width, width), width)


def forward_kernel(*refs):
    weights = refs[:7]
    tile_in, x_in, cot_in, seg_in, gains, inverse = refs[7:13]
    (
        w_out, normed_out, raw_out, qkv_out, table_out, mask_out, total_out, mix_out,
        ffn_out, cot_out, saved_out, result_out, branch_out, kept_out, gain_out,
    ) = refs[13:28]
    (
        full, tiles, gain_rows, rows_all, cots, seg_rows, mixed, mixed_pair, wo_pair, attended,
        lent, local, pair_sent, pair_landed, sent, landed,
    ) = refs[28:]
    me, z, y, x, core = place()
    pair = (me ^ 1,)
    mine, other = pair_rows(core)

    def to_pair(number, source, target):
        return pltpu.make_async_remote_copy(
            src_ref=source,
            dst_ref=target,
            send_sem=pair_sent.at[number],
            recv_sem=pair_landed.at[number],
            device_id=pair,
            device_id_type=MESH,
        )

    def keep(number, source, target):
        return pltpu.make_async_copy(source, target, local.at[number])

    own_x = keep(1, x_in, rows_all.at[:, core])
    own_cot = keep(2, cot_in, cots.at[:, core])
    own_seg = keep(3, seg_in, seg_rows.at[core])
    first, later = pl.ds(0, 2), pl.ds(2, CHUNKS - 2)

    def piece_of(number, half, at, width, chunk, column):
        source = weights[number].at[:, pl.ds(pl.multiple_of(half * (weights[number].shape[1] // 2) + at, 256), width)]
        return source, full.at[chunk, z, y, x, mine, pl.ds(column, width)]

    def first_pieces(half):
        return (
            piece_of(0, half, 0, 512, 0, 0),
            piece_of(1, half, 0, 256, 0, 512),
            piece_of(2, half, 0, 256, 1, 0),
            piece_of(3, half, 0, 512, 1, 256),
        )

    def later_pieces(half, chunk):
        return tuple(piece_of(4 + k, half, 256 * chunk, 256, chunk + 2, 256 * k) for k in range(3))

    def place_later(chunk, carry):
        for source, target in later_pieces(1 - core, chunk):
            to_pair(18, source, target).start()
        for source, target in later_pieces(core, chunk):
            keep(4, source, target).start()
        return carry

    def placed(number, local_number, chunks):
        keep(local_number, full.at[chunks, z, y, x, mine, :], full.at[chunks, z, y, x, mine, :]).wait()
        whole = full.at[chunks, z, y, x, other, :]
        to_pair(number, whole, whole).wait_recv()

    give_x = to_pair(1, x_in, rows_all.at[:, core])
    take_x = to_pair(1, x_in, rows_all.at[:, 1 - core])
    give_cot = to_pair(2, cot_in, cots.at[:, core])
    take_cot = to_pair(2, cot_in, cots.at[:, 1 - core])
    give_seg = to_pair(3, seg_in, seg_rows.at[core])
    take_seg = to_pair(3, seg_in, seg_rows.at[1 - core])
    for source, target in first_pieces(core):
        keep(0, source, target).start()
    greet(me, z)
    for source, target in first_pieces(1 - core):
        to_pair(0, source, target).start()
    own_tile = keep(5, tile_in, tiles.at[z, y, x, core])
    give_tile = to_pair(9, tile_in, tiles.at[z, y, x, core])
    own_tile.start()
    give_tile.start()
    own_seg.start()
    give_seg.start()
    own_x.start()
    give_x.start()
    lax.fori_loop(0, CHUNKS - 2, place_later, 0)
    own_cot.start()
    give_cot.start()
    placed(0, 0, first)
    own_tile.wait()
    to_pair(9, tile_in, tiles.at[z, y, x, 1 - core]).wait_recv()
    gather = Gather(full, tiles, sent, landed)
    give_wo = to_pair(4, full.at[1, :, :, :, :, pl.ds(256, 512)], wo_pair)
    keep_w = keep(0, full.at[pl.ds(0, 2)], w_out)
    keep_gain = keep(11, gain_rows, gain_out)
    keep_cot = keep(2, cots, cot_out)
    def attention(normed, raw, qkv, table, mask, mask_turned, total, total_turned, keys, values):
        def early_copies(batch):
            return (
                keep(4, normed, normed_out.at[batch]),
                keep(5, raw, raw_out.at[batch]),
                keep(6, qkv, qkv_out.at[batch]),
                keep(7, table.at[batch], table_out.at[batch]),
                keep(8, mask_turned.at[batch], mask_out.at[batch]),
            )

        def late_copies(batch):
            return (
                keep(9, total_turned, total_out.at[batch]),
                keep(10, mixed.at[batch], mix_out.at[batch]),
            )

        def prepare(batch):
            segment = jnp.concatenate([seg_rows[0, batch], seg_rows[1, batch]], axis=1).astype(F32)
            column = jnp.broadcast_to(segment, (128, SEQ)).T
            below = jnp.zeros((SEQ, 128), F32)
            for k in range(0, SEQ, 128):
                below += (segment[:, k : k + 128] < column).astype(F32)
            before = jnp.sum(below, axis=1, keepdims=True)
            spot = lax.broadcasted_iota(jnp.int32, (SEQ, 128), 0).astype(F32) - before
            angle = spot * inverse[...]
            sine = jnp.sin(angle)
            first = lane_index((SEQ, 128)) % 64 < 32
            table[batch, :, 0:128] = jnp.cos(angle)
            table[batch, :, 128:256] = jnp.where(first, -sine, sine)
            for quarter in range(4):
                span = pl.ds(quarter * 256, 256)
                width = (quarter + 1) * 256
                same = segment[:, :width] == column[quarter * 256 : quarter * 256 + 256, 0:1]
                spots = lax.broadcasted_iota(jnp.int32, (256, width), 0) + quarter * 256
                behind = lane_index((256, width)) <= spots
                mask[batch, span, 0:width] = jnp.where(same & behind, 1.0, 0.0).astype(BF16)
                first_key = quarter * 256
                same = segment[:, first_key:] == column[first_key : first_key + 256, 0:1]
                spots = lax.broadcasted_iota(jnp.int32, same.shape, 0)
                behind = spots <= lane_index(same.shape)
                turned = jnp.where(same & behind, 1.0, 0.0).astype(BF16)
                mask_turned[batch, span, first_key:] = turned

        def project(batch):
            total[...] = jnp.zeros_like(total)
            ones = head_ones()

            def value_block(half, carry):
                span = pl.ds(pl.multiple_of(half * 512, 512), 512)
                value_weights = full[1, :, :, :, :, 0:256].reshape(1024, 256)
                value = contract(normed[span, :], value_weights, 1, 0).astype(BF16)
                qkv[span, 768:1024] = value
                value = value.astype(F32)
                for group in range(4):
                    low, high = split_pair(value, group)
                    values[group, 0, span, :] = low.astype(BF16)
                    values[group, 1, span, :] = high.astype(BF16)
                return carry

            def block(half, carry):
                span = pl.ds(pl.multiple_of(half * 512, 512), 512)
                rows = rows_all[batch, half].astype(F32)
                scale = lax.rsqrt(jnp.mean(rows * rows, axis=1, keepdims=True) + EPS)
                unit = (rows * scale * gain_rows[0:1]).astype(BF16)
                normed[span, :] = unit
                weights = full[0].reshape(1024, WIDE)
                product = contract(unit, weights, 1, 0)
                raw[span, :] = product.astype(BF16)
                level = lax.rsqrt(head_means(product * product, ones) + EPS)
                turned = product * level * gains[...]
                cosine = tiled(table[batch, span, 0:128], 6)
                sine_signed = tiled(table[batch, span, 128:256], 6)
                turned = turned * cosine + half_turn(turned) * sine_signed
                query = turned[:, 0:512] * 0.125
                key = turned[:, 512:768].astype(BF16).astype(F32)
                qkv[span, 0:512] = query.astype(BF16)
                qkv[span, 512:768] = key.astype(BF16)
                for group in range(4):
                    low, high = split_pair(key, group)
                    keys[group, 0, span, :] = low.astype(BF16)
                    keys[group, 1, span, :] = high.astype(BF16)
                return carry

            lax.fori_loop(0, 2, block, 0)

            @pl.when(batch == 0)
            def _():
                gather.tick(EAGER - 1, (0, 1, 2))
                give_wo.start()
                keep_w.start()

            lax.fori_loop(0, 2, value_block, 0)

        def attend(batch, quarter):
            span = pl.ds(quarter * 256, 256)
            width = (quarter + 1) * 256
            allowed = mask[batch, span, 0:width].astype(F32)
            lane = lane_index((256, 128))

            def group_step(group, carry):
                queries = qkv[span, lanes_at(group, 128)]
                parts, sums = [], []
                for side in range(2):
                    scores = contract(queries, keys[group, side, 0:width, :], 1, 1)
                    raised = jnp.exp(scores) * allowed
                    sums.append(1.0 / jnp.sum(raised, axis=1, keepdims=True))
                    parts.append(
                        contract(raised.astype(BF16), values[group, side, 0:width, :], 1, 0)
                    )
                result = (parts[0] + parts[1]) * jnp.where(lane < 64, sums[0], sums[1])
                mixed[batch, span, lanes_at(group, 128)] = result.astype(BF16)
                old = total[span, :]
                old = jnp.where(lane == 2 * group, sums[0], old)
                total[span, :] = jnp.where(lane == 2 * group + 1, sums[1], old)
                return carry

            lax.fori_loop(0, 4, group_step, 0)

        def piece(number, carry):
            batch, part = number // 4, number % 4

            @pl.when(part == 0)
            def _():
                @pl.when(batch > 0)
                def _():
                    for copy in early_copies(0) + late_copies(0):
                        copy.wait()

                project(batch)
                for copy in early_copies(batch):
                    copy.start()

            for turn in range(2):

                @pl.when((number % 2 == turn) & (number < 2 * SPREAD))
                def _():
                    gather.tick(EAGER + number // 2, ((0, 2), (1,))[turn])

            for quarter in range(4):

                @pl.when(part == quarter)
                def _():
                    attend(batch, quarter)

            @pl.when(part == 3)
            def _():
                total_turned[...] = total[...].T[0:8, :]
                for copy in late_copies(batch):
                    copy.start()
                to_pair(5 + batch, mixed.at[batch, lanes_at(1 - core, 512), :], mixed_pair.at[batch]).start()

            return carry

        own_seg.wait()
        take_seg.wait_recv()
        def early(time, carry):
            for step in range(6):

                @pl.when(time == step)
                def _():
                    gather.tick_gains(step)

            @pl.when(time == 2)
            def _():
                placed(18, 4, later)

            gather.tick(time, (0, 1, 2))
            for batch in range(2):

                @pl.when(time == 2 + 2 * batch)
                def _():
                    prepare(batch)

            return carry

        lax.fori_loop(0, EAGER - 1, early, 0)
        for block in range(8):
            quad = tiles[block // 2, block % 2]
            quad = quad[0, 0] + quad[0, 1] + quad[1, 0] + quad[1, 1]
            gain_rows[:, 128 * block : 128 * block + 128] = quad
        keep_gain.start()
        own_x.wait()
        own_cot.wait()
        take_x.wait_recv()
        take_cot.wait_recv()
        keep_cot.start()
        lax.fori_loop(0, 8, piece, 0)
        for copy in early_copies(1) + late_copies(1):
            copy.wait()

    pl.run_scoped(
        attention,
        pltpu.VMEM((SEQ, 1024), BF16),
        pltpu.VMEM((SEQ, WIDE), BF16),
        pltpu.VMEM((SEQ, 1024), BF16),
        pltpu.VMEM((2, SEQ, 256), F32),
        pltpu.VMEM((2, SEQ, SEQ), BF16),
        pltpu.VMEM((2, SEQ, SEQ), BF16),
        pltpu.VMEM((SEQ, 128), F32),
        pltpu.VMEM((8, SEQ), F32),
        pltpu.VMEM((4, 2, SEQ, 128), BF16),
        pltpu.VMEM((4, 2, SEQ, 128), BF16),
    )
    give_wo.wait_send()
    give_wo.wait_recv()
    give_x.wait_send()

    def swap_mixed(batch):
        return to_pair(5 + batch, mixed.at[batch, lanes_at(1 - core, 512), :], mixed_pair.at[batch])

    def join(batch, carry):
        swap_mixed(batch).wait_recv()
        span = lanes_at(core, 512)
        own_wo = full[1, :, :, :, :, 256:768].reshape(1024, 512)
        result = rows_all[batch, core].astype(F32)
        result += contract(mixed[batch, span, :], own_wo, 1, 1)
        result += contract(mixed_pair[batch], wo_pair[...].reshape(1024, 512), 1, 1)
        attended[batch] = result
        scale = lax.rsqrt(jnp.mean(result * result, axis=1, keepdims=True) + EPS)
        rows_all[batch, core] = (result * scale * gain_rows[1:2]).astype(BF16)
        to_pair(7 + batch, rows_all.at[batch, core], rows_all.at[batch, core]).start()
        return carry

    lax.fori_loop(0, 2, join, 0)
    keep_ffn = keep(3, rows_all, ffn_out)

    def feed_forward(result, back, saved):
        last = CHUNKS - 3

        def save(chunk, batch, half):
            return keep(4 + batch, saved.at[batch], saved_out.at[chunk, batch, half])

        def lend(batch):
            return (
                to_pair(10 + batch, cots.at[batch, 1 - core], lent.at[0, batch]),
                to_pair(12 + batch, rows_all.at[batch, 1 - core], lent.at[1, batch]),
            )

        result[...] = jnp.zeros_like(result)
        back[...] = jnp.zeros_like(back)

        def chunk_step(chunk, carry):
            def block(part, inner):
                batch = part % 2
                own = (part < 2) != (chunk == last)
                half = jnp.where(own, core, 1 - core)
                for turn in range(2):

                    @pl.when((part == 2 * turn + 1) & (chunk < LATER))
                    def _():
                        gather.tick(EAGER + SPREAD + chunk, ((0, 2), (1,))[turn])

                @pl.when((chunk == 0) & (part >= 2))
                def _():
                    to_pair(
                        7 + batch, rows_all.at[batch, core], rows_all.at[batch, 1 - core]
                    ).wait_recv()

                @pl.when((chunk == 1) & (part == 0))
                def _():
                    keep_ffn.start()

                @pl.when((chunk == last) & (part == 0))
                def _():
                    keep_w.wait()
                    keep_gain.wait()
                    for each in range(2):
                        swap_mixed(each).wait_send()
                    keep_ffn.wait()
                    keep_cot.wait()

                @pl.when((chunk > 0) | (part > 1))
                def _():
                    save(chunk, batch, half).wait()

                up_weights = full[chunk + 2, :, :, :, :, 0:512].reshape(1024, 512)
                down_weights = full[chunk + 2, :, :, :, :, 512:768].reshape(1024, 256)
                for piece in range(2):
                    rows = pl.ds(256 * piece, 256)
                    both = contract(rows_all[batch, half, rows, :], up_weights, 1, 0)
                    grad = contract(cots[batch, half, rows, :], down_weights, 1, 0)
                    gate, up = both[:, 0:256], both[:, 256:512]
                    bend = 1.0 / (1.0 + jnp.exp(-gate))
                    silu = gate * bend
                    active = (silu * up).astype(BF16)
                    grad_up = (grad * silu).astype(BF16)
                    grad_gate = (grad * up * bend * (1.0 + gate * (1.0 - bend))).astype(BF16)
                    saved[batch, rows, 0:256] = grad_gate
                    saved[batch, rows, 256:512] = grad_up
                    saved[batch, rows, 512:768] = active
                    result[batch, half, rows, :] += contract(active, down_weights, 1, 1)
                    pulled = jnp.concatenate([grad_gate, grad_up], axis=1)
                    back[batch, half, rows, :] += contract(pulled, up_weights, 1, 1)
                save(chunk, batch, half).start()

                @pl.when((chunk == last) & (part < 2))
                def _():
                    cots[batch, half] = result[batch, half].astype(BF16)
                    rows_all[batch, half] = back[batch, half].astype(BF16)
                    for copy in lend(batch):
                        copy.start()

                return inner

            lax.fori_loop(0, 4, block, 0)
            return carry

        lax.fori_loop(0, CHUNKS - 2, chunk_step, 0)

        def give_branch(batch, side):
            columns = pl.ds(512 * side, 512)
            return to_pair(
                14 + 2 * batch + side, cots.at[batch, core, :, columns], mixed.at[batch, columns, :]
            )

        def keep_branch(batch, side):
            columns = pl.ds(512 * side, 512)
            target = branch_out.at[batch, 1 - core, :, columns]
            return keep(8 + 2 * batch + side, mixed.at[batch, columns, :], target)

        def ends(batch):
            return (
                keep(batch, lent.at[0, batch], result_out.at[batch]),
                keep(2 + batch, attended.at[batch], kept_out.at[batch]),
                keep(6 + batch, cots.at[batch, core], branch_out.at[batch, core]),
            )

        def close(batch, carry):
            for copy in lend(batch):
                copy.wait_recv()
            joined = attended[batch]
            outputs = joined + result[batch, core] + lent[0, batch].astype(F32)
            lent[0, batch] = outputs.astype(BF16)
            scale = lax.rsqrt(jnp.mean(joined * joined, axis=1, keepdims=True) + EPS)
            unit = joined * scale
            pulled = (back[batch, core] + lent[1, batch].astype(F32)) * gain_rows[1:2]
            shared = jnp.mean(pulled * unit, axis=1, keepdims=True)
            total = cots[batch, core].astype(F32) + scale * (pulled - unit * shared)
            attended[batch] = total
            cots[batch, core] = total.astype(BF16)
            for side in range(2):
                give_branch(batch, side).start()
            for copy in ends(batch):
                copy.start()
            return carry

        lax.fori_loop(0, 2, close, 0)
        for batch in range(2):
            for side in range(2):
                give_branch(batch, side).wait_recv()
                keep_branch(batch, side).start()
        for batch in range(2):
            save(last, batch, core).wait()
            for copy in ends(batch):
                copy.wait()
            for side in range(2):
                keep_branch(batch, side).wait()
                give_branch(batch, side).wait_send()
            for copy in lend(batch):
                copy.wait_send()

    pl.run_scoped(
        feed_forward,
        pltpu.VMEM((2, 2, 512, 1024), F32),
        pltpu.VMEM((2, 2, 512, 1024), F32),
        pltpu.VMEM((2, 512, WIDE), BF16),
    )
    for number, chunks in ((0, first), (18, later)):
        whole = full.at[chunks, z, y, x, mine, :]
        to_pair(number, whole, whole).wait_send()
    give_seg.wait_send()
    for batch in range(2):
        to_pair(7 + batch, rows_all.at[batch, core], rows_all.at[batch, core]).wait_send()
    give_tile.wait_send()
    give_cot.wait_send()
    gather.drain()


def forward_call(weights, tile, inputs, cotangent, segments, gains):
    rows = inputs.shape[1]
    counter = np.arange(128) % 32
    inverse = jnp.asarray(THETA ** (-2.0 * counter / 64), F32)[None]
    shapes = [
        ((2, 4, 2, 2, 64, WIDE), BF16),
        ((2, SEQ, 1024), BF16),
        ((2, SEQ, WIDE), BF16),
        ((2, SEQ, 1024), BF16),
        ((2, SEQ, 256), F32),
        ((2, SEQ, SEQ), BF16),
        ((2, 8, SEQ), F32),
        ((2, SEQ, 512), BF16),
        ((2, 2, rows, 1024), BF16),
        ((2, 2, rows, 1024), BF16),
        ((CHUNKS - 2, 2, 2, rows, WIDE), BF16),
        ((2, rows, 1024), BF16),
        ((2, 2, rows, 1024), BF16),
        ((2, rows, 1024), F32),
        ((8, 1024), F32),
    ]
    anywhere = pl.BlockSpec(memory_space=pl.ANY)
    inside = pl.BlockSpec(memory_space=pltpu.VMEM)
    return pl.pallas_call(
        forward_kernel,
        out_shape=[jax.ShapeDtypeStruct(*shape) for shape in shapes],
        in_specs=[anywhere] * (len(weights) + 4) + [inside] * 2,
        out_specs=[anywhere] * len(shapes),
        scratch_shapes=[
            pltpu.VMEM((CHUNKS, 4, 2, 2, 64, WIDE), BF16),
            pltpu.VMEM((4, 2, 2, 2, 8, 128), F32),
            pltpu.VMEM((8, 1024), F32),
            pltpu.VMEM((2, 2, rows, 1024), BF16),
            pltpu.VMEM((2, 2, rows, 1024), BF16),
            pltpu.VMEM((2, 2, 1, rows), jnp.int32),
            pltpu.VMEM((2, SEQ, 512), BF16),
            pltpu.VMEM((2, rows, 512), BF16),
            pltpu.VMEM((4, 2, 2, 64, 512), BF16),
            pltpu.VMEM((2, rows, 1024), F32),
            pltpu.VMEM((2, 2, rows, 1024), BF16),
            pltpu.SemaphoreType.DMA((12,)),
            pltpu.SemaphoreType.DMA((19,)),
            pltpu.SemaphoreType.DMA((19,)),
        ]
        + semaphores(),
        compiler_params=params(0),
        name="forward",
    )(*weights, tile, inputs, cotangent, segments[:, None, :], gains, inverse)


def pack_gains(attn_gain, ffn_gain):
    count = attn_gain.shape[0]
    slot = lax.axis_index("fsdp") % (128 // count)
    pair = jnp.stack([attn_gain, ffn_gain]).astype(F32)
    place_of = (jnp.arange(128 // count) == slot).astype(F32)
    spread = (place_of[None, :, None] * pair[:, None, :]).reshape(2, 128)
    return jnp.concatenate([spread, jnp.zeros((6, 128), F32)])


def backward_kernel(*refs):
    (
        w_in, normed_in, raw_in, qkv_in, table_in, mask_in, total_in, mix_in, ffn_in, cot_in,
        saved_in, branch_in, kept_in, x_in, gain_rows, head_gains,
    ) = refs[:16]
    grad_out, sums_out, head_out = refs[16:19]
    sums = refs[19]
    lands = (refs[20:24], refs[24:28], refs[28:32])
    (
        totals, pair_land, rows_all, cots, saved, branch, grads, qkv, raw, table, total, mask, mixed,
        grad_mixed, wo, keys, values, key_sum, value_sum, head_sum, head_land, kept,
        local, pair_sent, pair_landed, head_sent, head_landed, sent, landed,
    ) = refs[32:]
    me, z, y, x, core = place()
    mine, other = pair_rows(core)
    scatter = Scatter(sums, lands, totals, sent, landed)

    def to_pair(number, source, target):
        return pltpu.make_async_remote_copy(
            src_ref=source,
            dst_ref=target,
            send_sem=pair_sent.at[number],
            recv_sem=pair_landed.at[number],
            device_id=(me ^ 1,),
            device_id_type=MESH,
        )

    def load(number, source, target):
        return pltpu.make_async_copy(source, target, local.at[number])

    loads = [
        load(2, saved_in.at[0], saved),
        load(0, ffn_in, rows_all),
        load(1, cot_in, cots),
        load(3, branch_in, branch),
        load(4, w_in.at[1, :, :, pl.ds(256, 512)], wo),
        load(5, mix_in, mixed),
    ]
    def batch_loads(batch):
        return (
            load(6, qkv_in.at[batch], qkv),
            load(7, raw_in.at[batch], raw),
            load(8, table_in.at[batch], table),
            load(9, total_in.at[batch], total),
            load(10, mask_in.at[batch], mask),
        )

    for copy in loads[:3]:
        copy.start()
    greet(me, z, 16)
    head_sum[...] = jnp.zeros_like(head_sum)

    def put(slot, columns, left, right):
        product = contract(left, right, 0, 0).astype(BF16)
        sums[slot, :, :, :, :, columns] = product.reshape(4, 2, 2, 64, columns.size)

    def up_terms(chunk):
        slot = lax.rem(chunk, SUM_SLOTS)
        flat = saved[:, :, :, 0:512].reshape(2048, 512)
        put(slot, pl.ds(0, 512), rows_all[...].reshape(2048, 1024), flat)

    def down_terms(chunk):
        slot = lax.rem(chunk, SUM_SLOTS)
        flat = saved[:, :, :, 512:768].reshape(2048, 256)
        put(slot, pl.ds(512, 256), cots[...].reshape(2048, 1024), flat)

    loads[0].wait()
    loads[1].wait()
    up_terms(0)
    loads[2].wait()
    down_terms(0)
    load(2, saved_in.at[1], saved).start()
    for copy in loads[3:]:
        copy.start()
    for copy in batch_loads(0):
        copy.start()
    def mixed_back(half, carry):
        product = contract(branch[half].reshape(1024, 1024), wo[...].reshape(1024, 512), 1, 0)
        grad_mixed[half] = product.astype(BF16)
        return carry

    def pull_back(grad, span, columns, gain, number):
        plain = raw[span, columns].astype(F32)
        width = plain.shape[1]
        row = lax.broadcasted_iota(jnp.int32, (width, width), 0) // 64
        column = lax.broadcasted_iota(jnp.int32, (width, width), 1) // 64
        ones = jnp.where(row == column, 1.0 / 64.0, 0.0).astype(BF16)
        level = lax.rsqrt(contract((plain * plain).astype(BF16), ones, 1, 0) + EPS)
        unit = plain * level
        turned = grad * table[span, 0:128] - half_turn(grad) * table[span, 128:256]
        terms = turned * unit
        head_sum[number] += jnp.sum(terms.reshape(-1, 8, width), axis=0)
        scaled = terms * gain
        shared = contract(scaled.astype(BF16), ones, 1, 0)
        return level * (turned * gain - unit * shared)

    def sides(pair, parity):
        low = lane_index(pair.shape) < 64
        rows = pair.astype(F32)
        first, second = jnp.where(low, rows, 0.0), jnp.where(low, 0.0, rows)
        if parity == 0:
            second = pltpu.roll(second, 64, 1)
        else:
            first = pltpu.roll(first, 64, 1)
        return first.astype(BF16), second.astype(BF16)

    def attend_back(batch, couple, parity):
        key_pair = qkv[:, pl.ds(pl.multiple_of(512 + couple * 128, 128), 128)].astype(F32)
        value_pair = qkv[:, pl.ds(pl.multiple_of(768 + couple * 128, 128), 128)].astype(F32)
        for target, pair in ((keys, key_pair), (values, value_pair)):
            low, high = split_pair(pair, parity)
            target[0] = low.astype(BF16)
            target[1] = high.astype(BF16)
        if parity == 0:
            key_sum[...] = jnp.zeros_like(key_sum)
            value_sum[...] = jnp.zeros_like(value_sum)
        group = couple * 2 + parity
        picks = lax.broadcasted_iota(jnp.int32, (8, 128), 0) == lane_index((8, 128)) // 64
        picks = jnp.where(picks, 1.0, 0.0).astype(BF16)
        for quarter in range(4):
            span = pl.ds(quarter * 256, 256)
            width = (quarter + 1) * 256
            allowed = mask[0:width, span].astype(F32)
            queries = qkv[span, lanes_at(group, 128)]
            pulled = grad_mixed[batch, span, lanes_at(group, 128)]
            product = pulled.astype(F32) * mixed[batch, span, lanes_at(group, 128)].astype(F32)
            coarse = product.astype(BF16)
            rest = (product - coarse.astype(F32)).astype(BF16)
            centers = contract(picks, coarse, 1, 1) + contract(picks, rest, 1, 1)
            query_sides, pulled_sides = sides(queries, parity), sides(pulled, parity)
            levels = [total[pl.ds(2 * group + side, 1), span] for side in range(2)]
            scores = contract(keys[:, 0:width, :].reshape(2 * width, 128), queries, 1, 1)
            grad_probs = contract(values[:, 0:width, :].reshape(2 * width, 128), pulled, 1, 1)
            low_probs, grad_scores = [], []
            for side in range(2):
                rows = slice(side * width, side * width + width)
                probs = jnp.exp(scores[rows]) * allowed * levels[side]
                low_probs.append(probs.astype(BF16))
                grad_scores.append((probs * (grad_probs[rows] - centers[side : side + 1])).astype(BF16))
            stacked = jnp.concatenate(grad_scores, axis=0)
            grad_query = contract(stacked, keys[:, 0:width, :].reshape(2 * width, 128), 0, 0)
            wide = jnp.concatenate(grad_scores, axis=1)
            grad_key = contract(wide, jnp.concatenate(query_sides, axis=0), 1, 0)
            wide = jnp.concatenate(low_probs, axis=1)
            grad_value = contract(wide, jnp.concatenate(pulled_sides, axis=0), 1, 0)
            key_sum[0:width, :] += grad_key
            value_sum[0:width, :] += grad_value
            grad_raw = pull_back(
                grad_query * 0.125, span, lanes_at(group, 128), head_gains[:, 0:128], 0
            )
            grads[batch, span, lanes_at(group, 128)] = grad_raw.astype(BF16)
        if parity == 1:
            whole = pl.ds(0, SEQ)
            columns = pl.ds(pl.multiple_of(512 + couple * 128, 128), 128)
            grad_raw = pull_back(key_sum[...], whole, columns, head_gains[:, 512:640], 1)
            grads[batch, :, columns] = grad_raw.astype(BF16)
            columns = pl.ds(pl.multiple_of(768 + couple * 128, 128), 128)
            grads[batch, :, columns] = value_sum[...].astype(BF16)

    def head_copy(step):
        bit = (1, 2, 4, 8, 16)[step]
        return pltpu.make_async_remote_copy(
            src_ref=head_sum,
            dst_ref=head_land.at[step],
            send_sem=head_sent.at[step],
            recv_sem=head_landed.at[step],
            device_id=(me ^ bit,),
            device_id_type=MESH,
        )

    def send_heads(step):
        if step > 0:
            head_copy(step - 1).wait()
            head_sum[...] += head_land[step - 1]
        if step < 5:
            head_copy(step).start()

    def near_normed(batch, half):
        part = grads[batch, pl.ds(pl.multiple_of(half * 512, 512), 512), :]
        first = contract(part[:, 0:768], saved[0].reshape(1024, WIDE), 1, 1)
        value_weights = saved[1].reshape(1024, WIDE)[:, 0:256]
        return first + contract(part[:, 768:1024], value_weights, 1, 1)

    def work(time):
        @pl.when(time == 0)
        def _():
            for copy in loads[3:]:
                copy.wait()
            lax.fori_loop(0, 2, mixed_back, 0)

        @pl.when((time >= 1) & (time <= 8))
        def _():
            unit = time - 1
            batch, couple, parity = unit // 4, (unit // 2) % 2, unit % 2

            @pl.when(unit % 4 == 0)
            def _():
                for copy in batch_loads(batch):
                    copy.wait()

            for each in range(2):

                @pl.when(parity == each)
                def _():
                    attend_back(batch, couple, each)

            @pl.when(unit == 3)
            def _():
                for copy in batch_loads(1):
                    copy.start()

        for step in range(6):

            @pl.when(time == 9 + step)
            def _():
                send_heads(step)

        @pl.when(time == 10)
        def _():
            load(2, w_in, saved).wait()
            load(7, x_in, cots.at[1]).start()
            load(6, kept_in.at[0], kept).start()
            lend(0)

        @pl.when((time == 12) | (time == 13))
        def _():
            batch = time - 12
            swap(batch).wait()
            load(6, kept_in.at[batch], kept).wait()

            @pl.when(batch == 0)
            def _():
                load(7, x_in, cots.at[1]).wait()

            rows = cots[1, batch].astype(F32)
            scale = lax.rsqrt(jnp.mean(rows * rows, axis=1, keepdims=True) + EPS)
            unit = rows * scale
            pulled = near_normed(batch, core) + pair_land[batch].astype(F32)
            pulled = pulled * gain_rows[0:1]
            shared = jnp.mean(pulled * unit, axis=1, keepdims=True)
            grad = kept[...] + scale * (pulled - unit * shared)
            cots[0, batch] = grad.astype(BF16)
            store_grad(batch).start()

            @pl.when(batch == 0)
            def _():
                load(6, kept_in.at[1], kept).start()

    def swap(batch):
        return to_pair(1 + batch, cots.at[0, batch], pair_land.at[batch])

    def lend(batch):
        cots[0, batch] = near_normed(batch, 1 - core).astype(BF16)
        swap(batch).start()

    def store_grad(batch):
        return load(8 + batch, cots.at[0, batch], grad_out.at[batch])

    def hand(number, chunks, half):
        return to_pair(
            3 + number, totals.at[chunks, other, :], sums_out.at[half, chunks]
        )

    def own_sums(number, chunks):
        return load(3 + number, totals.at[chunks, mine, :], sums_out.at[core, chunks])

    def next_terms(time):
        @pl.when(time + 1 < CHUNKS - 2)
        def _():
            load(2, saved_in.at[0], saved).wait()
            up_terms(time + 1)
            down_terms(time + 1)

        @pl.when(time + 2 < CHUNKS - 2)
        def _():
            load(2, saved_in.at[time + 2], saved).start()

        @pl.when(time == CHUNKS - 4)
        def _():
            load(0, normed_in, rows_all).start()
            load(2, w_in, saved).start()

        @pl.when(time == CHUNKS - 3)
        def _():
            load(0, normed_in, rows_all).wait()
            slot = (CHUNKS - 2) % SUM_SLOTS
            put(slot, pl.ds(0, 768), rows_all[...].reshape(2048, 1024), grads[:, :, 0:768].reshape(2048, 768))

        @pl.when(time == CHUNKS - 2)
        def _():
            slot = (CHUNKS - 1) % SUM_SLOTS
            put(slot, pl.ds(0, 256), rows_all[...].reshape(2048, 1024), grads[:, :, 768:1024].reshape(2048, 256))
            put(slot, pl.ds(256, 512), branch[...].reshape(2048, 1024), mixed[...].reshape(2048, 512))

        @pl.when(time == 10)
        def _():
            lend(1)

        @pl.when(time == CHUNKS + 3)
        def _():
            hand(0, pl.ds(2, CHUNKS - 2), core).start()
            own_sums(0, pl.ds(2, CHUNKS - 2)).start()

    def body(time, carry):
        scatter.tick(time, (0, 2))
        work(time)
        scatter.tick(time, (1,))
        next_terms(time)
        return carry

    lax.fori_loop(0, CHUNKS + 5, body, 0)
    head_store = load(7, head_sum, head_out)
    head_store.start()
    hand(1, pl.ds(0, 2), core).start()
    own_sums(1, pl.ds(0, 2)).start()
    for number, chunks in ((0, pl.ds(2, CHUNKS - 2)), (1, pl.ds(0, 2))):
        hand(number, chunks, core).wait_send()
        hand(number, chunks, 1 - core).wait_recv()
        own_sums(number, chunks).wait()
    for batch in range(2):
        store_grad(batch).wait()
    head_store.wait()


def backward_call(forward, inputs, gains):
    rows = inputs.shape[1]
    (
        w, normed, raw, qkv, table, mask, total, mix, ffn, cot, saved, _, branch, kept, gain_rows,
    ) = forward
    anywhere = pl.BlockSpec(memory_space=pl.ANY)
    inside = pl.BlockSpec(memory_space=pltpu.VMEM)
    return pl.pallas_call(
        backward_kernel,
        out_shape=[
            jax.ShapeDtypeStruct((2, rows, 1024), BF16),
            jax.ShapeDtypeStruct((2, CHUNKS, 32, WIDE), F32),
            jax.ShapeDtypeStruct((2, 8, 128), F32),
        ],
        in_specs=[anywhere] * 14 + [inside] * 2,
        out_specs=[anywhere] * 3,
        scratch_shapes=[pltpu.VMEM((SUM_SLOTS, 4, 2, 2, 64, WIDE), BF16)]
        + land_shapes()
        + [
            pltpu.VMEM((CHUNKS, 64, WIDE), F32),
            pltpu.VMEM((2, rows, 1024), BF16),
            pltpu.VMEM((2, 2, rows, 1024), BF16),
            pltpu.VMEM((2, 2, rows, 1024), BF16),
            pltpu.VMEM((2, 2, rows, WIDE), BF16),
            pltpu.VMEM((2, 2, rows, 1024), BF16),
            pltpu.VMEM((2, SEQ, 1024), BF16),
            pltpu.VMEM((SEQ, 1024), BF16),
            pltpu.VMEM((SEQ, WIDE), BF16),
            pltpu.VMEM((SEQ, 256), F32),
            pltpu.VMEM((8, SEQ), F32),
            pltpu.VMEM((SEQ, SEQ), BF16),
            pltpu.VMEM((2, SEQ, 512), BF16),
            pltpu.VMEM((2, SEQ, 512), BF16),
            pltpu.VMEM((2, 512, 512), BF16),
            pltpu.VMEM((2, SEQ, 128), BF16),
            pltpu.VMEM((2, SEQ, 128), BF16),
            pltpu.VMEM((SEQ, 128), F32),
            pltpu.VMEM((SEQ, 128), F32),
            pltpu.VMEM((2, 8, 128), F32),
            pltpu.VMEM((5, 2, 8, 128), F32),
            pltpu.VMEM((rows, 1024), F32),
            pltpu.SemaphoreType.DMA((11,)),
            pltpu.SemaphoreType.DMA((5,)),
            pltpu.SemaphoreType.DMA((5,)),
            pltpu.SemaphoreType.DMA((5,)),
            pltpu.SemaphoreType.DMA((5,)),
        ]
        + semaphores(),
        compiler_params=params(1),
        name="backward",
    )(
        w.reshape(2, 2, rows, WIDE), normed.reshape(2, 2, rows, 1024), raw, qkv, table, mask, total,
        mix, ffn, cot, saved, branch, kept, inputs, gain_rows, gains,
    )


def unpack(out):
    def both(chunk, start, stop):
        return jnp.concatenate([out[0, chunk, :, start:stop], out[1, chunk, :, start:stop]], axis=1)

    def wide_of(start):
        return out[:, 2:, :, start : start + 256].transpose(2, 0, 1, 3).reshape(out.shape[2], -1)

    return (
        both(0, 0, 512),
        both(0, 512, 768),
        both(1, 0, 256),
        both(1, 256, 768),
        wide_of(0),
        wide_of(256),
        wide_of(512),
    )


def gain_terms(gain, weights, grads):
    total = sum(jnp.sum(w.astype(F32) * g, axis=1) for w, g in zip(weights, grads))
    return total / gain.astype(F32)


def local_grid(
    inputs,
    segments,
    attn_gain,
    w_query,
    key_projection,
    value_projection,
    w_output,
    query_gain,
    key_norm_gain,
    ffn_gain,
    w_gate,
    w_up,
    w_down,
    cotangent,
):
    attn_weights = (w_query, key_projection, value_projection)
    weights = attn_weights + (w_output.T, w_gate, w_up, w_down.T)
    gains = [query_gain] * 8 + [key_norm_gain] * 4
    gains = jnp.concatenate(gains).astype(F32)[None]
    forward = forward_call(
        weights, pack_gains(attn_gain, ffn_gain), inputs, cotangent, segments, gains
    )
    input_grad, sums, heads = backward_call(forward, inputs, gains)
    query, key, value, output_t, gate, up, down_t = unpack(sums)
    heads = jnp.sum(heads, axis=1)
    heads = heads[:, :64] + heads[:, 64:]
    return (
        forward[11],
        input_grad,
        gain_terms(attn_gain, attn_weights, (query, key, value)),
        query,
        key,
        value,
        output_t.T,
        heads[0],
        heads[1],
        gain_terms(ffn_gain, (w_gate, w_up), (gate, up)),
        gate,
        up,
        down_t.T,
    )


def from_behind(block, axis, distance):
    devices = range(lax.axis_size(axis))
    route = [(i - distance, i) for i in devices if i - distance in devices]
    return lax.ppermute(block, axis, route)


def row_norm(values, gain_row):
    return values * lax.rsqrt(jnp.mean(values * values, axis=-1, keepdims=True) + EPS) * gain_row


def angles(places, head_width):
    counter = jnp.arange(head_width // 2, dtype=jnp.float32)
    inverse = jnp.power(jnp.float32(THETA), -2.0 * counter / head_width)
    turned = places.astype(jnp.float32)[:, None] * inverse[None, :]
    return (jnp.cos(turned), jnp.sin(turned))


def prepare_inputs(raw_rows, gain_row, cosine_table, sine_table_rows, head_count):
    token_count = raw_rows.shape[0]
    head_width = gain_row.shape[0]
    split_rows = raw_rows.reshape(token_count, head_count, head_width)
    normed = row_norm(split_rows, gain_row)
    first_half = normed[..., : head_width // 2]
    second = normed[..., head_width // 2 :]
    cos_rows = cosine_table[:, None, :]
    sin_rows = sine_table_rows[:, None, :]
    turned = jnp.concatenate(
        [first_half * cos_rows - second * sin_rows, second * cos_rows + first_half * sin_rows],
        axis=-1,
    )
    return turned.reshape(token_count, head_count * head_width)


def plain_product(left_rows, right_rows):
    return jnp.dot(left_rows, right_rows, preferred_element_type=jnp.float32)


def rows_product(left_rows, right_rows):
    return lax.dot_general(
        left_rows, right_rows, (((0,), (0,)), ((), ())), preferred_element_type=jnp.float32
    )


def cols_product(left_rows, right_rows):
    return lax.dot_general(
        left_rows, right_rows, (((1,), (1,)), ((), ())), preferred_element_type=jnp.float32
    )


def silu_product(gate_raw, upward):
    return gate_raw * jax.nn.sigmoid(gate_raw) * upward


def add_sets(former_set, latter_set):
    if former_set is None:
        return latter_set
    return tuple((former + latter for former, latter in zip(former_set, latter_set)))


def local(
    inputs,
    segments,
    attn_gain,
    w_query,
    key_projection,
    value_projection,
    w_output,
    query_gain,
    key_norm_gain,
    ffn_gain,
    w_gate,
    w_up,
    w_down,
    cotangent,
):
    batches = inputs.shape[0]
    tokens = inputs.shape[1]
    head_width = query_gain.shape[0]
    query_width = w_query.shape[1]
    kv_width = key_projection.shape[1]
    query_head_rows = query_width // head_width
    kv_heads = kv_width // head_width
    heads_per_group = query_head_rows // kv_heads
    scale = 1.0 / math.sqrt(head_width)
    query_gain_f = query_gain.astype(jnp.float32)
    key_gain_f = key_norm_gain.astype(jnp.float32)
    device_index = lax.axis_index("fsdp")
    places_row = jnp.arange(tokens, dtype=jnp.int32)
    causal = places_row[None, :] <= places_row[:, None]
    same_run = device_index * tokens // SEQ == (device_index - 1) * tokens // SEQ
    outputs_list = []
    grads_list = []
    shard_sums = None
    gain_sums = None
    for batch_index in range(batches):
        gathered = (
            lax.all_gather(attn_gain, "fsdp", axis=0, tiled=True),
            lax.all_gather(w_query, "fsdp", axis=0, tiled=True),
            lax.all_gather(key_projection, "fsdp", axis=0, tiled=True),
            lax.all_gather(value_projection, "fsdp", axis=0, tiled=True),
            lax.all_gather(w_output, "fsdp", axis=1, tiled=True),
            lax.all_gather(ffn_gain, "fsdp", axis=0, tiled=True),
            lax.all_gather(w_gate, "fsdp", axis=0, tiled=True),
            lax.all_gather(w_up, "fsdp", axis=0, tiled=True),
            lax.all_gather(w_down, "fsdp", axis=1, tiled=True),
        )
        (
            gain_attn,
            full_query,
            full_key,
            full_value,
            full_output,
            gain_ffn,
            full_gate,
            full_up,
            full_down,
        ) = gathered
        hidden = inputs[batch_index].astype(jnp.float32)
        segment = segments[batch_index]
        normed_f, norm_pull = jax.vjp(row_norm, hidden, gain_attn.astype(jnp.float32))
        normed = normed_f.astype(jnp.bfloat16)
        query_raw = plain_product(normed, full_query)
        key_projected = plain_product(normed, full_key)
        value_reduced = plain_product(normed, full_value).astype(jnp.bfloat16)
        lower_count = jnp.sum((segment[None, :] < segment[:, None]).astype(jnp.int32), axis=1)
        local_places = places_row - lower_count
        cos_local, sin_local = angles(local_places, head_width)
        key_sent = prepare_inputs(key_projected, key_gain_f, cos_local, sin_local, kv_heads).astype(
            jnp.bfloat16
        )
        remote_key, remote_value, remote_segment = from_behind(
            (key_sent, value_reduced, segment.astype(jnp.bfloat16)), "fsdp", 1
        )
        remote_match = (remote_segment.astype(jnp.int32)[None, :] == segment[:, None]) & same_run
        places_all = local_places + jnp.sum(remote_match.astype(jnp.int32), axis=1)
        cosine_table, sine_table_rows = angles(places_all, head_width)
        query_f, query_pull = jax.vjp(
            lambda raw_rows, gain_row: prepare_inputs(
                raw_rows, gain_row, cosine_table, sine_table_rows, query_head_rows
            ),
            query_raw,
            query_gain_f,
        )
        key_f, key_pull = jax.vjp(
            lambda raw_rows, gain_row: prepare_inputs(
                raw_rows, gain_row, cosine_table, sine_table_rows, kv_heads
            ),
            key_projected,
            key_gain_f,
        )
        query_low = query_f.astype(jnp.bfloat16)
        key_low = key_f.astype(jnp.bfloat16)
        allowed = jnp.concatenate(
            [remote_match, causal & (segment[None, :] == segment[:, None])], axis=1
        )
        query_split = query_low.reshape(tokens, kv_heads, heads_per_group, head_width).transpose(
            1, 0, 2, 3
        )
        key_split = (
            jnp.concatenate([remote_key, key_low], axis=0)
            .reshape(2 * tokens, kv_heads, head_width)
            .transpose(1, 0, 2)
        )
        value_split = (
            jnp.concatenate([remote_value, value_reduced], axis=0)
            .reshape(2 * tokens, kv_heads, head_width)
            .transpose(1, 0, 2)
        )

        def head_forward(blocks):
            query_part, key_part, value_part = blocks
            scores = (
                jnp.einsum("tgd,ld->gtl", query_part, key_part, preferred_element_type=jnp.float32)
                * scale
            )
            scores = jnp.where(allowed[None], scores, NEG)
            row_peak = jnp.max(scores, axis=-1, keepdims=True)
            raised = jnp.exp(scores - row_peak)
            row_total = jnp.sum(raised, axis=-1, keepdims=True)
            prob_rows = (raised / row_total).astype(jnp.bfloat16)
            mixed_part = jnp.einsum(
                "gtl,ld->tgd", prob_rows, value_part, preferred_element_type=jnp.float32
            )
            return (mixed_part.astype(jnp.bfloat16), (row_peak + jnp.log(row_total))[..., 0])

        mixed_split, log_totals = lax.map(head_forward, (query_split, key_split, value_split))
        attn_mix = mixed_split.transpose(1, 0, 2, 3).reshape(tokens, query_width)
        attended = hidden + plain_product(attn_mix, full_output)
        ffn_f, ffn_pull = jax.vjp(row_norm, attended, gain_ffn.astype(jnp.float32))
        ffn_in = ffn_f.astype(jnp.bfloat16)
        gate_raw = plain_product(ffn_in, full_gate)
        upward = plain_product(ffn_in, full_up)
        active_f, active_pull = jax.vjp(silu_product, gate_raw, upward)
        active = active_f.astype(jnp.bfloat16)
        result = attended + plain_product(active, full_down)
        outputs_list.append(result.astype(jnp.bfloat16))
        back_query, back_key, back_value, back_output, back_gate, back_up, back_down = (
            lax.all_gather(w_query, "fsdp", axis=0, tiled=True),
            lax.all_gather(key_projection, "fsdp", axis=0, tiled=True),
            lax.all_gather(value_projection, "fsdp", axis=0, tiled=True),
            lax.all_gather(w_output, "fsdp", axis=1, tiled=True),
            lax.all_gather(w_gate, "fsdp", axis=0, tiled=True),
            lax.all_gather(w_up, "fsdp", axis=0, tiled=True),
            lax.all_gather(w_down, "fsdp", axis=1, tiled=True),
        )
        grad_result = cotangent[batch_index]
        grad_down_t = rows_product(grad_result, active)
        grad_active = cols_product(grad_result, back_down)
        grad_gate_f, grad_up_f = active_pull(grad_active)
        grad_gate_low = grad_gate_f.astype(jnp.bfloat16)
        grad_up_low = grad_up_f.astype(jnp.bfloat16)
        grad_gate_w = rows_product(ffn_in, grad_gate_low)
        grad_up_w = rows_product(ffn_in, grad_up_low)
        grad_ffn_in = cols_product(grad_gate_low, back_gate) + cols_product(grad_up_low, back_up)
        grad_attended_norm, grad_ffn_gain = ffn_pull(grad_ffn_in)
        grad_attended = grad_result.astype(jnp.float32) + grad_attended_norm
        grad_branch = grad_attended.astype(jnp.bfloat16)
        grad_output_t = rows_product(grad_branch, attn_mix)
        grad_mixed = cols_product(grad_branch, back_output).astype(jnp.bfloat16)
        grad_split = grad_mixed.reshape(tokens, kv_heads, heads_per_group, head_width).transpose(
            1, 0, 2, 3
        )

        def head_backward(blocks):
            query_part, key_part, value_part, grad_part, log_part = blocks
            scores = (
                jnp.einsum("tgd,ld->gtl", query_part, key_part, preferred_element_type=jnp.float32)
                * scale
            )
            scores = jnp.where(allowed[None], scores, NEG)
            prob_rows = jnp.exp(scores - log_part[..., None])
            grad_probs = jnp.einsum(
                "tgd,ld->gtl", grad_part, value_part, preferred_element_type=jnp.float32
            )
            center = jnp.sum(prob_rows * grad_probs, axis=-1, keepdims=True)
            grad_scores = (prob_rows * (grad_probs - center)).astype(jnp.bfloat16)
            grad_query_part = (
                jnp.einsum("gtl,ld->tgd", grad_scores, key_part, preferred_element_type=jnp.float32)
                * scale
            )
            grad_key_part = (
                jnp.einsum(
                    "gtl,tgd->ld", grad_scores, query_part, preferred_element_type=jnp.float32
                )
                * scale
            )
            grad_value_part = jnp.einsum(
                "gtl,tgd->ld",
                prob_rows.astype(jnp.bfloat16),
                grad_part,
                preferred_element_type=jnp.float32,
            )
            return (grad_query_part, grad_key_part, grad_value_part)

        grad_query_split, grad_key_split, grad_value_split = lax.map(
            head_backward, (query_split, key_split, value_split, grad_split, log_totals)
        )
        grad_query_rot = grad_query_split.transpose(1, 0, 2, 3).reshape(tokens, query_width)
        grad_key_all = grad_key_split.transpose(1, 0, 2).reshape(2 * tokens, kv_width)
        grad_value_all = grad_value_split.transpose(1, 0, 2).reshape(2 * tokens, kv_width)
        back_key_grad, back_value_grad = (
            from_behind(grad_key_all[:tokens].astype(jnp.bfloat16), "fsdp", -1).astype(jnp.float32),
            from_behind(grad_value_all[:tokens].astype(jnp.bfloat16), "fsdp", -1).astype(
                jnp.float32
            ),
        )
        grad_key_rot = grad_key_all[tokens:] + back_key_grad
        grad_value_low = (grad_value_all[tokens:] + back_value_grad).astype(jnp.bfloat16)
        grad_query_raw, grad_query_gain = query_pull(grad_query_rot)
        grad_key_raw, grad_key_gain = key_pull(grad_key_rot)
        grad_query_low = grad_query_raw.astype(jnp.bfloat16)
        grad_key_low = grad_key_raw.astype(jnp.bfloat16)
        grad_query_w = rows_product(normed, grad_query_low)
        grad_key_w = rows_product(normed, grad_key_low)
        grad_value_w = rows_product(normed, grad_value_low)
        grad_normed = (
            cols_product(grad_query_low, back_query)
            + cols_product(grad_key_low, back_key)
            + cols_product(grad_value_low, back_value)
        )
        grad_hidden_norm, grad_attn_gain = norm_pull(grad_normed)
        grads_list.append((grad_attended + grad_hidden_norm).astype(jnp.bfloat16))
        gain_sums = add_sets(gain_sums, (grad_query_gain, grad_key_gain))
        shard_terms = (
            lax.psum_scatter(grad_attn_gain, "fsdp", scatter_dimension=0, tiled=True),
            lax.psum_scatter(grad_query_w, "fsdp", scatter_dimension=0, tiled=True),
            lax.psum_scatter(grad_key_w, "fsdp", scatter_dimension=0, tiled=True),
            lax.psum_scatter(grad_value_w, "fsdp", scatter_dimension=0, tiled=True),
            lax.psum_scatter(grad_output_t, "fsdp", scatter_dimension=0, tiled=True),
            lax.psum_scatter(grad_ffn_gain, "fsdp", scatter_dimension=0, tiled=True),
            lax.psum_scatter(grad_gate_w, "fsdp", scatter_dimension=0, tiled=True),
            lax.psum_scatter(grad_up_w, "fsdp", scatter_dimension=0, tiled=True),
            lax.psum_scatter(grad_down_t, "fsdp", scatter_dimension=0, tiled=True),
        )
        shard_sums = add_sets(shard_sums, shard_terms)
    head_sums = lax.psum((gain_sums[0], gain_sums[1]), "fsdp")
    return (
        jnp.stack(outputs_list),
        jnp.stack(grads_list),
        shard_sums[0],
        shard_sums[1],
        shard_sums[2],
        shard_sums[3],
        shard_sums[4].T,
        head_sums[0],
        head_sums[1],
        shard_sums[5],
        shard_sums[6],
        shard_sums[7],
        shard_sums[8].T,
    )


def solution(mesh):
    return jax.shard_map(
        local_grid if mesh.shape["fsdp"] == 32 else local,
        mesh=mesh,
        in_specs=(
            P(None, "fsdp", None),
            P(None, "fsdp"),
            P("fsdp"),
            P("fsdp", None),
            P("fsdp", None),
            P("fsdp", None),
            P(None, "fsdp"),
            P(),
            P(),
            P("fsdp"),
            P("fsdp", None),
            P("fsdp", None),
            P(None, "fsdp"),
            P(None, "fsdp", None),
        ),
        out_specs=(
            P(None, "fsdp", None),
            P(None, "fsdp", None),
            P("fsdp"),
            P("fsdp", None),
            P("fsdp", None),
            P("fsdp", None),
            P(None, "fsdp"),
            P(),
            P(),
            P("fsdp"),
            P("fsdp", None),
            P("fsdp", None),
            P(None, "fsdp"),
        ),
        check_vma=False,
    )
```
